256 devices in a mesh: tm: 8 (over z_lo, x), space: 8 (over y, core), dp: 4 (over z_hi).
Axes of the slice: x: 4, y: 4, z: 8 (z_hi: 4, z_lo: 2; z = z_hi * 2 + z_lo), core: 2. Of those that a mesh axis runs over, the one named last changes fastest.
Arguments:
- frames_in: bfloat16 [4, 32, 1536, 640], P('dp', 'tm', 'space'), may hold values from -6 to 6
- w_time: bfloat16 [1920, 640], replicated, may hold values from -0.125 to 0.125
- w_down: bfloat16 [640, 1280], replicated, may hold values from -0.25 to 0.25
- w_query: bfloat16 [1280, 1280], replicated, may hold values from -0.15625 to 0.15625
- w_key: bfloat16 [1280, 1280], replicated, may hold values from -0.15625 to 0.15625
- grad_skip: bfloat16 [4, 32, 1536, 640], P('dp', 'tm', 'space'), may hold values from -6 to 6
- grad_out: bfloat16 [4, 8, 1536, 1280], P('dp', 'tm', 'space'), may hold values from -6 to 6
Outputs:
- input_grad: bfloat16 [4, 32, 1536, 640], P('dp', 'tm', 'space')
- time_weight_grad: float32 [1920, 640], P(('space', 'dp'))
- down_weight_grad: float32 [640, 1280], P(('space', 'dp'))
The draws below stay inside these ranges and needn't reach their ends.
All inputs are finite; a program needn't handle non-finite values.
Results may differ from the reference program's by a relative error of at most 0.008.
Values may be sent and summed in bfloat16 or wider, within the bound.
A program may use at most 256 MiB of HBM per device.

```python
import math
import jax
import jax.numpy as jnp
from jax import lax

C1 = 640
C2 = 1280
DH = 64
CLIPS = 4
FRAMES = 32
COARSE = 8
PIX = 1536


def strengthened(drawn, stream_key, source, target, blocks, factor):
    owner, partner = [(jnp.arange(drawn.shape[dim]) // (drawn.shape[dim] // blocks)).reshape([-1 if axis == dim else 1 for axis in range(drawn.ndim)]) for dim in (source, target)]
    chosen = jax.random.permutation(stream_key, blocks)[partner]
    strong = (owner == chosen) | (owner == (partner + blocks // 2) % blocks)
    return jnp.where(strong, factor * drawn, drawn)


def shard_levels(rng, extent, shards, low, top_value):
    factor_of = 1.0
    for position, shards_of in shards:
        steps = jax.random.uniform(jax.random.fold_in(jax.random.fold_in(rng, 6), position), (shards_of,), jnp.float32, low / len(shards), top_value / len(shards))
        factor_of = factor_of * jnp.repeat(jnp.exp(steps), extent[position] // shards_of).reshape((-1,) + (1,) * (len(extent) - 1 - position))
    return factor_of


def gaussian(rng, shape, width, limit, shards=(), dtype=jnp.bfloat16):
    entries = jax.random.normal(rng, shape, jnp.float32) * width
    if len(shards) > 0:
        entries = shard_levels(rng, shape, shards, -0.22, 0.18) * entries
    return jnp.clip(entries, min=-limit, max=limit).astype(dtype)


def bell_draw_with(key, dims, scale, bound, shards, heavy, held_as=jnp.bfloat16):
    array = scale * jax.random.normal(key, dims, jnp.float32)
    if shards:
        array = array * shard_levels(key, dims, shards, -0.22, 0.18)
    return jnp.clip(strengthened(array, jax.random.fold_in(key, 3), *heavy), -bound, bound).astype(held_as)


def setup_inputs(seed: int = 0) -> dict:
    splits = jax.random.split(jax.random.key(seed), 8)
    frames_in = bell_draw_with(splits[0], (CLIPS, FRAMES, PIX, C1), 1.0, 6.0, ((0, 4), (1, 8), (2, 8)), (2, 3, 8, 2.0))
    w_time = gaussian(splits[1], (3 * C1, C1), (3 * C1) ** -0.5, 0.125)
    w_down = gaussian(splits[2], (C1, C2), C1 ** -0.5, 0.25)
    w_query = gaussian(splits[3], (C2, C2), C2 ** -0.5, 0.15625)
    w_key = gaussian(splits[4], (C2, C2), C2 ** -0.5, 0.15625)
    grad_skip = gaussian(splits[5], (CLIPS, FRAMES, PIX, C1), 1.0, 6.0, ((0, 4), (1, 8), (2, 8)))
    grad_out = gaussian(splits[6], (CLIPS, COARSE, PIX, C2), 1.0, 6.0, ((0, 4), (1, 8), (2, 8)))
    return dict(frames_in=frames_in, w_time=w_time, w_down=w_down, w_query=w_query, w_key=w_key, grad_skip=grad_skip, grad_out=grad_out)


norm_eps = 1e-06
exact_precision = lax.Precision.HIGHEST

def contract_last(left_mat, right_mat):
    return lax.dot_general(left_mat, right_mat, (((1,), (1,)), ((), ())), preferred_element_type=jnp.float32)

def contract_first(left_mat, right_mat):
    return lax.dot_general(left_mat, right_mat, (((0,), (0,)), ((), ())), preferred_element_type=jnp.float32)

def head_norm(head_rows):
    factor = lax.rsqrt(lax.optimization_barrier(jnp.mean(head_rows * head_rows, axis=-1, keepdims=True)) + norm_eps)
    return (head_rows * factor, factor)

def coarse_backward(coarse, upstream, w_query, w_key, head_dim, first_row, num_rows):
    clip_count, frame_count, pixel_count, coarse_width = coarse.shape
    head_count = coarse_width // head_dim
    shape_heads = (clip_count, frame_count, pixel_count, head_count, head_dim)
    coarse_rows = coarse.reshape(-1, coarse_width)
    queries = jnp.dot(coarse_rows, w_query, preferred_element_type=jnp.float32).reshape(shape_heads)
    key_proj = jnp.dot(coarse_rows, w_key, preferred_element_type=jnp.float32).reshape(shape_heads)
    query_n, query_f = head_norm(queries)
    key_n, key_f = head_norm(key_proj)
    score_scale = 1.0 / math.sqrt(head_dim)
    scores = jnp.einsum('asphd,arphd->aphsr', query_n, key_n, precision=exact_precision) * score_scale
    raised = jnp.exp(scores)
    attn_probs = raised / lax.optimization_barrier(jnp.sum(raised, axis=-1, keepdims=True))
    value_rows = coarse.astype(jnp.float32).reshape(shape_heads)
    cotangent = upstream.astype(jnp.float32).reshape(shape_heads)
    back_probs = jnp.einsum('asphd,arphd->aphsr', cotangent, value_rows, precision=exact_precision)
    back_scores = attn_probs * (back_probs - lax.optimization_barrier(jnp.sum(attn_probs * back_probs, axis=-1, keepdims=True)))
    probs_cols = lax.dynamic_slice_in_dim(attn_probs, first_row, num_rows, 4)
    scores_cols = lax.dynamic_slice_in_dim(back_scores, first_row, num_rows, 4)
    scores_rows = lax.dynamic_slice_in_dim(back_scores, first_row, num_rows, 3)
    back_values = jnp.einsum('aphsr,asphd->arphd', probs_cols, cotangent, precision=exact_precision)
    back_kn = jnp.einsum('aphsr,asphd->arphd', scores_cols, query_n, precision=exact_precision) * score_scale
    back_qn = jnp.einsum('aphsr,arphd->asphd', scores_rows, key_n, precision=exact_precision) * score_scale
    query_own = lax.dynamic_slice_in_dim(query_n, first_row, num_rows, 1)
    query_fac = lax.dynamic_slice_in_dim(query_f, first_row, num_rows, 1)
    key_own = lax.dynamic_slice_in_dim(key_n, first_row, num_rows, 1)
    key_fac = lax.dynamic_slice_in_dim(key_f, first_row, num_rows, 1)
    back_query = (query_fac * (back_qn - query_own * lax.optimization_barrier(jnp.mean(back_qn * query_own, axis=-1, keepdims=True)))).astype(jnp.bfloat16)
    back_key = (key_fac * (back_kn - key_own * lax.optimization_barrier(jnp.mean(back_kn * key_own, axis=-1, keepdims=True)))).astype(jnp.bfloat16)
    projected = contract_last(back_query.reshape(-1, coarse_width), w_query) + contract_last(back_key.reshape(-1, coarse_width), w_key)
    own_cotangent = lax.dynamic_slice_in_dim(cotangent, first_row, num_rows, 1)
    combined = own_cotangent.reshape(-1, coarse_width) + back_values.reshape(-1, coarse_width) + projected
    return combined.astype(jnp.bfloat16).reshape(clip_count, num_rows, pixel_count, coarse_width)

def reference(frames_in, w_time, w_down, w_query, w_key, grad_skip, grad_out):

    def one_clip(clip_items):
        clip_frames, skip_cot, out_cot = clip_items
        frame_count, pixel_count, channels = clip_frames.shape
        coarse_width = w_down.shape[1]
        coarse_frames = frame_count // 4
        zero_frame = jnp.zeros_like(clip_frames[:1])
        earlier = jnp.concatenate([zero_frame, clip_frames[:-1]], axis=0)
        later_frames = jnp.concatenate([clip_frames[1:], zero_frame], axis=0)
        stacked = jnp.concatenate([earlier, clip_frames, later_frames], axis=-1).reshape(-1, 3 * channels)
        pre_act = jnp.dot(stacked, w_time, preferred_element_type=jnp.float32)
        logistic = 1.0 / (1.0 + jnp.exp(-pre_act))
        skip_out = (clip_frames.reshape(-1, channels).astype(jnp.float32) + pre_act * logistic).astype(jnp.bfloat16)
        projected = jnp.dot(skip_out, w_down, preferred_element_type=jnp.float32).reshape(1, coarse_frames, 4, pixel_count, coarse_width)
        coarse = (0.25 * lax.optimization_barrier(jnp.sum(projected, axis=2))).astype(jnp.bfloat16)
        back_coarse = coarse_backward(coarse, out_cot[None], w_query, w_key, DH, 0, coarse_frames)
        spread = contract_last(back_coarse.reshape(-1, coarse_width), w_down).reshape(1, coarse_frames, 1, pixel_count, channels)
        back_skip = (skip_cot.astype(jnp.float32).reshape(1, coarse_frames, 4, pixel_count, channels) + 0.25 * spread).reshape(-1, channels)
        back_pre = (back_skip * logistic * (1.0 + pre_act * (1.0 - logistic))).astype(jnp.bfloat16)
        pre_frames = back_pre.reshape(frame_count, pixel_count, channels)
        zero_grad = jnp.zeros_like(pre_frames[:1])
        pre_later = jnp.concatenate([pre_frames[1:], zero_grad], axis=0).reshape(-1, channels)
        pre_earlier = jnp.concatenate([zero_grad, pre_frames[:-1]], axis=0).reshape(-1, channels)
        input_grad = back_skip + contract_last(pre_later, w_time[:channels]) + contract_last(back_pre, w_time[channels:2 * channels]) + contract_last(pre_earlier, w_time[2 * channels:])
        time_term = contract_first(stacked, back_pre)
        skip_blocks = skip_out.reshape(1, coarse_frames, 4, pixel_count, channels).astype(jnp.float32)
        down_term = 0.25 * jnp.einsum('asipc,aspd->cd', skip_blocks, back_coarse.astype(jnp.float32), precision=exact_precision)
        return (input_grad.astype(jnp.bfloat16).reshape(frame_count, pixel_count, channels), time_term, down_term)
    input_grads, time_terms, down_terms = lax.map(one_clip, (frames_in, grad_skip, grad_out))
    grad_scale = 1.0 / math.sqrt(frames_in.shape[0] * frames_in.shape[1] * frames_in.shape[2])
    return (input_grads, grad_scale * lax.optimization_barrier(jnp.sum(time_terms, axis=0)), grad_scale * lax.optimization_barrier(jnp.sum(down_terms, axis=0)))
```

```python
import math

import jax
import jax.numpy as jnp
from jax import lax
from jax.experimental import pallas as pl
from jax.experimental.pallas import tpu as pltpu
from jax.sharding import PartitionSpec as P

C1, C2, DH = 640, 1280, 64
TM, YS, XS, DP = 8, 4, 4, 4
FINE, PIX = 4, 192
OWN = PIX // TM
ROWS_ALL = 4 * 32 * 1536
EPS = 1e-06
MESH = pl.DeviceIdType.MESH
F32, BF16 = jnp.float32, jnp.bfloat16
COLS_FINE = ((0, 256), (256, 512), (512, 640))
COLS_COARSE = tuple((n, n + 256) for n in range(0, C2, 256))


def dot(left, right):
    return jnp.dot(left, right, preferred_element_type=F32)


def dot_last(left, right):
    return lax.dot_general(left, right, (((1,), (1,)), ((), ())), preferred_element_type=F32)


def dot_first(left, right):
    return lax.dot_general(left, right, (((0,), (0,)), ((), ())), preferred_element_type=F32)


def fold_tail(tail):
    return jnp.concatenate([tail[:, :C1], tail[:, C1:]], axis=0)


def open_tail(tail):
    return jnp.concatenate([tail[:8], tail[8:]], axis=1)


class Ring:
    def __init__(self, remote, parts, bufs, pos, plus, minus, first):
        self.parts, self.pos = parts, pos
        self.ra, self.rb, self.fp, self.fm = bufs
        lo, hi = pl.ds(0, 2), pl.ds(2, 2)
        self.ahead, self.behind, far = (pos + 1) % 4, (pos + 3) % 4, (pos + 2) % 4
        self.copies = [
            remote(parts.at[far, lo], self.ra, first, plus),
            remote(parts.at[far, hi], self.rb, first + 1, minus),
            remote(parts.at[self.ahead, hi], self.fp.at[hi], first + 2, plus),
            remote(parts.at[self.behind, lo], self.fm.at[lo], first + 3, minus),
            remote(parts.at[self.ahead, lo], self.fp.at[lo], first + 4, plus),
            remote(parts.at[self.behind, hi], self.fm.at[hi], first + 5, minus),
        ]

    def start(self):
        for copy in self.copies[:4]:
            copy.start()

    def middle(self):
        parts = self.parts
        self.copies[0].wait_recv()
        parts[self.ahead, 0:2] = (parts[self.ahead, 0:2].astype(F32) + self.ra[...].astype(F32)).astype(BF16)
        self.copies[4].start()
        self.copies[1].wait_recv()
        parts[self.behind, 2:4] = (parts[self.behind, 2:4].astype(F32) + self.rb[...].astype(F32)).astype(BF16)
        self.copies[5].start()

    def arrived(self):
        for copy in self.copies[2:]:
            copy.wait_recv()

    def total(self, i):
        return self.parts[self.pos, i].astype(F32) + self.fp[i].astype(F32) + self.fm[i].astype(F32)

    def finish(self):
        for copy in self.copies:
            copy.wait_send()


def kernel(
    frames, w_time, w_down, w_query, w_key, grad_skip, grad_out,
    ig_out, time_out, down_out,
    ext, wt, wd, wq, wk, gs, go, pre, skipsum, work, qf, kf, cb, gb, bq, bk,
    g_send, g_recv, c_send, c_recv, b_send, b_recv, bc, spread, bpe,
    t_sum, d_sum, cs_y, cs_x, p_y, p_x, y_ra, y_rb, y_fp, y_fm, x_ra, x_rb, x_fp, x_fm,
    p2_y, p2_x, y2_ra, y2_rb, y2_fp, y2_fm, x2_ra, x2_rb, x2_fp, x2_fm,
    z_buf, z_recv, w_buf, w_recv, final,
    local_sem, send_sem, recv_sem,
):
    tm, space, dp = lax.axis_index("tm"), lax.axis_index("space"), lax.axis_index("dp")
    core, y, zlo, x = space % 2, space // 2, tm // XS, tm % XS

    def at(tm_=None, space_=None, dp_=None):
        return {
            "tm": tm if tm_ is None else tm_,
            "space": space if space_ is None else space_,
            "dp": dp if dp_ is None else dp_,
        }

    loads = [
        pltpu.make_async_copy(src, dst, local_sem.at[i])
        for i, (src, dst) in enumerate(
            (
                (frames.at[0], ext.at[pl.ds(1, FINE)]),
                (w_time, wt),
                (grad_out.at[0, 0], go),
                (w_down, wd),
                (w_query, wq),
                (w_key, wk),
                (grad_skip.at[0], gs),
            )
        )
    ]
    for load in loads:
        load.start()

    peers_tm = [at(tm_=(tm + k) % TM) for k in range(1, TM)]
    partner = at(space_=y * 2 + 1 - core)
    y_plus, y_minus = (at(space_=((y + k) % YS) * 2 + core) for k in (1, 3))
    x_plus, x_minus = (at(tm_=zlo * XS + (x + k) % XS) for k in (1, 3))
    peers_dp = [at(dp_=(dp + k) % DP) for k in range(1, DP)]
    barrier = pltpu.get_barrier_semaphore()
    greeted = peers_tm + [partner, y_plus, y_minus] + peers_dp
    for peer in greeted:
        pl.semaphore_signal(barrier, inc=1, device_id=peer, device_id_type=MESH)
    pl.semaphore_wait(barrier, len(greeted))

    def remote(src, dst, sem, device, landed=None):
        return pltpu.make_async_remote_copy(
            src_ref=src,
            dst_ref=dst,
            send_sem=send_sem.at[sem],
            recv_sem=recv_sem.at[sem if landed is None else landed],
            device_id=device,
            device_id_type=MESH,
        )

    def exchange(send, recv, first):
        copies = [
            remote(send.at[(tm + k) % TM], recv.at[tm], first + k, at(tm_=(tm + k) % TM), landed=first + k)
            for k in range(1, TM)
        ]
        own = pltpu.make_async_copy(send.at[tm], recv.at[tm], local_sem.at[7 + first // TM])
        for copy in copies:
            copy.start()
        own.start()

        def receive():
            for k in range(1, TM):
                src = (tm + TM - k) % TM
                remote(send.at[src], recv.at[src], first + k, at(tm_=src)).wait_recv()
            own.wait()

        return copies, receive

    def pack(src, dst):
        for j in range(TM):
            rows = src[OWN * j : OWN * (j + 1), :].astype(F32)
            dst[j, :, :C2] = rows[:16].astype(BF16)
            dst[j, :, C2:] = fold_tail(rows[16:]).astype(BF16)

    def unpack_attn(src, dst):
        for g in range(2):
            rows = [src[f, :, :C2].astype(F32)[8 * g : 8 * g + 8] for f in range(TM)]
            dst[64 * g : 64 * g + 64, :] = jnp.concatenate(rows, axis=0).astype(BF16)
        rows = [open_tail(src[f, :, C2:].astype(F32)) for f in range(TM)]
        dst[128:192, :] = jnp.concatenate(rows, axis=0).astype(BF16)

    prev, nxt = at(tm_=(tm + TM - 1) % TM), at(tm_=(tm + 1) % TM)
    halo_first = remote(frames.at[0, 0], ext.at[FINE + 1], 24, prev)
    halo_last = remote(frames.at[0, FINE - 1], ext.at[0], 25, nxt)
    halo_first.start()
    halo_last.start()

    loads[2].wait()
    pack(go, g_send)

    loads[0].wait()
    loads[1].wait()
    for lo, hi in COLS_FINE:
        n = hi - lo
        pre[:, :, lo:hi] = dot(ext[1:5].reshape(FINE * PIX, C1), wt[C1 : 2 * C1, lo:hi]).reshape(FINE, PIX, n)
        pre[1:4, :, lo:hi] += dot(ext[1:4].reshape(3 * PIX, C1), wt[:C1, lo:hi]).reshape(3, PIX, n)
        pre[0:3, :, lo:hi] += dot(ext[2:5].reshape(3 * PIX, C1), wt[2 * C1 :, lo:hi]).reshape(3, PIX, n)

    halo_first.wait_recv()
    halo_last.wait_recv()
    g_copies, g_receive = exchange(g_send, g_recv, 0)

    def clear_ends(cells):
        @pl.when(tm == 0)
        def _():
            cells[0] = jnp.zeros((PIX, C1), BF16)

        @pl.when(tm == TM - 1)
        def _():
            cells[FINE + 1] = jnp.zeros((PIX, C1), BF16)

    clear_ends(ext)
    for lo, hi in COLS_FINE:
        pre[0, :, lo:hi] += dot(ext[0], wt[:C1, lo:hi])
        pre[3, :, lo:hi] += dot(ext[5], wt[2 * C1 :, lo:hi])
        total = None
        for t in range(FINE):
            act = pre[t, :, lo:hi]
            logistic = 1.0 / (1.0 + jnp.exp(-act))
            skip = (ext[t + 1, :, lo:hi].astype(F32) + act * logistic).astype(BF16).astype(F32)
            total = skip if total is None else total + skip
            pre[t, :, lo:hi] = logistic * (1.0 + act * (1.0 - logistic))
        skipsum[:, lo:hi] = total.astype(BF16)

    loads[3].wait()
    for lo, hi in COLS_COARSE:
        work[:, lo:hi] = 0.25 * dot(skipsum[...], wd[:, lo:hi])
    pack(work, c_send)
    c_copies, c_receive = exchange(c_send, c_recv, 8)

    loads[4].wait()
    loads[5].wait()
    c_receive()
    unpack_attn(c_recv, cb)
    for lo, hi in COLS_COARSE:
        qf[:, lo:hi] = dot(cb[...], wq[:, lo:hi])
        kf[:, lo:hi] = dot(cb[...], wk[:, lo:hi])
    g_receive()
    unpack_attn(g_recv, gb)

    row_i = lax.broadcasted_iota(jnp.int32, (128, 128), 0)
    col_i = lax.broadcasted_iota(jnp.int32, (128, 128), 1)
    ones = ((row_i // DH) == (col_i // DH)).astype(F32).astype(BF16)
    mask = ((row_i[:64] % 8) == (col_i[:64] % 8)).astype(F32)
    left = (lax.broadcasted_iota(jnp.int32, (64, 128), 1) < DH).astype(F32)
    left_b, right_b = left.astype(BF16), (1.0 - left).astype(BF16)

    def heads(rows):
        return jnp.concatenate([rows * left_b, rows * right_b], axis=0)

    def attend(i, carry):
        cols = pl.ds(pl.multiple_of(i * 128, 128), 128)
        q, k = qf[:, cols], kf[:, cols]
        rq = lax.rsqrt(dot((q * q).astype(BF16), ones) * (1.0 / DH) + EPS)
        rk = lax.rsqrt(dot((k * k).astype(BF16), ones) * (1.0 / DH) + EPS)
        qn, kn = q * rq, k * rk
        qb, kb = qn.astype(BF16), kn.astype(BF16)
        bqn, bkn = [], []
        for g in range(3):
            rows = slice(64 * g, 64 * g + 64)
            cg, gg = cb[rows, cols], gb[rows, cols]
            keys = heads(kb[rows])
            raised = jnp.exp(dot_last(qb[rows], keys) * 0.125) * mask
            probs = raised / dot(raised.astype(BF16), ones)
            back_probs = dot_last(gg, heads(cg))
            back_scores = probs * (back_probs - dot((probs * back_probs).astype(BF16), ones))
            probs_b, scores_b = probs.astype(BF16), back_scores.astype(BF16)
            values = dot_first(probs_b, gg)
            back_k = dot_first(scores_b, qb[rows])
            work[rows, cols] = gg.astype(F32) + values[:64] * left + values[64:] * (1.0 - left)
            bkn.append((back_k[:64] * left + back_k[64:] * (1.0 - left)) * 0.125)
            bqn.append(dot(scores_b, keys) * 0.125)
        bqn, bkn = jnp.concatenate(bqn, axis=0), jnp.concatenate(bkn, axis=0)
        bq[:, cols] = (rq * (bqn - qn * (dot((bqn * qn).astype(BF16), ones) * (1.0 / DH)))).astype(BF16)
        bk[:, cols] = (rk * (bkn - kn * (dot((bkn * kn).astype(BF16), ones) * (1.0 / DH)))).astype(BF16)
        return carry

    lax.fori_loop(0, C2 // 128, attend, 0)
    for lo, hi in COLS_COARSE:
        work[:, lo:hi] += dot_last(bq[...], wq[lo:hi, :]) + dot_last(bk[...], wk[lo:hi, :])
    for f in range(TM):
        rows = [work[64 * g + 8 * f : 64 * g + 8 * f + 8, :] for g in range(3)]
        b_send[f, :, :C2] = jnp.concatenate(rows[:2], axis=0).astype(BF16)
        b_send[f, :, C2:] = fold_tail(rows[2]).astype(BF16)
    b_copies, b_receive = exchange(b_send, b_recv, 16)
    b_receive()
    for j in range(0, TM, 2):
        rows = []
        for src in (j, j + 1):
            rows += [b_recv[src, :, :C2].astype(F32), open_tail(b_recv[src, :, C2:].astype(F32))]
        bc[OWN * j : OWN * (j + 2), :] = jnp.concatenate(rows, axis=0).astype(BF16)

    d_sum[C1:, :] = jnp.zeros((8, C2), F32)

    def down(i, carry):
        cols = pl.ds(pl.multiple_of(i * 128, 128), 128)
        d_sum[cols, :] = dot_first(skipsum[:, cols], bc[...])
        return carry

    lax.fori_loop(0, C1 // 128, down, 0)

    def down_unit(part_y, part_core, part_dp):
        odd = part_dp % 2 * 4
        start = pl.multiple_of(160 * part_y + 80 * part_core + (20 * part_dp - odd), 8)
        rows = d_sum[pl.ds(start, 32 if odd else 24), :][odd : odd + 24]
        return jnp.concatenate([rows[:, :C1], rows[:, C1:], jnp.zeros((16, C1), F32)], axis=0).reshape(4, 16, C1)

    def time_unit(part_y, part_core, part_dp):
        odd = part_dp % 2 * 4
        start = pl.multiple_of(480 * part_y + 240 * part_core + (60 * part_dp - odd), 8)
        return t_sum[pl.ds(start, 72 if odd else 64), :][odd : odd + 64]

    def pack_down(part_y, carry):
        for h in range(DP):
            cs_x[:, part_y, h] = down_unit(part_y, 1 - core, h).astype(BF16)
        return carry

    lax.fori_loop(0, YS, pack_down, 0)
    swap_x = remote(cs_x, p_x, 26, partner)
    swap_x.start()

    loads[6].wait()
    for lo, hi in COLS_FINE:
        spread[:, lo:hi] = 0.25 * dot_last(bc[...], wd[lo:hi, :])
        for t in range(FINE):
            back = gs[t, :, lo:hi].astype(F32) + spread[:, lo:hi]
            bpe[t + 1, :, lo:hi] = (back * pre[t, :, lo:hi]).astype(BF16)
    back_first = remote(bpe.at[1], bpe.at[FINE + 1], 28, prev)
    back_last = remote(bpe.at[FINE], bpe.at[0], 29, nxt)
    back_first.start()
    back_last.start()

    swap_x.wait_recv()

    def add_down(part_y, carry):
        for h in range(DP):
            p_x[:, part_y, h] = (p_x[:, part_y, h].astype(F32) + down_unit(part_y, core, h)).astype(BF16)
        return carry

    lax.fori_loop(0, YS, add_down, 0)
    ring_x = Ring(remote, p_x, (x_ra, x_rb, x_fp, x_fm), x, x_plus, x_minus, 30)
    ring_x.start()

    t_sum[3 * C1 :, :] = jnp.zeros((8, C1), F32)
    for k in range(3):

        def time_block(i, carry, k=k):
            cols = pl.ds(pl.multiple_of(i * 128, 128), 128)
            block = ext[k : k + FINE, :, cols].reshape(FINE * PIX, 128)
            start = pl.multiple_of(k * C1 + i * 128, 128)
            t_sum[pl.ds(start, 128), :] = dot_first(block, bpe[1 : FINE + 1].reshape(FINE * PIX, C1))
            return carry

        lax.fori_loop(0, C1 // 128, time_block, 0)

    def pack_time(part_y, carry):
        for h in range(DP):
            cs_y[part_y, h] = time_unit(part_y, 1 - core, h).astype(BF16)
        return carry

    lax.fori_loop(0, YS, pack_time, 0)
    swap_y = remote(cs_y, p_y, 27, partner)
    swap_y.start()
    ring_x.middle()
    swap_y.wait_recv()

    def add_time(part_y, carry):
        for h in range(DP):
            p_y[part_y, h] = (p_y[part_y, h].astype(F32) + time_unit(part_y, core, h)).astype(BF16)
        return carry

    lax.fori_loop(0, YS, add_time, 0)
    ring_y = Ring(remote, p_y, (y_ra, y_rb, y_fp, y_fm), y, y_plus, y_minus, 36)
    ring_y.start()

    back_first.wait_recv()
    back_last.wait_recv()
    clear_ends(bpe)
    for lo, hi in COLS_FINE:
        n = hi - lo
        for t in range(0, FINE, 2):
            rows = [bpe[t + k : t + k + 2].reshape(2 * PIX, C1) for k in range(3)]
            acc = dot_last(rows[2], wt[lo:hi, :])
            acc += dot_last(rows[1], wt[C1 + lo : C1 + hi, :])
            acc += dot_last(rows[0], wt[2 * C1 + lo : 2 * C1 + hi, :])
            acc = acc.reshape(2, PIX, n) + gs[t : t + 2, :, lo:hi].astype(F32) + spread[:, lo:hi]
            gs[t : t + 2, :, lo:hi] = acc.astype(BF16)
    store = pltpu.make_async_copy(gs, ig_out.at[0], local_sem.at[10])
    store.start()

    ring_x.arrived()
    for part_y in range(YS):
        p2_x[part_y] = ring_x.total(part_y).astype(BF16)
    ring2_x = Ring(remote, p2_x, (x2_ra, x2_rb, x2_fp, x2_fm), y, y_plus, y_minus, 42)
    ring2_x.start()
    ring_y.middle()
    ring2_x.middle()
    ring_y.arrived()
    for h in range(DP):
        p2_y[:, h] = ring_y.total(h).astype(BF16).reshape(XS, 16, C1)
    ring2_y = Ring(remote, p2_y, (y2_ra, y2_rb, y2_fp, y2_fm), x, x_plus, x_minus, 48)
    ring2_y.start()
    ring2_y.middle()
    ring2_x.arrived()
    for h in range(DP):
        z_buf[1, h] = ring2_x.total(h).astype(BF16)
    ring2_y.arrived()
    for h in range(DP):
        z_buf[0, h] = ring2_y.total(h).astype(BF16)

    swap_z = remote(z_buf.at[1 - zlo], z_recv, 54, at(tm_=(1 - zlo) * XS + x))
    swap_z.start()
    swap_z.wait_recv()
    w_buf[...] = (z_buf[zlo].astype(F32) + z_recv[...].astype(F32)).astype(BF16)
    dp_copies = [remote(w_buf.at[(dp + k) % DP], w_recv.at[k - 1], 54 + k, peers_dp[k - 1]) for k in range(1, DP)]
    for copy in dp_copies:
        copy.start()
    total = w_buf[dp].astype(F32)
    for k in range(1, DP):
        dp_copies[k - 1].wait_recv()
        total += w_recv[k - 1].astype(F32)
    final[tm] = total.astype(BF16)
    last_copies = [remote(final.at[tm], final.at[tm], 57 + k, peers_tm[k - 1]) for k in range(1, TM)]
    for copy in last_copies:
        copy.start()
    for k in range(1, TM):
        src = (tm + TM - k) % TM
        remote(final.at[src], final.at[src], 57 + k, at(tm_=src)).wait_recv()
    scale = 1.0 / math.sqrt(ROWS_ALL)
    time_out[...] = (final[0:4].astype(F32) * scale).reshape(64, C1)[:60]
    rows = (final[4:7].astype(F32) * (0.25 * scale)).reshape(48, C1)
    down_out[:, :C1] = rows[:20]
    down_out[:, C1:] = rows[24:44]

    for copy in [halo_first, halo_last, back_first, back_last, swap_x, swap_y, swap_z]:
        copy.wait_send()
    for copy in g_copies + c_copies + b_copies + dp_copies + last_copies:
        copy.wait_send()
    for ring in (ring_x, ring_y, ring2_x, ring2_y):
        ring.finish()
    store.wait()


def shards(*args):
    v = pltpu.VMEM
    scratch = [
        v((FINE + 2, PIX, C1), BF16), v((3 * C1, C1), BF16), v((C1, C2), BF16), v((C2, C2), BF16), v((C2, C2), BF16),
        v((FINE, PIX, C1), BF16), v((PIX, C2), BF16), v((FINE, PIX, C1), F32), v((PIX, C1), BF16),
        v((PIX, C2), F32), v((PIX, C2), F32), v((PIX, C2), F32),
        v((PIX, C2), BF16), v((PIX, C2), BF16), v((PIX, C2), BF16), v((PIX, C2), BF16),
        *[v((TM, 16, C2 + C1), BF16)] * 6,
        v((PIX, C2), BF16), v((PIX, C1), F32), v((FINE + 2, PIX, C1), BF16),
        v((3 * C1 + 8, C1), F32), v((C1 + 8, C2), F32),
        v((YS, DP, 64, C1), BF16), v((XS, YS, DP, 16, C1), BF16),
        v((YS, DP, 64, C1), BF16), v((XS, YS, DP, 16, C1), BF16),
        *[v((2, 64, C1), BF16)] * 2, *[v((4, 64, C1), BF16)] * 2,
        *[v((2, DP, 16, C1), BF16)] * 2, *[v((4, DP, 16, C1), BF16)] * 2,
        v((XS, DP, 16, C1), BF16), v((YS, DP, 16, C1), BF16),
        *[v((2, 16, C1), BF16)] * 2, *[v((4, 16, C1), BF16)] * 2,
        *[v((2, 16, C1), BF16)] * 2, *[v((4, 16, C1), BF16)] * 2,
        v((2, DP, 16, C1), BF16), v((DP, 16, C1), BF16), v((DP, 16, C1), BF16), v((DP - 1, 16, C1), BF16),
        v((TM, 16, C1), BF16),
        pltpu.SemaphoreType.DMA((11,)), pltpu.SemaphoreType.DMA((65,)), pltpu.SemaphoreType.DMA((65,)),
    ]
    return pl.pallas_call(
        kernel,
        out_shape=(
            jax.ShapeDtypeStruct((1, FINE, PIX, C1), BF16),
            jax.ShapeDtypeStruct((60, C1), F32),
            jax.ShapeDtypeStruct((20, C2), F32),
        ),
        in_specs=[pl.BlockSpec(memory_space=pl.ANY)] * 7,
        out_specs=(
            pl.BlockSpec(memory_space=pl.ANY),
            pl.BlockSpec(memory_space=pltpu.VMEM),
            pl.BlockSpec(memory_space=pltpu.VMEM),
        ),
        scratch_shapes=scratch,
        compiler_params=pltpu.CompilerParams(
            collective_id=0, has_side_effects=True, vmem_limit_bytes=62 * 1024 * 1024
        ),
        cost_estimate=pl.CostEstimate(flops=9 * 10**9, bytes_accessed=16 * 10**6, transcendentals=10**6),
    )(*args)


def solution(mesh):
    fine, whole = P("dp", "tm", "space", None), P()
    rows = P(("space", "dp"), None)
    return jax.shard_map(
        shards,
        mesh=mesh,
        in_specs=(fine, whole, whole, whole, whole, fine, fine),
        out_specs=(fine, rows, rows),
        check_vma=False,
    )
```

```python
import math

import jax
import jax.numpy as jnp
from jax import lax
from jax.experimental import pallas as pl
from jax.experimental.pallas import tpu as pltpu
from jax.sharding import PartitionSpec as P

C1, C2, DH = 640, 1280, 64
TM, YS, XS, DP = 8, 4, 4, 4
FINE, PIX = 4, 192
ROWS_ALL = 4 * 32 * 1536
EPS = 1e-06
MESH = pl.DeviceIdType.MESH
F32, BF16 = jnp.float32, jnp.bfloat16
COLS_FINE = ((0, 256), (256, 512), (512, 640))
COLS_COARSE = tuple((n, n + 256) for n in range(0, C2, 256))
CHUNKS, WIDE = 3, 64
DC = 512
TILES = 5


def dot(left, right):
    return jnp.dot(left, right, preferred_element_type=F32)


def dot_last(left, right):
    return lax.dot_general(left, right, (((1,), (1,)), ((), ())), preferred_element_type=F32)


def dot_first(left, right):
    return lax.dot_general(left, right, (((0,), (0,)), ((), ())), preferred_element_type=F32)


def fold_tail(tail):
    return jnp.concatenate([tail[:, :C1], tail[:, C1:]], axis=0)


def open_tail(tail):
    return jnp.concatenate([tail[:8], tail[8:]], axis=1)


class Ring:
    def __init__(self, remote, parts, bufs, pos, plus, minus, first):
        self.parts, self.pos = parts, pos
        self.ra, self.rb, self.fp, self.fm = bufs
        lo, hi = pl.ds(0, 2), pl.ds(2, 2)
        self.ahead, self.behind, self.far = (pos + 1) % 4, (pos + 3) % 4, (pos + 2) % 4
        self.copies = [
            remote(parts.at[self.far, lo], self.ra, first, plus),
            remote(parts.at[self.far, hi], self.rb, first + 1, minus),
            remote(parts.at[self.ahead, hi], self.fp.at[hi], first + 2, plus),
            remote(parts.at[self.behind, lo], self.fm.at[lo], first + 3, minus),
            remote(parts.at[self.ahead, lo], self.fp.at[lo], first + 4, plus),
            remote(parts.at[self.behind, hi], self.fm.at[hi], first + 5, minus),
        ]

    def start(self):
        for copy in self.copies[:4]:
            copy.start()

    def middle(self):
        parts = self.parts
        self.copies[0].wait_recv()
        parts[self.ahead, 0:2] = (parts[self.ahead, 0:2].astype(F32) + self.ra[...].astype(F32)).astype(BF16)
        self.copies[4].start()
        self.copies[1].wait_recv()
        parts[self.behind, 2:4] = (parts[self.behind, 2:4].astype(F32) + self.rb[...].astype(F32)).astype(BF16)
        self.copies[5].start()

    def arrived(self):
        for copy in self.copies[2:]:
            copy.wait_recv()

    def total(self, i):
        return self.parts[self.pos, i].astype(F32) + self.fp[i].astype(F32) + self.fm[i].astype(F32)

    def finish(self):
        for copy in self.copies:
            copy.wait_send()


def attend(tiles, qf, kf, cb, gb, work, bq, bk):
    row_i = lax.broadcasted_iota(jnp.int32, (128, 128), 0)
    col_i = lax.broadcasted_iota(jnp.int32, (128, 128), 1)
    ones = ((row_i // DH) == (col_i // DH)).astype(F32).astype(BF16)
    mask = ((row_i[:WIDE] % 8) == (col_i[:WIDE] % 8)).astype(F32)
    left = (lax.broadcasted_iota(jnp.int32, (WIDE, 128), 1) < DH).astype(F32)
    left_b, right_b = left.astype(BF16), (1.0 - left).astype(BF16)
    count = len(tiles)
    units = [(i, slice(WIDE * g, WIDE * g + WIDE)) for i in range(count) for g in range(CHUNKS)]
    index = range(len(units))

    def heads(rows):
        return jnp.concatenate([rows * left_b, rows * right_b], axis=0)

    def fold(both):
        return jnp.where(left > 0.5, both[:WIDE], both[WIDE:])

    def head_sums(terms):
        sums = dot(jnp.concatenate([term.astype(BF16) for term in terms], axis=0), ones)
        rows = terms[0].shape[0]
        return [sums[rows * i : rows * i + rows] for i in range(len(terms))]

    q, k = [qf[:, c] for c in tiles], [kf[:, c] for c in tiles]
    factors = [lax.rsqrt(total * (1.0 / DH) + EPS) for total in head_sums([v * v for v in q + k])]
    rq, rk = factors[:count], factors[count:]
    qb = [(q[i] * rq[i]).astype(BF16) for i in range(count)]
    kb = [(k[i] * rk[i]).astype(BF16) for i in range(count)]
    queries = [qb[i][rows] for i, rows in units]
    keys = [heads(kb[i][rows]) for i, rows in units]
    raised = [jnp.exp(dot_last(queries[n], keys[n]) * 0.125) * mask for n in index]
    upstream = [gb[rows, tiles[i]] for i, rows in units]
    back_probs = [dot_last(upstream[n], heads(cb[rows, tiles[i]])) for n, (i, rows) in enumerate(units)]
    probs = [over / under for over, under in zip(raised, head_sums(raised))]
    means = head_sums([p * b for p, b in zip(probs, back_probs)])
    scores = [(p * (b - m)).astype(BF16) for p, b, m in zip(probs, back_probs, means)]
    for n, (i, rows) in enumerate(units):
        values = fold(dot_first(probs[n].astype(BF16), upstream[n]))
        work[rows, tiles[i]] = upstream[n].astype(F32) + values
    back_q = [dot(scores[n], keys[n]) * 0.125 for n in index]
    back_k = [fold(dot_first(scores[n], queries[n])) * 0.125 for n in index]
    qn = [rows.astype(F32) for rows in queries]
    kn = [kb[i][rows].astype(F32) for i, rows in units]
    mean_q = head_sums([b * v for b, v in zip(back_q, qn)])
    mean_k = head_sums([b * v for b, v in zip(back_k, kn)])
    for n, (i, rows) in enumerate(units):
        bq[rows, tiles[i]] = (rq[i][rows] * (back_q[n] - qn[n] * (mean_q[n] * (1.0 / DH)))).astype(BF16)
        bk[rows, tiles[i]] = (rk[i][rows] * (back_k[n] - kn[n] * (mean_k[n] * (1.0 / DH)))).astype(BF16)


def kernel(
    frames, w_time, w_down, w_query, w_key, grad_skip, grad_out,
    ig_out, sums_out,
    ext, wt, wd, wq, wk, gs, go, pre, skipsum, work, qf, kf, cb, gb, bq, bk,
    g_send, g_recv, c_send, c_recv, b_send, b_recv, bc, spread, bpe,
    t_sum, d_sum, cs_y, cs_x, p_y, p_x, y_ra, y_rb, y_fp, y_fm, x_ra, x_rb, x_fp, x_fm,
    p2_y, p2_x, y2_ra, y2_rb, y2_fp, y2_fm, x2_ra, x2_rb, x2_fp, x2_fm,
    z_buf, z_recv, final,
    local_sem, send_sem, recv_sem,
):
    tm, space, dp = lax.axis_index("tm"), lax.axis_index("space"), lax.axis_index("dp")
    core, y, zlo, x = space % 2, space // 2, tm // XS, tm % XS

    def at(tm_=None, space_=None, dp_=None):
        return {
            "tm": tm if tm_ is None else tm_,
            "space": space if space_ is None else space_,
            "dp": dp if dp_ is None else dp_,
        }

    loads = [
        pltpu.make_async_copy(src, dst, local_sem.at[i])
        for i, (src, dst) in enumerate(
            (
                (frames.at[0], ext.at[pl.ds(1, FINE)]),
                (w_time, wt),
                (w_down, wd),
                (grad_out.at[0, 0], go),
                (w_query, wq),
                (w_key, wk),
                (grad_skip.at[0], gs),
            )
        )
    ]
    for load in loads:
        load.start()

    peers_tm = [at(tm_=(tm + k) % TM) for k in range(1, TM)]
    partner = at(space_=y * 2 + 1 - core)
    y_plus, y_minus = (at(space_=((y + k) % YS) * 2 + core) for k in (1, 3))
    x_plus, x_minus = (at(tm_=zlo * XS + (x + k) % XS) for k in (1, 3))
    zpos = dp * 2 + zlo
    on_z = [(zpos + k) % 8 for k in range(1, 8)]
    peers_z = [at(tm_=z % 2 * XS + x, dp_=z // 2) for z in on_z]
    barrier = pltpu.get_barrier_semaphore()
    other_z = [at(tm_=tm_, dp_=(dp + k) % DP) for k in range(1, DP) for tm_ in (x, XS + x)]
    greeted = peers_tm + [partner, y_plus, y_minus] + other_z
    for peer in greeted:
        pl.semaphore_signal(barrier, inc=1, device_id=peer, device_id_type=MESH)
    pl.semaphore_wait(barrier, len(greeted))

    def remote(src, dst, sem, device, landed=None):
        return pltpu.make_async_remote_copy(
            src_ref=src,
            dst_ref=dst,
            send_sem=send_sem.at[sem],
            recv_sem=recv_sem.at[sem if landed is None else landed],
            device_id=device,
            device_id_type=MESH,
        )

    def exchange(send, recv, c, first):
        copies = [
            remote(send.at[c, (tm + k) % TM], recv.at[c, tm], first + k, at(tm_=(tm + k) % TM)) for k in range(1, TM)
        ]
        own = pltpu.make_async_copy(send.at[c, tm], recv.at[c, tm], local_sem.at[7 + first // TM])
        for copy in copies:
            copy.start()
        own.start()

        def receive():
            for k in range(1, TM):
                src = (tm + TM - k) % TM
                remote(send.at[c, src], recv.at[c, src], first + k, at(tm_=src)).wait_recv()
            own.wait()

        sent.extend(copies)
        return receive

    sent = []

    def send(copy):
        copy.start()
        sent.append(copy)
        return copy

    def pack(src, dst, c):
        rows = src[c * WIDE : (c + 1) * WIDE, :].astype(F32)
        for f in range(TM):
            dst[c, f] = fold_tail(rows[8 * f : 8 * f + 8]).astype(BF16)

    def unpack(src, dst, c):
        rows = [open_tail(src[c, f].astype(F32)) for f in range(TM)]
        dst[c * WIDE : (c + 1) * WIDE, :] = jnp.concatenate(rows, axis=0).astype(BF16)

    prev, nxt = at(tm_=(tm + TM - 1) % TM), at(tm_=(tm + 1) % TM)
    halos = []
    for c in range(CHUNKS):
        rows = pl.ds(c * WIDE, WIDE)
        first = send(remote(frames.at[0, 0, rows], ext.at[FINE + 1, rows], 72 + 2 * c, prev))
        last = send(remote(frames.at[0, FINE - 1, rows], ext.at[0, rows], 73 + 2 * c, nxt))
        halos.append((first, last))

    loads[0].wait()
    loads[1].wait()
    for lo, hi in COLS_FINE:
        n = hi - lo
        pre[:, :, lo:hi] = dot(ext[1:5].reshape(FINE * PIX, C1), wt[C1 : 2 * C1, lo:hi]).reshape(FINE, PIX, n)
        pre[1:4, :, lo:hi] += dot(ext[1:4].reshape(3 * PIX, C1), wt[:C1, lo:hi]).reshape(3, PIX, n)
        pre[0:3, :, lo:hi] += dot(ext[2:5].reshape(3 * PIX, C1), wt[2 * C1 :, lo:hi]).reshape(3, PIX, n)
    loads[3].wait()
    for c in range(CHUNKS):
        pack(go, g_send, c)

    loads[2].wait()
    c_receive, g_receive = [], []
    for c in range(CHUNKS):
        rows = slice(c * WIDE, (c + 1) * WIDE)
        for copy in halos[c]:
            copy.wait_recv()

        @pl.when(tm == 0)
        def _():
            ext[0, rows] = jnp.zeros((WIDE, C1), BF16)

        @pl.when(tm == TM - 1)
        def _():
            ext[FINE + 1, rows] = jnp.zeros((WIDE, C1), BF16)

        for lo, hi in COLS_FINE:
            pre[0, rows, lo:hi] += dot(ext[0, rows], wt[:C1, lo:hi])
            pre[3, rows, lo:hi] += dot(ext[5, rows], wt[2 * C1 :, lo:hi])
            total = None
            for t in range(FINE):
                act = pre[t, rows, lo:hi]
                logistic = 1.0 / (1.0 + jnp.exp(-act))
                skip = (ext[t + 1, rows, lo:hi].astype(F32) + act * logistic).astype(BF16).astype(F32)
                total = skip if total is None else total + skip
                pre[t, rows, lo:hi] = logistic * (1.0 + act * (1.0 - logistic))
            skipsum[rows, lo:hi] = total.astype(BF16)
        for lo, hi in COLS_COARSE:
            work[rows, lo:hi] = 0.25 * dot(skipsum[rows, :], wd[:, lo:hi])
        pack(work, c_send, c)
        c_receive.append(exchange(c_send, c_recv, c, 8 * c))
    for c in range(CHUNKS):
        g_receive.append(exchange(g_send, g_recv, c, 24 + 8 * c))

    loads[4].wait()
    loads[5].wait()
    for c in range(CHUNKS):
        c_receive[c]()
        unpack(c_recv, cb, c)
    for lo, hi in COLS_COARSE:
        qf[:, lo:hi] = dot(cb[...], wq[:, lo:hi])
        kf[:, lo:hi] = dot(cb[...], wk[:, lo:hi])
    for c in range(CHUNKS):
        g_receive[c]()
        unpack(g_recv, gb, c)

    def attend_some(i, carry):
        tiles = [pl.ds(pl.multiple_of((i * TILES + u) * 128, 128), 128) for u in range(TILES)]
        attend(tiles, qf, kf, cb, gb, work, bq, bk)
        return carry

    lax.fori_loop(0, C2 // 128 // TILES, attend_some, 0)
    for lo, hi in COLS_COARSE:
        work[:, lo:hi] += dot_last(bq[...], wq[lo:hi, :]) + dot_last(bk[...], wk[lo:hi, :])
    b_receive = []
    for c in range(CHUNKS):
        pack(work, b_send, c)
        b_receive.append(exchange(b_send, b_recv, c, 48 + 8 * c))
    for c in range(CHUNKS):
        b_receive[c]()
        unpack(b_recv, bc, c)

    loads[6].wait()
    for lo, hi in COLS_FINE:
        spread[:, lo:hi] = 0.25 * dot_last(bc[...], wd[lo:hi, :])
        for t in range(FINE):
            back = gs[t, :, lo:hi].astype(F32) + spread[:, lo:hi]
            bpe[t + 1, :, lo:hi] = (back * pre[t, :, lo:hi]).astype(BF16)
    back_first = send(remote(bpe.at[1], bpe.at[FINE + 1], 78, prev))
    back_last = send(remote(bpe.at[FINE], bpe.at[0], 79, nxt))

    def time_unit(part_y, part_core, part_dp):
        start = pl.multiple_of(480 * part_y + 240 * part_core + 60 * part_dp // 8 * 8, 8)
        return t_sum[pl.ds(start, 64), :]

    def down_unit(part_y, part_core, part_dp):
        start = pl.multiple_of(160 * part_y + 80 * part_core + 20 * part_dp // 8 * 8, 8)
        rows = d_sum[pl.ds(start, 24), :]
        return jnp.concatenate([rows[:16], fold_tail(rows[16:]), jnp.zeros((16, 128), F32)], axis=1)

    swap_y = []
    for part_y in range(YS):

        def time_block(i, carry):
            cols = pl.ds(pl.multiple_of(i % 5 * 128, 128), 128)
            block = ext[pl.ds(i // 5, FINE), :, cols].reshape(FINE * PIX, 128)
            start = pl.multiple_of(i * 128, 128)
            t_sum[pl.ds(start, 128), :] = dot_first(block, bpe[1 : FINE + 1].reshape(FINE * PIX, C1))
            return carry

        lax.fori_loop(4 * part_y, min(4 * part_y + 4, 15), time_block, 0)
        for h in range(DP):
            cs_y[part_y, h] = time_unit(part_y, 1 - core, h).astype(BF16)
        swap_y.append(send(remote(cs_y.at[part_y], p_y.at[part_y], 80 + part_y, partner)))

    def down(i, carry):
        cols = pl.ds(pl.multiple_of(i * 128, 128), 128)
        d_sum[cols, :] = dot_first(skipsum[:, cols], bc[...])
        return carry

    lax.fori_loop(0, C1 // 128, down, 0)

    def pack_down(part_y, carry):
        for h in range(DP):
            unit = down_unit(part_y, 1 - core, h).astype(BF16)
            for part_x in range(XS):
                cs_x[part_x, part_y, h] = unit[:, DC * part_x : DC * part_x + DC]
        return carry

    lax.fori_loop(0, YS, pack_down, 0)
    swap_x = send(remote(cs_x, p_x, 84, partner))

    ring_y = Ring(remote, p_y, (y_ra, y_rb, y_fp, y_fm), y, y_plus, y_minus, 86)
    for part_y, copies in (
        (ring_y.far, ring_y.copies[:2]),
        (ring_y.ahead, ring_y.copies[2:3]),
        (ring_y.behind, ring_y.copies[3:4]),
        (y, []),
    ):
        remote(cs_y.at[part_y], p_y.at[part_y], 80 + part_y, partner).wait_recv()
        for h in range(DP):
            p_y[part_y, h] = (p_y[part_y, h].astype(F32) + time_unit(part_y, core, h)).astype(BF16)
        for copy in copies:
            copy.start()

    swap_x.wait_recv()

    def add_down(part_y, carry):
        for h in range(DP):
            unit = down_unit(part_y, core, h)
            for part_x in range(XS):
                more = unit[:, DC * part_x : DC * part_x + DC]
                p_x[part_x, part_y, h] = (p_x[part_x, part_y, h].astype(F32) + more).astype(BF16)
        return carry

    lax.fori_loop(0, YS, add_down, 0)
    ring_x = Ring(remote, p_x, (x_ra, x_rb, x_fp, x_fm), x, x_plus, x_minus, 92)
    ring_x.start()

    back_first.wait_recv()
    back_last.wait_recv()

    @pl.when(tm == 0)
    def _():
        bpe[0] = jnp.zeros((PIX, C1), BF16)

    @pl.when(tm == TM - 1)
    def _():
        bpe[FINE + 1] = jnp.zeros((PIX, C1), BF16)

    def input_grad(lo, hi):
        for t in range(0, FINE, 2):
            rows = [bpe[t + k : t + k + 2].reshape(2 * PIX, C1) for k in range(3)]
            acc = dot_last(rows[2], wt[lo:hi, :])
            acc += dot_last(rows[1], wt[C1 + lo : C1 + hi, :])
            acc += dot_last(rows[0], wt[2 * C1 + lo : 2 * C1 + hi, :])
            acc = acc.reshape(2, PIX, hi - lo) + gs[t : t + 2, :, lo:hi].astype(F32) + spread[:, lo:hi]
            gs[t : t + 2, :, lo:hi] = acc.astype(BF16)

    input_grad(*COLS_FINE[0])
    ring_y.middle()
    input_grad(*COLS_FINE[1])
    ring_x.middle()
    input_grad(*COLS_FINE[2])
    store = pltpu.make_async_copy(gs, ig_out.at[0], local_sem.at[16])
    store.start()

    ring_y.arrived()
    for h in range(DP):
        p2_y[:, h] = ring_y.total(h).astype(BF16).reshape(XS, 16, C1)
    ring2_y = Ring(remote, p2_y, (y2_ra, y2_rb, y2_fp, y2_fm), x, x_plus, x_minus, 98)
    ring2_y.start()
    ring_x.arrived()
    for part_y in range(YS):
        p2_x[part_y] = ring_x.total(part_y).astype(BF16)
    ring2_x = Ring(remote, p2_x, (x2_ra, x2_rb, x2_fp, x2_fm), y, y_plus, y_minus, 104)
    ring2_x.start()
    ring2_y.middle()
    ring2_x.middle()
    ring2_y.arrived()
    for h in range(DP):
        z_buf[0, h] = ring2_y.total(h).astype(BF16)
    ring2_x.arrived()
    for h in range(DP):
        z_buf[1, h, :, :DC] = ring2_x.total(h).astype(BF16)
        z_buf[1, h, :, DC:] = jnp.zeros((16, C1 - DC), BF16)

    z_copies = [
        send(remote(z_buf.at[z % 2, z // 2], z_recv.at[k], 110 + k, peers_z[k])) for k, z in enumerate(on_z)
    ]
    total = z_buf[zlo, dp].astype(F32)
    for k in range(7):
        z_copies[k].wait_recv()
        total += z_recv[k].astype(F32)
    final[tm] = total.astype(BF16)
    for k in range(1, TM):
        send(remote(final.at[tm], final.at[tm], 117 + k, peers_tm[k - 1]))
    for k in range(1, TM):
        src = (tm + TM - k) % TM
        remote(final.at[src], final.at[src], 117 + k, at(tm_=src)).wait_recv()
    sums_out[...] = final[...]

    for copy in sent:
        copy.wait_send()
    for ring in (ring_x, ring_y, ring2_x, ring2_y):
        ring.finish()
    store.wait()


def finish(ig, sums, ig_out, time_out, down_out, sem):
    copy = pltpu.make_async_copy(ig, ig_out, sem)
    copy.start()
    odd = lax.axis_index("dp") % 2 == 1
    scale = 1.0 / math.sqrt(ROWS_ALL)
    rows = sums[:XS].astype(F32).reshape(64, C1) * scale
    time_out[...] = jnp.where(odd, rows[4:64], rows[:60])
    wide = jnp.concatenate([sums[XS + part_x, :, :DC] for part_x in range(XS)], axis=1).astype(F32) * (0.25 * scale)
    rows = jnp.concatenate([wide[:, :C2], open_tail(wide[:, C2 : C2 + C1])], axis=0)
    down_out[...] = jnp.where(odd, rows[4:24], rows[:20])
    copy.wait()


def shards(*args):
    v, hbm = pltpu.VMEM, pl.BlockSpec(memory_space=pl.ANY)
    vmem = pl.BlockSpec(memory_space=pltpu.VMEM)
    scratch = [
        v((FINE + 2, PIX, C1), BF16), v((3 * C1, C1), BF16), v((C1, C2), BF16), v((C2, C2), BF16), v((C2, C2), BF16),
        v((FINE, PIX, C1), BF16), v((PIX, C2), BF16), v((FINE, PIX, C1), F32), v((PIX, C1), BF16),
        v((PIX, C2), F32), v((PIX, C2), F32), v((PIX, C2), F32),
        v((PIX, C2), BF16), v((PIX, C2), BF16), v((PIX, C2), BF16), v((PIX, C2), BF16),
        *[v((CHUNKS, TM, 16, C1), BF16)] * 6,
        v((PIX, C2), BF16), v((PIX, C1), F32), v((FINE + 2, PIX, C1), BF16),
        v((3 * C1, C1), F32), v((C1, C2), F32),
        v((YS, DP, 64, C1), BF16), v((XS, YS, DP, 16, DC), BF16),
        v((YS, DP, 64, C1), BF16), v((XS, YS, DP, 16, DC), BF16),
        *[v((2, 64, C1), BF16)] * 2, *[v((4, 64, C1), BF16)] * 2,
        *[v((2, DP, 16, DC), BF16)] * 2, *[v((4, DP, 16, DC), BF16)] * 2,
        v((XS, DP, 16, C1), BF16), v((YS, DP, 16, DC), BF16),
        *[v((2, 16, C1), BF16)] * 2, *[v((4, 16, C1), BF16)] * 2,
        *[v((2, 16, DC), BF16)] * 2, *[v((4, 16, DC), BF16)] * 2,
        v((2, DP, 16, C1), BF16), v((7, 16, C1), BF16), v((TM, 16, C1), BF16),
        pltpu.SemaphoreType.DMA((17,)), pltpu.SemaphoreType.DMA((125,)), pltpu.SemaphoreType.DMA((125,)),
    ]
    fine = jax.ShapeDtypeStruct((1, FINE, PIX, C1), BF16)
    ig, sums = pl.pallas_call(
        kernel,
        out_shape=(fine, jax.ShapeDtypeStruct((TM, 16, C1), BF16)),
        in_specs=[hbm] * 7,
        out_specs=(hbm, vmem),
        scratch_shapes=scratch,
        compiler_params=pltpu.CompilerParams(
            collective_id=0, has_side_effects=True, vmem_limit_bytes=60 * 1024 * 1024
        ),
        cost_estimate=pl.CostEstimate(flops=9 * 10**9, bytes_accessed=16 * 10**6, transcendentals=10**6),
    )(*args)
    return pl.pallas_call(
        finish,
        out_shape=(fine, jax.ShapeDtypeStruct((60, C1), F32), jax.ShapeDtypeStruct((20, C2), F32)),
        in_specs=[hbm, vmem],
        out_specs=(hbm, vmem, vmem),
        scratch_shapes=[pltpu.SemaphoreType.DMA],
        cost_estimate=pl.CostEstimate(flops=10**5, bytes_accessed=2 * 10**6, transcendentals=0),
    )(ig, sums)


def solution(mesh):
    fine, whole = P("dp", "tm", "space", None), P()
    rows = P(("space", "dp"), None)
    return jax.shard_map(
        shards,
        mesh=mesh,
        in_specs=(fine, whole, whole, whole, whole, fine, fine),
        out_specs=(fine, rows, rows),
        check_vma=False,
    )
```

```python
import math

import jax
import jax.numpy as jnp
from jax import lax
from jax.experimental import pallas as pl
from jax.experimental.pallas import tpu as pltpu
from jax.sharding import PartitionSpec as P

C1, C2, DH = 640, 1280, 64
TM, YS, XS, DP = 8, 4, 4, 4
FINE, PIX = 4, 192
ROWS_ALL = 4 * 32 * 1536
EPS = 1e-06
MESH = pl.DeviceIdType.MESH
F32, BF16 = jnp.float32, jnp.bfloat16
COLS_FINE = ((0, 256), (256, 512), (512, 640))
COLS_COARSE = tuple((n, n + 256) for n in range(0, C2, 256))
CHUNKS, WIDE = 3, 64
DC = 512
TILES = 5


def dot(left, right):
    return jnp.dot(left, right, preferred_element_type=F32)


def dot_last(left, right):
    return lax.dot_general(left, right, (((1,), (1,)), ((), ())), preferred_element_type=F32)


def dot_first(left, right):
    return lax.dot_general(left, right, (((0,), (0,)), ((), ())), preferred_element_type=F32)


def fold_tail(tail):
    return jnp.concatenate([tail[:, :C1], tail[:, C1:]], axis=0)


def open_tail(tail):
    return jnp.concatenate([tail[:8], tail[8:]], axis=1)


class Ring:
    def __init__(self, remote, parts, bufs, pos, plus, minus, first):
        self.parts, self.pos = parts, pos
        self.ra, self.rb, self.fp, self.fm = bufs
        lo, hi = pl.ds(0, 2), pl.ds(2, 2)
        self.ahead, self.behind, self.far = (pos + 1) % 4, (pos + 3) % 4, (pos + 2) % 4
        self.copies = [
            remote(parts.at[self.far, lo], self.ra, first, plus),
            remote(parts.at[self.far, hi], self.rb, first + 1, minus),
            remote(parts.at[self.ahead, hi], self.fp.at[hi], first + 2, plus),
            remote(parts.at[self.behind, lo], self.fm.at[lo], first + 3, minus),
            remote(parts.at[self.ahead, lo], self.fp.at[lo], first + 4, plus),
            remote(parts.at[self.behind, hi], self.fm.at[hi], first + 5, minus),
        ]

    def start(self):
        for copy in self.copies[:4]:
            copy.start()

    def middle(self):
        parts = self.parts
        self.copies[0].wait_recv()
        parts[self.ahead, 0:2] = (parts[self.ahead, 0:2].astype(F32) + self.ra[...].astype(F32)).astype(BF16)
        self.copies[4].start()
        self.copies[1].wait_recv()
        parts[self.behind, 2:4] = (parts[self.behind, 2:4].astype(F32) + self.rb[...].astype(F32)).astype(BF16)
        self.copies[5].start()

    def arrived(self):
        for copy in self.copies[2:]:
            copy.wait_recv()

    def total(self, i):
        return self.parts[self.pos, i].astype(F32) + self.fp[i].astype(F32) + self.fm[i].astype(F32)

    def finish(self):
        for copy in self.copies:
            copy.wait_send()


def attend(tiles, qf, kf, cb, gb, work, bq, bk):
    row_i = lax.broadcasted_iota(jnp.int32, (128, 128), 0)
    col_i = lax.broadcasted_iota(jnp.int32, (128, 128), 1)
    ones = ((row_i // DH) == (col_i // DH)).astype(F32).astype(BF16)
    mask = ((row_i[:WIDE] % 8) == (col_i[:WIDE] % 8)).astype(F32)
    left = (lax.broadcasted_iota(jnp.int32, (WIDE, 128), 1) < DH).astype(F32)
    left_b, right_b = left.astype(BF16), (1.0 - left).astype(BF16)
    count = len(tiles)
    units = [(i, slice(WIDE * g, WIDE * g + WIDE)) for i in range(count) for g in range(CHUNKS)]
    index = range(len(units))

    def heads(rows):
        return jnp.concatenate([rows * left_b, rows * right_b], axis=0)

    def fold(both):
        return jnp.where(left > 0.5, both[:WIDE], both[WIDE:])

    def head_sums(terms):
        sums = dot(jnp.concatenate([term.astype(BF16) for term in terms], axis=0), ones)
        rows = terms[0].shape[0]
        return [sums[rows * i : rows * i + rows] for i in range(len(terms))]

    q, k = [qf[:, c] for c in tiles], [kf[:, c] for c in tiles]
    factors = [lax.rsqrt(total * (1.0 / DH) + EPS) for total in head_sums([v * v for v in q + k])]
    rq, rk = factors[:count], factors[count:]
    qb = [(q[i] * rq[i]).astype(BF16) for i in range(count)]
    kb = [(k[i] * rk[i]).astype(BF16) for i in range(count)]
    queries = [qb[i][rows] for i, rows in units]
    keys = [heads(kb[i][rows]) for i, rows in units]
    raised = [jnp.exp(dot_last(queries[n], keys[n]) * 0.125) * mask for n in index]
    upstream = [gb[rows, tiles[i]] for i, rows in units]
    back_probs = [dot_last(upstream[n], heads(cb[rows, tiles[i]])) for n, (i, rows) in enumerate(units)]
    probs = [over / under for over, under in zip(raised, head_sums(raised))]
    means = head_sums([p * b for p, b in zip(probs, back_probs)])
    scores = [(p * (b - m)).astype(BF16) for p, b, m in zip(probs, back_probs, means)]
    for n, (i, rows) in enumerate(units):
        values = fold(dot_first(probs[n].astype(BF16), upstream[n]))
        work[rows, tiles[i]] = upstream[n].astype(F32) + values
    back_q = [dot(scores[n], keys[n]) * 0.125 for n in index]
    back_k = [fold(dot_first(scores[n], queries[n])) * 0.125 for n in index]
    qn = [rows.astype(F32) for rows in queries]
    kn = [kb[i][rows].astype(F32) for i, rows in units]
    mean_q = head_sums([b * v for b, v in zip(back_q, qn)])
    mean_k = head_sums([b * v for b, v in zip(back_k, kn)])
    for n, (i, rows) in enumerate(units):
        bq[rows, tiles[i]] = (rq[i][rows] * (back_q[n] - qn[n] * (mean_q[n] * (1.0 / DH)))).astype(BF16)
        bk[rows, tiles[i]] = (rk[i][rows] * (back_k[n] - kn[n] * (mean_k[n] * (1.0 / DH)))).astype(BF16)


def kernel(
    frames, w_time, w_down, w_query, w_key, grad_skip, grad_out,
    ig_out, sums_out,
    ext, wt, wd, wq, wk, gs, go, pre, skipsum, work, qf, kf, cb, gb, bq, bk,
    g_send, g_recv, c_send, c_recv, b_send, b_recv, bc, spread, bpe,
    t_sum, d_sum, cs_y, cs_x, p_y, p_x, y_ra, y_rb, y_fp, y_fm, x_ra, x_rb, x_fp, x_fm,
    p2_y, p2_x, r2_y, r2_x,
    z_buf, z_recv, final,
    local_sem, send_sem, recv_sem,
):
    tm, space, dp = lax.axis_index("tm"), lax.axis_index("space"), lax.axis_index("dp")
    core, y, zlo, x = space % 2, space // 2, tm // XS, tm % XS

    def at(tm_=None, space_=None, dp_=None):
        return {
            "tm": tm if tm_ is None else tm_,
            "space": space if space_ is None else space_,
            "dp": dp if dp_ is None else dp_,
        }

    loads = [
        pltpu.make_async_copy(src, dst, local_sem.at[i])
        for i, (src, dst) in enumerate(
            (
                (frames.at[0], ext.at[pl.ds(1, FINE)]),
                (w_time, wt),
                (w_down, wd),
                (grad_out.at[0, 0], go),
                (w_query, wq),
                (w_key, wk),
                (grad_skip.at[0], gs),
            )
        )
    ]
    loads[0].start()
    loads[1].start()

    peers_tm = [at(tm_=(tm + k) % TM) for k in range(1, TM)]
    partner = at(space_=y * 2 + 1 - core)
    peers_y = [at(space_=((y + k) % YS) * 2 + core) for k in range(1, YS)]
    peers_x = [at(tm_=zlo * XS + (x + k) % XS) for k in range(1, XS)]
    zpos = dp * 2 + zlo
    on_z = [(zpos + k) % 8 for k in range(1, 8)]
    peers_z = [at(tm_=z % 2 * XS + x, dp_=z // 2) for z in on_z]
    barrier = pltpu.get_barrier_semaphore()
    other_z = [at(tm_=tm_, dp_=(dp + k) % DP) for k in range(1, DP) for tm_ in (x, XS + x)]
    greeted = peers_tm + [partner] + peers_y + other_z
    for peer in greeted:
        pl.semaphore_signal(barrier, inc=1, device_id=peer, device_id_type=MESH)
    pl.semaphore_wait(barrier, len(greeted))

    def remote(src, dst, sem, device, landed=None):
        return pltpu.make_async_remote_copy(
            src_ref=src,
            dst_ref=dst,
            send_sem=send_sem.at[sem],
            recv_sem=recv_sem.at[sem if landed is None else landed],
            device_id=device,
            device_id_type=MESH,
        )

    def exchange(send, recv, c, first):
        copies = [
            remote(send.at[c, (tm + k) % TM], recv.at[c, tm], first + k, at(tm_=(tm + k) % TM)) for k in range(1, TM)
        ]
        own = pltpu.make_async_copy(send.at[c, tm], recv.at[c, tm], local_sem.at[7 + first // TM])
        for copy in copies:
            copy.start()
        own.start()

        def receive():
            for k in range(1, TM):
                src = (tm + TM - k) % TM
                remote(send.at[c, src], recv.at[c, src], first + k, at(tm_=src)).wait_recv()
            own.wait()

        sent.extend(copies)
        return receive

    sent = []

    def send(copy):
        copy.start()
        sent.append(copy)
        return copy

    def pack(src, dst, c):
        rows = src[c * WIDE : (c + 1) * WIDE, :].astype(F32)
        for f in range(TM):
            dst[c, f] = fold_tail(rows[8 * f : 8 * f + 8]).astype(BF16)

    def unpack(src, dst, c):
        rows = [open_tail(src[c, f].astype(F32)) for f in range(TM)]
        dst[c * WIDE : (c + 1) * WIDE, :] = jnp.concatenate(rows, axis=0).astype(BF16)

    prev, nxt = at(tm_=(tm + TM - 1) % TM), at(tm_=(tm + 1) % TM)
    halos = []
    for c in range(CHUNKS):
        rows = pl.ds(c * WIDE, WIDE)
        first = send(remote(frames.at[0, 0, rows], ext.at[FINE + 1, rows], 72 + 2 * c, prev))
        last = send(remote(frames.at[0, FINE - 1, rows], ext.at[0, rows], 73 + 2 * c, nxt))
        halos.append((first, last))
    for load in loads[2:]:
        load.start()

    loads[0].wait()
    loads[1].wait()
    for lo, hi in COLS_FINE:
        n = hi - lo
        pre[:, :, lo:hi] = dot(ext[1:5].reshape(FINE * PIX, C1), wt[C1 : 2 * C1, lo:hi]).reshape(FINE, PIX, n)
        pre[1:4, :, lo:hi] += dot(ext[1:4].reshape(3 * PIX, C1), wt[:C1, lo:hi]).reshape(3, PIX, n)
        pre[0:3, :, lo:hi] += dot(ext[2:5].reshape(3 * PIX, C1), wt[2 * C1 :, lo:hi]).reshape(3, PIX, n)
    loads[3].wait()
    for c in range(CHUNKS):
        pack(go, g_send, c)

    loads[2].wait()
    c_receive, g_receive = [], []
    for c in range(CHUNKS):
        rows = slice(c * WIDE, (c + 1) * WIDE)
        for copy in halos[c]:
            copy.wait_recv()

        @pl.when(tm == 0)
        def _():
            ext[0, rows] = jnp.zeros((WIDE, C1), BF16)

        @pl.when(tm == TM - 1)
        def _():
            ext[FINE + 1, rows] = jnp.zeros((WIDE, C1), BF16)

        for lo, hi in COLS_FINE:
            pre[0, rows, lo:hi] += dot(ext[0, rows], wt[:C1, lo:hi])
            pre[3, rows, lo:hi] += dot(ext[5, rows], wt[2 * C1 :, lo:hi])
            total = None
            for t in range(FINE):
                act = pre[t, rows, lo:hi]
                logistic = 1.0 / (1.0 + jnp.exp(-act))
                skip = (ext[t + 1, rows, lo:hi].astype(F32) + act * logistic).astype(BF16).astype(F32)
                total = skip if total is None else total + skip
                pre[t, rows, lo:hi] = logistic * (1.0 + act * (1.0 - logistic))
            skipsum[rows, lo:hi] = total.astype(BF16)
        for lo, hi in COLS_COARSE:
            work[rows, lo:hi] = 0.25 * dot(skipsum[rows, :], wd[:, lo:hi])
        pack(work, c_send, c)
        c_receive.append(exchange(c_send, c_recv, c, 8 * c))
    for c in range(CHUNKS):
        g_receive.append(exchange(g_send, g_recv, c, 24 + 8 * c))

    loads[4].wait()
    loads[5].wait()
    for c in range(CHUNKS):
        c_receive[c]()
        unpack(c_recv, cb, c)
    for lo, hi in COLS_COARSE:
        qf[:, lo:hi] = dot(cb[...], wq[:, lo:hi])
        kf[:, lo:hi] = dot(cb[...], wk[:, lo:hi])
    for c in range(CHUNKS):
        g_receive[c]()
        unpack(g_recv, gb, c)

    def attend_some(i, carry):
        tiles = [pl.ds(pl.multiple_of((i * TILES + u) * 128, 128), 128) for u in range(TILES)]
        attend(tiles, qf, kf, cb, gb, work, bq, bk)
        return carry

    lax.fori_loop(0, C2 // 128 // TILES, attend_some, 0)
    for lo, hi in COLS_COARSE:
        work[:, lo:hi] += dot_last(bq[...], wq[lo:hi, :]) + dot_last(bk[...], wk[lo:hi, :])
    b_receive = []
    for c in range(CHUNKS):
        pack(work, b_send, c)
        b_receive.append(exchange(b_send, b_recv, c, 48 + 8 * c))
    for c in range(CHUNKS):
        b_receive[c]()
        unpack(b_recv, bc, c)

    loads[6].wait()
    for lo, hi in COLS_FINE:
        spread[:, lo:hi] = 0.25 * dot_last(bc[...], wd[lo:hi, :])
        for t in range(FINE):
            back = gs[t, :, lo:hi].astype(F32) + spread[:, lo:hi]
            bpe[t + 1, :, lo:hi] = (back * pre[t, :, lo:hi]).astype(BF16)
    back_first = send(remote(bpe.at[1], bpe.at[FINE + 1], 78, prev))
    back_last = send(remote(bpe.at[FINE], bpe.at[0], 79, nxt))

    def time_unit(part_y, part_core, part_dp):
        start = pl.multiple_of(480 * part_y + 240 * part_core + 60 * part_dp // 8 * 8, 8)
        return t_sum[pl.ds(start, 64), :]

    def down_unit(part_y, part_core, part_dp):
        start = pl.multiple_of(160 * part_y + 80 * part_core + 20 * part_dp // 8 * 8, 8)
        rows = d_sum[pl.ds(start, 24), :]
        return jnp.concatenate([rows[:16], fold_tail(rows[16:]), jnp.zeros((16, 128), F32)], axis=1)

    swap_y = []
    back_rows = bpe[1 : FINE + 1].reshape(FINE * PIX, C1)
    for k in range(3):
        for lo, hi in COLS_FINE:
            block = ext[k : k + FINE, :, lo:hi].reshape(FINE * PIX, hi - lo)
            t_sum[k * C1 + lo : k * C1 + hi, :] = dot_first(block, back_rows)
            part_y = len(swap_y)
            if part_y < YS and k * C1 + hi >= 480 * (part_y + 1):
                for h in range(DP):
                    cs_y[part_y, h] = time_unit(part_y, 1 - core, h).astype(BF16)
                swap_y.append(send(remote(cs_y.at[part_y], p_y.at[part_y], 80 + part_y, partner)))

    for lo, hi in COLS_FINE:
        d_sum[lo:hi, :] = dot_first(skipsum[:, lo:hi], bc[...])

    def pack_down(part_y, carry):
        for h in range(DP):
            unit = down_unit(part_y, 1 - core, h).astype(BF16)
            for part_x in range(XS):
                cs_x[part_x, part_y, h] = unit[:, DC * part_x : DC * part_x + DC]
        return carry

    lax.fori_loop(0, YS, pack_down, 0)
    swap_x = send(remote(cs_x, p_x, 84, partner))

    ring_y = Ring(remote, p_y, (y_ra, y_rb, y_fp, y_fm), y, peers_y[0], peers_y[2], 86)
    for part_y, copies in (
        (ring_y.far, ring_y.copies[:2]),
        (ring_y.ahead, ring_y.copies[2:3]),
        (ring_y.behind, ring_y.copies[3:4]),
        (y, []),
    ):
        remote(cs_y.at[part_y], p_y.at[part_y], 80 + part_y, partner).wait_recv()
        for h in range(DP):
            p_y[part_y, h] = (p_y[part_y, h].astype(F32) + time_unit(part_y, core, h)).astype(BF16)
        for copy in copies:
            copy.start()

    swap_x.wait_recv()

    def add_down(part_y, carry):
        for h in range(DP):
            unit = down_unit(part_y, core, h)
            for part_x in range(XS):
                more = unit[:, DC * part_x : DC * part_x + DC]
                p_x[part_x, part_y, h] = (p_x[part_x, part_y, h].astype(F32) + more).astype(BF16)
        return carry

    lax.fori_loop(0, YS, add_down, 0)
    ring_x = Ring(remote, p_x, (x_ra, x_rb, x_fp, x_fm), x, peers_x[0], peers_x[2], 92)
    ring_x.start()

    back_first.wait_recv()
    back_last.wait_recv()

    @pl.when(tm == 0)
    def _():
        bpe[0] = jnp.zeros((PIX, C1), BF16)

    @pl.when(tm == TM - 1)
    def _():
        bpe[FINE + 1] = jnp.zeros((PIX, C1), BF16)

    def input_grad(lo, hi):
        for t in range(0, FINE, 2):
            rows = [bpe[t + k : t + k + 2].reshape(2 * PIX, C1) for k in range(3)]
            acc = dot_last(rows[2], wt[lo:hi, :])
            acc += dot_last(rows[1], wt[C1 + lo : C1 + hi, :])
            acc += dot_last(rows[0], wt[2 * C1 + lo : 2 * C1 + hi, :])
            acc = acc.reshape(2, PIX, hi - lo) + gs[t : t + 2, :, lo:hi].astype(F32) + spread[:, lo:hi]
            gs[t : t + 2, :, lo:hi] = acc.astype(BF16)

    input_grad(*COLS_FINE[0])
    input_grad(*COLS_FINE[1])
    ring_y.middle()
    input_grad(*COLS_FINE[2])
    ring_x.middle()
    store = pltpu.make_async_copy(gs, ig_out.at[0], local_sem.at[16])
    store.start()

    ring_y.arrived()
    for h in range(DP):
        p2_y[:, h] = ring_y.total(h).astype(BF16).reshape(XS, 16, C1)
    y_copies = [send(remote(p2_y.at[(x + k) % XS], r2_y.at[k - 1], 97 + k, peers_x[k - 1])) for k in range(1, XS)]
    ring_x.arrived()
    for part_y in range(YS):
        p2_x[part_y] = ring_x.total(part_y).astype(BF16)
    x_copies = [send(remote(p2_x.at[(y + k) % YS], r2_x.at[k - 1], 100 + k, peers_y[k - 1])) for k in range(1, YS)]
    for copy in y_copies:
        copy.wait_recv()
    z_buf[0] = (p2_y[x].astype(F32) + sum(r2_y[k].astype(F32) for k in range(XS - 1))).astype(BF16)
    for copy in x_copies:
        copy.wait_recv()
    z_buf[1, :, :, :DC] = (p2_x[y].astype(F32) + sum(r2_x[k].astype(F32) for k in range(YS - 1))).astype(BF16)
    z_buf[1, :, :, DC:] = jnp.zeros((DP, 16, C1 - DC), BF16)

    z_copies = [
        send(remote(z_buf.at[z % 2, z // 2], z_recv.at[k], 110 + k, peers_z[k])) for k, z in enumerate(on_z)
    ]
    total = z_buf[zlo, dp].astype(F32)
    for k in range(7):
        z_copies[k].wait_recv()
        total += z_recv[k].astype(F32)
    final[tm] = total.astype(BF16)
    for k in range(1, TM):
        send(remote(final.at[tm], final.at[tm], 117 + k, peers_tm[k - 1]))
    for k in range(1, TM):
        src = (tm + TM - k) % TM
        remote(final.at[src], final.at[src], 117 + k, at(tm_=src)).wait_recv()
    sums_out[...] = final[...]

    for copy in sent:
        copy.wait_send()
    for ring in (ring_x, ring_y):
        ring.finish()
    store.wait()


def finish(ig, sums, ig_out, time_out, down_out, held, load_sem, store_sem):
    loads = [pltpu.make_async_copy(ig.at[0, t], held.at[t], load_sem.at[t]) for t in range(FINE)]
    stores = [pltpu.make_async_copy(held.at[t], ig_out.at[0, t], store_sem.at[t]) for t in range(FINE)]
    for load in loads:
        load.start()
    odd = lax.axis_index("dp") % 2 == 1
    scale = 1.0 / math.sqrt(ROWS_ALL)
    rows = sums[:XS].astype(F32).reshape(64, C1) * scale
    time_out[...] = jnp.where(odd, rows[4:64], rows[:60])
    wide = jnp.concatenate([sums[XS + part_x, :, :DC] for part_x in range(XS)], axis=1).astype(F32) * (0.25 * scale)
    rows = jnp.concatenate([wide[:, :C2], open_tail(wide[:, C2 : C2 + C1])], axis=0)
    down_out[...] = jnp.where(odd, rows[4:24], rows[:20])
    for load, store in zip(loads, stores):
        load.wait()
        store.start()
    for store in stores:
        store.wait()


def shards(*args):
    v, hbm = pltpu.VMEM, pl.BlockSpec(memory_space=pl.ANY)
    vmem = pl.BlockSpec(memory_space=pltpu.VMEM)
    scratch = [
        v((FINE + 2, PIX, C1), BF16), v((3 * C1, C1), BF16), v((C1, C2), BF16), v((C2, C2), BF16), v((C2, C2), BF16),
        v((FINE, PIX, C1), BF16), v((PIX, C2), BF16), v((FINE, PIX, C1), F32), v((PIX, C1), BF16),
        v((PIX, C2), F32), v((PIX, C2), F32), v((PIX, C2), F32),
        v((PIX, C2), BF16), v((PIX, C2), BF16), v((PIX, C2), BF16), v((PIX, C2), BF16),
        *[v((CHUNKS, TM, 16, C1), BF16)] * 6,
        v((PIX, C2), BF16), v((PIX, C1), F32), v((FINE + 2, PIX, C1), BF16),
        v((3 * C1, C1), F32), v((C1, C2), F32),
        v((YS, DP, 64, C1), BF16), v((XS, YS, DP, 16, DC), BF16),
        v((YS, DP, 64, C1), BF16), v((XS, YS, DP, 16, DC), BF16),
        *[v((2, 64, C1), BF16)] * 2, *[v((4, 64, C1), BF16)] * 2,
        *[v((2, DP, 16, DC), BF16)] * 2, *[v((4, DP, 16, DC), BF16)] * 2,
        v((XS, DP, 16, C1), BF16), v((YS, DP, 16, DC), BF16),
        v((XS - 1, DP, 16, C1), BF16), v((YS - 1, DP, 16, DC), BF16),
        v((2, DP, 16, C1), BF16), v((7, 16, C1), BF16), v((TM, 16, C1), BF16),
        pltpu.SemaphoreType.DMA((17,)), pltpu.SemaphoreType.DMA((125,)), pltpu.SemaphoreType.DMA((125,)),
    ]
    fine = jax.ShapeDtypeStruct((1, FINE, PIX, C1), BF16)
    ig, sums = pl.pallas_call(
        kernel,
        out_shape=(fine, jax.ShapeDtypeStruct((TM, 16, C1), BF16)),
        in_specs=[hbm] * 7,
        out_specs=(hbm, vmem),
        scratch_shapes=scratch,
        compiler_params=pltpu.CompilerParams(
            collective_id=0, has_side_effects=True, vmem_limit_bytes=60 * 1024 * 1024
        ),
        cost_estimate=pl.CostEstimate(flops=9 * 10**9, bytes_accessed=16 * 10**6, transcendentals=10**6),
    )(*args)
    return pl.pallas_call(
        finish,
        out_shape=(fine, jax.ShapeDtypeStruct((60, C1), F32), jax.ShapeDtypeStruct((20, C2), F32)),
        in_specs=[hbm, vmem],
        out_specs=(hbm, vmem, vmem),
        scratch_shapes=[
            v((FINE, PIX, C1), BF16),
            pltpu.SemaphoreType.DMA((FINE,)),
            pltpu.SemaphoreType.DMA((FINE,)),
        ],
        cost_estimate=pl.CostEstimate(flops=10**5, bytes_accessed=2 * 10**6, transcendentals=0),
    )(ig, sums)


def solution(mesh):
    fine, whole = P("dp", "tm", "space", None), P()
    rows = P(("space", "dp"), None)
    return jax.shard_map(
        shards,
        mesh=mesh,
        in_specs=(fine, whole, whole, whole, whole, fine, fine),
        out_specs=(fine, rows, rows),
        check_vma=False,
    )
```

```python
import math

import jax
import jax.numpy as jnp
from jax import lax
from jax.experimental import pallas as pl
from jax.experimental.pallas import tpu as pltpu
from jax.sharding import PartitionSpec as P

C1, C2, DH = 640, 1280, 64
TM, YS, XS, DP = 8, 4, 4, 4
FINE, PIX = 4, 192
ROWS_ALL = 4 * 32 * 1536
EPS = 1e-06
MESH = pl.DeviceIdType.MESH
F32, BF16 = jnp.float32, jnp.bfloat16
COLS_FINE = ((0, 256), (256, 512), (512, 640))
COLS_COARSE = tuple((n, n + 256) for n in range(0, C2, 256))
CHUNKS, WIDE = 3, 64
DC = 512
TILES = 5
PIECES = ((0, 384), (384, 640))


def dot(left, right):
    return jnp.dot(left, right, preferred_element_type=F32)


def dot_last(left, right):
    return lax.dot_general(left, right, (((1,), (1,)), ((), ())), preferred_element_type=F32)


def dot_first(left, right):
    return lax.dot_general(left, right, (((0,), (0,)), ((), ())), preferred_element_type=F32)


def fold_tail(tail):
    return jnp.concatenate([tail[:, :C1], tail[:, C1:]], axis=0)


def open_tail(tail):
    return jnp.concatenate([tail[:8], tail[8:]], axis=1)


class Ring:
    def __init__(self, remote, parts, bufs, pos, plus, minus, first):
        self.parts, self.pos = parts, pos
        self.ra, self.rb, self.fp, self.fm = bufs
        lo, hi = pl.ds(0, 2), pl.ds(2, 2)
        self.ahead, self.behind, self.far = (pos + 1) % 4, (pos + 3) % 4, (pos + 2) % 4
        self.copies = [
            remote(parts.at[self.far, lo], self.ra, first, plus),
            remote(parts.at[self.far, hi], self.rb, first + 1, minus),
            remote(parts.at[self.ahead, hi], self.fp.at[hi], first + 2, plus),
            remote(parts.at[self.behind, lo], self.fm.at[lo], first + 3, minus),
            remote(parts.at[self.ahead, lo], self.fp.at[lo], first + 4, plus),
            remote(parts.at[self.behind, hi], self.fm.at[hi], first + 5, minus),
        ]

    def start(self):
        for copy in self.copies[:4]:
            copy.start()

    def middle(self):
        parts = self.parts
        self.copies[0].wait_recv()
        parts[self.ahead, 0:2] = (parts[self.ahead, 0:2].astype(F32) + self.ra[...].astype(F32)).astype(BF16)
        self.copies[4].start()
        self.copies[1].wait_recv()
        parts[self.behind, 2:4] = (parts[self.behind, 2:4].astype(F32) + self.rb[...].astype(F32)).astype(BF16)
        self.copies[5].start()

    def arrived(self):
        for copy in self.copies[2:]:
            copy.wait_recv()

    def total(self, i):
        return self.parts[self.pos, i].astype(F32) + self.fp[i].astype(F32) + self.fm[i].astype(F32)

    def finish(self):
        for copy in self.copies:
            copy.wait_send()


def attend_units(tiles):
    return [(i, slice(WIDE * g, WIDE * g + WIDE)) for i in range(len(tiles)) for g in range(CHUNKS)]


def pair_ones():
    rows, cols = (lax.broadcasted_iota(jnp.int32, (128, 128), d) for d in (0, 1))
    return ((rows // DH) == (cols // DH)).astype(F32).astype(BF16)


def pair_left():
    return (lax.broadcasted_iota(jnp.int32, (WIDE, 128), 1) < DH).astype(F32)


def pair_rows(rows):
    left = pair_left()
    return jnp.concatenate([rows * left.astype(BF16), rows * (1.0 - left).astype(BF16)], axis=0)


def head_sums(terms):
    sums = dot(jnp.concatenate([term.astype(BF16) for term in terms], axis=0), pair_ones())
    rows = terms[0].shape[0]
    return [sums[rows * i : rows * i + rows] for i in range(len(terms))]


def attend_scores(tiles, qf, kf, probs_ref, bq, bk):
    row_i, col_i = (lax.broadcasted_iota(jnp.int32, (WIDE, 128), d) for d in (0, 1))
    mask = ((row_i % 8) == (col_i % 8)).astype(F32)
    count, units = len(tiles), attend_units(tiles)
    q, k = [qf[:, c] for c in tiles], [kf[:, c] for c in tiles]
    factors = [lax.rsqrt(total * (1.0 / DH) + EPS) for total in head_sums([v * v for v in q + k])]
    qb = [(q[i] * factors[i]).astype(BF16) for i in range(count)]
    kb = [(k[i] * factors[count + i]).astype(BF16) for i in range(count)]
    for i, c in enumerate(tiles):
        qf[:, c], kf[:, c] = factors[i], factors[count + i]
        bq[:, c], bk[:, c] = qb[i], kb[i]
    raised = [jnp.exp(dot_last(qb[i][rows], pair_rows(kb[i][rows])) * 0.125) * mask for i, rows in units]
    for (i, rows), over, under in zip(units, raised, head_sums(raised)):
        probs_ref[rows, tiles[i]] = over / under


def attend_back(tiles, qf, kf, probs_ref, cb, gb, work, bq, bk):
    units = attend_units(tiles)
    index, left = range(len(units)), pair_left()

    def fold(both):
        return jnp.where(left > 0.5, both[:WIDE], both[WIDE:])

    queries = [bq[rows, tiles[i]] for i, rows in units]
    plain_keys = [bk[rows, tiles[i]] for i, rows in units]
    keys = [pair_rows(rows) for rows in plain_keys]
    upstream = [gb[rows, tiles[i]] for i, rows in units]
    probs = [probs_ref[rows, tiles[i]] for i, rows in units]
    back_probs = [dot_last(upstream[n], pair_rows(cb[rows, tiles[i]])) for n, (i, rows) in enumerate(units)]
    means = head_sums([p * b for p, b in zip(probs, back_probs)])
    scores = [(p * (b - m)).astype(BF16) for p, b, m in zip(probs, back_probs, means)]
    for n, (i, rows) in enumerate(units):
        values = fold(dot_first(probs[n].astype(BF16), upstream[n]))
        work[rows, tiles[i]] = upstream[n].astype(F32) + values
    back_q = [dot(scores[n], keys[n]) * 0.125 for n in index]
    back_k = [fold(dot_first(scores[n], queries[n])) * 0.125 for n in index]
    qn, kn = [rows.astype(F32) for rows in queries], [rows.astype(F32) for rows in plain_keys]
    mean_q = head_sums([b * v for b, v in zip(back_q, qn)])
    mean_k = head_sums([b * v for b, v in zip(back_k, kn)])
    for n, (i, rows) in enumerate(units):
        c = tiles[i]
        bq[rows, c] = (qf[rows, c] * (back_q[n] - qn[n] * (mean_q[n] * (1.0 / DH)))).astype(BF16)
        bk[rows, c] = (kf[rows, c] * (back_k[n] - kn[n] * (mean_k[n] * (1.0 / DH)))).astype(BF16)


def kernel(
    frames, w_time, w_down, w_query, w_key, grad_skip, grad_out,
    ig_out, time0_out, time1_out, down_out,
    ext, wt, wd, wq, wk, gs, go, pre, skipsum, work, qf, kf, cb, gb, bq, bk, probs,
    g_send, g_recv, c_send, c_recv, b_send, b_recv, bc, spread, bpe, t_sum, d_sum,
    cs_0, p_0, ra_0, rb_0, fp_0, fm_0, p2_0, r2_0, zs_0, zr_0, f_0,
    cs_1, p_1, ra_1, rb_1, fp_1, fm_1, p2_1, r2_1, zs_1, zr_1, f_1,
    cs_x, p_x, x_ra, x_rb, x_fp, x_fm, p2_x, r2_x, zs_x, zr_x, f_x,
    local_sem, send_sem, recv_sem,
):
    tm, space, dp = lax.axis_index("tm"), lax.axis_index("space"), lax.axis_index("dp")
    core, y, zlo, x = space % 2, space // 2, tm // XS, tm % XS

    def at(tm_=None, space_=None, dp_=None):
        return {
            "tm": tm if tm_ is None else tm_,
            "space": space if space_ is None else space_,
            "dp": dp if dp_ is None else dp_,
        }

    loads = [
        pltpu.make_async_copy(src, dst, local_sem.at[i])
        for i, (src, dst) in enumerate(
            (
                (frames.at[0], ext.at[pl.ds(1, FINE)]),
                (w_time, wt),
                (w_down, wd),
                (grad_out.at[0, 0], go),
                (w_query, wq),
                (w_key, wk),
                (grad_skip.at[0], gs),
            )
        )
    ]
    loads[0].start()
    loads[1].start()

    peers_tm = [at(tm_=(tm + k) % TM) for k in range(1, TM)]
    partner = at(space_=y * 2 + 1 - core)
    peers_y = [at(space_=((y + k) % YS) * 2 + core) for k in range(1, YS)]
    peers_x = [at(tm_=zlo * XS + (x + k) % XS) for k in range(1, XS)]
    zpos = dp * 2 + zlo
    on_z = [(zpos + k) % 8 for k in range(1, 8)]
    peers_z = [at(tm_=z % 2 * XS + x, dp_=z // 2) for z in on_z]
    barrier = pltpu.get_barrier_semaphore()
    other_z = [at(tm_=tm_, dp_=(dp + k) % DP) for k in range(1, DP) for tm_ in (x, XS + x)]
    greeted = peers_tm + [partner] + peers_y + other_z
    for peer in greeted:
        pl.semaphore_signal(barrier, inc=1, device_id=peer, device_id_type=MESH)
    pl.semaphore_wait(barrier, len(greeted))

    def remote(src, dst, sem, device, landed=None):
        return pltpu.make_async_remote_copy(
            src_ref=src,
            dst_ref=dst,
            send_sem=send_sem.at[sem],
            recv_sem=recv_sem.at[sem if landed is None else landed],
            device_id=device,
            device_id_type=MESH,
        )

    def exchange(send, recv, c, first):
        copies = [
            remote(send.at[c, (tm + k) % TM], recv.at[c, tm], first + k, at(tm_=(tm + k) % TM)) for k in range(1, TM)
        ]
        own = pltpu.make_async_copy(send.at[c, tm], recv.at[c, tm], local_sem.at[7 + first // TM])
        for copy in copies:
            copy.start()
        own.start()

        def receive():
            for k in range(1, TM):
                src = (tm + TM - k) % TM
                remote(send.at[c, src], recv.at[c, src], first + k, at(tm_=src)).wait_recv()
            own.wait()

        sent.extend(copies)
        return receive

    sent = []

    def send(copy):
        copy.start()
        sent.append(copy)
        return copy

    def pack(src, dst, c):
        rows = src[c * WIDE : (c + 1) * WIDE, :].astype(F32)
        for f in range(TM):
            dst[c, f] = fold_tail(rows[8 * f : 8 * f + 8]).astype(BF16)

    def unpack(src, dst, c):
        rows = [open_tail(src[c, f].astype(F32)) for f in range(TM)]
        dst[c * WIDE : (c + 1) * WIDE, :] = jnp.concatenate(rows, axis=0).astype(BF16)

    prev, nxt = at(tm_=(tm + TM - 1) % TM), at(tm_=(tm + 1) % TM)
    halos = []
    for c in range(CHUNKS):
        rows = pl.ds(c * WIDE, WIDE)
        first = send(remote(frames.at[0, 0, rows], ext.at[FINE + 1, rows], 72 + 2 * c, prev))
        last = send(remote(frames.at[0, FINE - 1, rows], ext.at[0, rows], 73 + 2 * c, nxt))
        halos.append((first, last))
    for load in loads[2:]:
        load.start()

    loads[0].wait()
    loads[1].wait()
    for lo, hi in COLS_FINE:
        n = hi - lo
        pre[:, :, lo:hi] = dot(ext[1:5].reshape(FINE * PIX, C1), wt[C1 : 2 * C1, lo:hi]).reshape(FINE, PIX, n)
        pre[1:4, :, lo:hi] += dot(ext[1:4].reshape(3 * PIX, C1), wt[:C1, lo:hi]).reshape(3, PIX, n)
        pre[0:3, :, lo:hi] += dot(ext[2:5].reshape(3 * PIX, C1), wt[2 * C1 :, lo:hi]).reshape(3, PIX, n)
    loads[3].wait()
    for c in range(CHUNKS):
        pack(go, g_send, c)

    loads[2].wait()
    c_receive, g_receive = [], []
    for c in range(CHUNKS):
        rows = slice(c * WIDE, (c + 1) * WIDE)
        for copy in halos[c]:
            copy.wait_recv()

        @pl.when(tm == 0)
        def _():
            ext[0, rows] = jnp.zeros((WIDE, C1), BF16)

        @pl.when(tm == TM - 1)
        def _():
            ext[FINE + 1, rows] = jnp.zeros((WIDE, C1), BF16)

        for lo, hi in COLS_FINE:
            pre[0, rows, lo:hi] += dot(ext[0, rows], wt[:C1, lo:hi])
            pre[3, rows, lo:hi] += dot(ext[5, rows], wt[2 * C1 :, lo:hi])
            total = None
            for t in range(FINE):
                act = pre[t, rows, lo:hi]
                logistic = 1.0 / (1.0 + jnp.exp(-act))
                skip = (ext[t + 1, rows, lo:hi].astype(F32) + act * logistic).astype(BF16).astype(F32)
                total = skip if total is None else total + skip
                pre[t, rows, lo:hi] = logistic * (1.0 + act * (1.0 - logistic))
            skipsum[rows, lo:hi] = total.astype(BF16)
        for lo, hi in COLS_COARSE:
            work[rows, lo:hi] = 0.25 * dot(skipsum[rows, :], wd[:, lo:hi])
        pack(work, c_send, c)
        c_receive.append(exchange(c_send, c_recv, c, 8 * c))
    for c in range(CHUNKS):
        g_receive.append(exchange(g_send, g_recv, c, 24 + 8 * c))

    loads[4].wait()
    loads[5].wait()
    for c in range(CHUNKS):
        c_receive[c]()
        unpack(c_recv, cb, c)
    for lo, hi in COLS_COARSE:
        qf[:, lo:hi] = dot(cb[...], wq[:, lo:hi])
        kf[:, lo:hi] = dot(cb[...], wk[:, lo:hi])
    def tiles_of(i):
        return [pl.ds(pl.multiple_of((i * TILES + u) * 128, 128), 128) for u in range(TILES)]

    def some_scores(i, carry):
        attend_scores(tiles_of(i), qf, kf, probs, bq, bk)
        return carry

    def some_back(i, carry):
        attend_back(tiles_of(i), qf, kf, probs, cb, gb, work, bq, bk)
        return carry

    lax.fori_loop(0, C2 // 128 // TILES, some_scores, 0)
    for c in range(CHUNKS):
        g_receive[c]()
        unpack(g_recv, gb, c)
    lax.fori_loop(0, C2 // 128 // TILES, some_back, 0)
    for lo, hi in COLS_COARSE:
        work[:, lo:hi] += dot_last(bq[...], wq[lo:hi, :]) + dot_last(bk[...], wk[lo:hi, :])
    b_receive = []
    for c in range(CHUNKS):
        pack(work, b_send, c)
        b_receive.append(exchange(b_send, b_recv, c, 48 + 8 * c))
    for c in range(CHUNKS):
        b_receive[c]()
        unpack(b_recv, bc, c)

    loads[6].wait()
    for lo, hi in COLS_FINE:
        spread[:, lo:hi] = 0.25 * dot_last(bc[...], wd[lo:hi, :])
        for t in range(FINE):
            back = gs[t, :, lo:hi].astype(F32) + spread[:, lo:hi]
            bpe[t + 1, :, lo:hi] = (back * pre[t, :, lo:hi]).astype(BF16)
    back_first = send(remote(bpe.at[1], bpe.at[FINE + 1], 78, prev))
    back_last = send(remote(bpe.at[FINE], bpe.at[0], 79, nxt))

    def time_unit(part_y, part_core, part_dp, lo, hi):
        start = pl.multiple_of(480 * part_y + 240 * part_core + 60 * part_dp // 8 * 8, 8)
        return t_sum[pl.ds(start, 64), lo:hi]

    def down_unit(part_y, part_core, part_dp):
        start = pl.multiple_of(160 * part_y + 80 * part_core + 20 * part_dp // 8 * 8, 8)
        rows = d_sum[pl.ds(start, 24), :]
        return jnp.concatenate([rows[:16], fold_tail(rows[16:]), jnp.zeros((16, 128), F32)], axis=1)

    cs, parts_t = (cs_0, cs_1), (p_0, p_1)
    rings = [
        Ring(remote, p_0, (ra_0, rb_0, fp_0, fm_0), y, peers_y[0], peers_y[2], 80),
        Ring(remote, p_1, (ra_1, rb_1, fp_1, fm_1), y, peers_y[0], peers_y[2], 86),
    ]

    def time_grad(piece):
        left, right = PIECES[piece]
        back_rows = bpe[1 : FINE + 1, :, left:right].reshape(FINE * PIX, right - left)
        part_y = 0
        for k in range(3):
            for lo, hi in COLS_FINE:
                block = ext[k : k + FINE, :, lo:hi].reshape(FINE * PIX, hi - lo)
                t_sum[k * C1 + lo : k * C1 + hi, left:right] = dot_first(block, back_rows)
                if part_y < YS and k * C1 + hi >= 480 * (part_y + 1):
                    for h in range(DP):
                        cs[piece][part_y, h] = time_unit(part_y, 1 - core, h, left, right).astype(BF16)
                    send(remote(cs[piece].at[part_y], parts_t[piece].at[part_y], 98 + 4 * piece + part_y, partner))
                    part_y += 1

    def time_ring(piece):
        ring, parts = rings[piece], parts_t[piece]
        for part_y, copies in (
            (ring.far, ring.copies[:2]),
            (ring.ahead, ring.copies[2:3]),
            (ring.behind, ring.copies[3:4]),
            (y, []),
        ):
            remote(cs[piece].at[part_y], parts.at[part_y], 98 + 4 * piece + part_y, partner).wait_recv()
            for h in range(DP):
                parts[part_y, h] = (
                    parts[part_y, h].astype(F32) + time_unit(part_y, core, h, *PIECES[piece])
                ).astype(BF16)
            for copy in copies:
                copy.start()

    time_grad(0)
    time_grad(1)
    time_ring(0)
    for lo, hi in COLS_FINE:
        d_sum[lo:hi, :] = dot_first(skipsum[:, lo:hi], bc[...])

    def pack_down(part_y, carry):
        for h in range(DP):
            unit = down_unit(part_y, 1 - core, h).astype(BF16)
            for part_x in range(XS):
                cs_x[part_x, part_y, h] = unit[:, DC * part_x : DC * part_x + DC]
        return carry

    lax.fori_loop(0, YS, pack_down, 0)
    swap_x = send(remote(cs_x, p_x, 106, partner))
    time_ring(1)

    swap_x.wait_recv()

    def add_down(part_y, carry):
        for h in range(DP):
            unit = down_unit(part_y, core, h)
            for part_x in range(XS):
                more = unit[:, DC * part_x : DC * part_x + DC]
                p_x[part_x, part_y, h] = (p_x[part_x, part_y, h].astype(F32) + more).astype(BF16)
        return carry

    lax.fori_loop(0, YS, add_down, 0)
    ring_x = Ring(remote, p_x, (x_ra, x_rb, x_fp, x_fm), x, peers_x[0], peers_x[2], 92)
    ring_x.start()

    back_first.wait_recv()
    back_last.wait_recv()

    @pl.when(tm == 0)
    def _():
        bpe[0] = jnp.zeros((PIX, C1), BF16)

    @pl.when(tm == TM - 1)
    def _():
        bpe[FINE + 1] = jnp.zeros((PIX, C1), BF16)

    def input_grad(lo, hi):
        for t in range(0, FINE, 2):
            rows = [bpe[t + k : t + k + 2].reshape(2 * PIX, C1) for k in range(3)]
            acc = dot_last(rows[2], wt[lo:hi, :])
            acc += dot_last(rows[1], wt[C1 + lo : C1 + hi, :])
            acc += dot_last(rows[0], wt[2 * C1 + lo : 2 * C1 + hi, :])
            acc = acc.reshape(2, PIX, hi - lo) + gs[t : t + 2, :, lo:hi].astype(F32) + spread[:, lo:hi]
            gs[t : t + 2, :, lo:hi] = acc.astype(BF16)

    input_grad(*COLS_FINE[0])
    rings[0].middle()
    input_grad(*COLS_FINE[1])
    rings[1].middle()
    input_grad(*COLS_FINE[2])
    ring_x.middle()
    store = pltpu.make_async_copy(gs, ig_out.at[0], local_sem.at[16])
    store.start()

    def over_x(piece, p2, r2, first):
        ring = rings[piece]
        ring.arrived()
        for h in range(DP):
            p2[:, h] = ring.total(h).astype(BF16).reshape(p2.shape[0], 16, p2.shape[3])
        return [send(remote(p2.at[(x + k) % XS], r2.at[k - 1], first + k, peers_x[k - 1])) for k in range(1, XS)]

    def added(copies, own, more):
        for copy in copies:
            copy.wait_recv()
        return (own.astype(F32) + sum(more[k].astype(F32) for k in range(len(copies)))).astype(BF16)

    last_waits = []

    class OverZ:
        def __init__(self, src, slots, first, owner):
            self.src, self.slots, self.first, self.owner = src, slots, first, owner
            other = zlo if owner == 0 else 1 - zlo
            copies = []
            for k in range(DP):
                h = (dp + k) % DP
                slot = other * DP + k
                target = at(tm_=owner * XS + x, dp_=h)
                copies.append(remote(src.at[h], slots.at[slot], first + k, target, landed=first + slot))
            for copy in copies[1:]:
                copy.start()

            @pl.when(zlo != owner)
            def _():
                copies[0].start()

            def finish():
                for copy in copies[1:]:
                    copy.wait_send()

                @pl.when(zlo != owner)
                def _():
                    copies[0].wait_send()

            last_waits.append(finish)

        def gather(self, final, first):
            copies = [
                remote(final.at[x], final.at[x], first + k, peers_tm[k - 1], landed=first + TM + x)
                for k in range(1, TM)
            ]

            @pl.when(zlo == self.owner)
            def _():
                total = self.src[dp].astype(F32)
                for slot in range(1, 2 * DP):
                    ref = self.slots.at[slot]
                    remote(ref, ref, self.first + slot, partner).wait_recv()
                    total += self.slots[slot].astype(F32)
                final[x] = total.astype(BF16)
                for copy in copies:
                    copy.start()

            def finish():
                for k in range(1, XS):
                    ref = final.at[(x + k) % XS]
                    remote(ref, ref, first, partner, landed=first + TM + (x + k) % XS).wait_recv()

                @pl.when(zlo != self.owner)
                def _():
                    remote(final.at[x], final.at[x], first, partner, landed=first + TM + x).wait_recv()

                @pl.when(zlo == self.owner)
                def _():
                    for copy in copies:
                        copy.wait_send()

            last_waits.append(finish)

    copies_0 = over_x(0, p2_0, r2_0, 107)
    copies_1 = over_x(1, p2_1, r2_1, 110)
    ring_x.arrived()
    for part_y in range(YS):
        p2_x[part_y] = ring_x.total(part_y).astype(BF16)
    copies_x = [send(remote(p2_x.at[(y + k) % YS], r2_x.at[k - 1], 113 + k, peers_y[k - 1])) for k in range(1, YS)]
    zs_0[...] = added(copies_0, p2_0[x], r2_0)
    over_z0 = OverZ(zs_0, zr_0, 117, 0)
    zs_1[...] = added(copies_1, p2_1[x], r2_1)
    over_z1 = OverZ(zs_1, zr_1, 125, 1)
    sums = added(copies_x, p2_x[y], r2_x)
    for half in range(2):
        zs_x[half] = sums[:, :, half * DC // 2 : (half + 1) * DC // 2]
    z_copies = [
        send(remote(zs_x.at[z % 2, z // 2], zr_x.at[k], 133 + k, peers_z[k])) for k, z in enumerate(on_z)
    ]
    over_z0.gather(f_0, 140)
    over_z1.gather(f_1, 152)
    f_x[tm] = added(z_copies, zs_x[zlo, dp], zr_x)
    for k in range(1, TM):
        send(remote(f_x.at[tm], f_x.at[tm], 163 + k, peers_tm[k - 1]))
    for k in range(1, TM):
        src = (tm + TM - k) % TM
        remote(f_x.at[src], f_x.at[src], 163 + k, at(tm_=src)).wait_recv()
    for wait in last_waits:
        wait()
    time0_out[...], time1_out[...], down_out[...] = f_0[...], f_1[...], f_x[...]

    for copy in sent:
        copy.wait_send()
    for ring in rings + [ring_x]:
        ring.finish()
    store.wait()


def finish(ig, time0, time1, down, ig_out, time_out, down_out, held, load_sem, store_sem):
    loads = [pltpu.make_async_copy(ig.at[0, t], held.at[t], load_sem.at[t]) for t in range(FINE)]
    stores = [pltpu.make_async_copy(held.at[t], ig_out.at[0, t], store_sem.at[t]) for t in range(FINE)]
    for load in loads:
        load.start()
    odd = lax.axis_index("dp") % 2 == 1
    scale = 1.0 / math.sqrt(ROWS_ALL)
    rows = jnp.concatenate([time0[...], time1[...]], axis=2).astype(F32).reshape(64, C1) * scale
    time_out[...] = jnp.where(odd, rows[4:64], rows[:60])
    halves = [down[half * XS + part_x] for part_x in range(XS) for half in range(2)]
    wide = jnp.concatenate(halves, axis=1).astype(F32) * (0.25 * scale)
    rows = jnp.concatenate([wide[:, :C2], open_tail(wide[:, C2 : C2 + C1])], axis=0)
    down_out[...] = jnp.where(odd, rows[4:24], rows[:20])
    for load, store in zip(loads, stores):
        load.wait()
        store.start()
    for store in stores:
        store.wait()


def reduce_scratch(n):
    v = pltpu.VMEM
    return [
        v((YS, DP, 64, n), BF16), v((YS, DP, 64, n), BF16),
        v((2, 64, n), BF16), v((2, 64, n), BF16), v((4, 64, n), BF16), v((4, 64, n), BF16),
        v((XS, DP, 16, n), BF16), v((XS - 1, DP, 16, n), BF16),
        v((DP, 16, n), BF16), v((2 * DP, 16, n), BF16), v((XS, 16, n), BF16),
    ]


def shards(*args):
    v, hbm = pltpu.VMEM, pl.BlockSpec(memory_space=pl.ANY)
    vmem = pl.BlockSpec(memory_space=pltpu.VMEM)
    scratch = [
        v((FINE + 2, PIX, C1), BF16), v((3 * C1, C1), BF16), v((C1, C2), BF16), v((C2, C2), BF16), v((C2, C2), BF16),
        v((FINE, PIX, C1), BF16), v((PIX, C2), BF16), v((FINE, PIX, C1), F32), v((PIX, C1), BF16),
        v((PIX, C2), F32), v((PIX, C2), F32), v((PIX, C2), F32),
        v((PIX, C2), BF16), v((PIX, C2), BF16), v((PIX, C2), BF16), v((PIX, C2), BF16), v((PIX, C2), F32),
        *[v((CHUNKS, TM, 16, C1), BF16)] * 6,
        v((PIX, C2), BF16), v((PIX, C1), F32), v((FINE + 2, PIX, C1), BF16),
        v((3 * C1, C1), F32), v((C1, C2), F32),
        *[s for lo, hi in PIECES for s in reduce_scratch(hi - lo)],
        v((XS, YS, DP, 16, DC), BF16), v((XS, YS, DP, 16, DC), BF16),
        *[v((2, DP, 16, DC), BF16)] * 2, *[v((4, DP, 16, DC), BF16)] * 2,
        v((YS, DP, 16, DC), BF16), v((YS - 1, DP, 16, DC), BF16),
        v((2, DP, 16, DC // 2), BF16), v((7, 16, DC // 2), BF16), v((TM, 16, DC // 2), BF16),
        pltpu.SemaphoreType.DMA((17,)), pltpu.SemaphoreType.DMA((171,)), pltpu.SemaphoreType.DMA((171,)),
    ]
    fine = jax.ShapeDtypeStruct((1, FINE, PIX, C1), BF16)
    ig, *sums = pl.pallas_call(
        kernel,
        out_shape=(
            fine,
            *[jax.ShapeDtypeStruct((XS, 16, hi - lo), BF16) for lo, hi in PIECES],
            jax.ShapeDtypeStruct((TM, 16, DC // 2), BF16),
        ),
        in_specs=[hbm] * 7,
        out_specs=(hbm, vmem, vmem, vmem),
        scratch_shapes=scratch,
        compiler_params=pltpu.CompilerParams(
            collective_id=0, has_side_effects=True, vmem_limit_bytes=60 * 1024 * 1024
        ),
        cost_estimate=pl.CostEstimate(flops=9 * 10**9, bytes_accessed=16 * 10**6, transcendentals=10**6),
    )(*args)
    return pl.pallas_call(
        finish,
        out_shape=(fine, jax.ShapeDtypeStruct((60, C1), F32), jax.ShapeDtypeStruct((20, C2), F32)),
        in_specs=[hbm, vmem, vmem, vmem],
        out_specs=(hbm, vmem, vmem),
        scratch_shapes=[
            v((FINE, PIX, C1), BF16),
            pltpu.SemaphoreType.DMA((FINE,)),
            pltpu.SemaphoreType.DMA((FINE,)),
        ],
        cost_estimate=pl.CostEstimate(flops=10**5, bytes_accessed=2 * 10**6, transcendentals=0),
    )(ig, *sums)


def solution(mesh):
    fine, whole = P("dp", "tm", "space", None), P()
    rows = P(("space", "dp"), None)
    return jax.shard_map(
        shards,
        mesh=mesh,
        in_specs=(fine, whole, whole, whole, whole, fine, fine),
        out_specs=(fine, rows, rows),
        check_vma=False,
    )
```

```python
import math

import jax
import jax.numpy as jnp
from jax import lax
from jax.experimental import pallas as pl
from jax.experimental.pallas import tpu as pltpu
from jax.sharding import PartitionSpec as P

C1, C2, DH = 640, 1280, 64
TM, YS, XS, DP = 8, 4, 4, 4
FINE, PIX = 4, 192
ROWS_ALL = 4 * 32 * 1536
EPS = 1e-06
MESH = pl.DeviceIdType.MESH
F32, BF16 = jnp.float32, jnp.bfloat16
COLS_FINE = ((0, 256), (256, 512), (512, 640))
COLS_COARSE = tuple((n, n + 256) for n in range(0, C2, 256))
CHUNKS, WIDE = 3, 64
FOLD = 384
DC = 512
TILES = 5
PIECES = ((0, 384), (384, 640))


def dot(left, right):
    return jnp.dot(left, right, preferred_element_type=F32)


def dot_last(left, right):
    return lax.dot_general(left, right, (((1,), (1,)), ((), ())), preferred_element_type=F32)


def dot_first(left, right):
    return lax.dot_general(left, right, (((0,), (0,)), ((), ())), preferred_element_type=F32)


def fold_tail(tail):
    return jnp.concatenate([tail[:, :C1], tail[:, C1:]], axis=0)


def fold_fine(rows):
    rest = jnp.concatenate([rows[:, FOLD:], jnp.zeros((8, 2 * FOLD - C1), F32)], axis=1)
    return jnp.concatenate([rows[:, :FOLD], rest], axis=0)


def open_fine(rows):
    return jnp.concatenate([rows[:8], rows[8:, : C1 - FOLD]], axis=1)


def open_tail(tail):
    return jnp.concatenate([tail[:8], tail[8:]], axis=1)


class Ring:
    def __init__(self, remote, parts, bufs, pos, plus, minus, first):
        self.parts, self.pos = parts, pos
        self.ra, self.rb, self.fp, self.fm = bufs
        lo, hi = pl.ds(0, 2), pl.ds(2, 2)
        self.ahead, self.behind, self.far = (pos + 1) % 4, (pos + 3) % 4, (pos + 2) % 4
        self.copies = [
            remote(parts.at[self.far, lo], self.ra, first, plus),
            remote(parts.at[self.far, hi], self.rb, first + 1, minus),
            remote(parts.at[self.ahead, hi], self.fp.at[hi], first + 2, plus),
            remote(parts.at[self.behind, lo], self.fm.at[lo], first + 3, minus),
            remote(parts.at[self.ahead, lo], self.fp.at[lo], first + 4, plus),
            remote(parts.at[self.behind, hi], self.fm.at[hi], first + 5, minus),
        ]

    def start(self):
        for copy in self.copies[:4]:
            copy.start()

    def middle(self):
        parts = self.parts
        self.copies[0].wait_recv()
        parts[self.ahead, 0:2] = (parts[self.ahead, 0:2].astype(F32) + self.ra[...].astype(F32)).astype(BF16)
        self.copies[4].start()
        self.copies[1].wait_recv()
        parts[self.behind, 2:4] = (parts[self.behind, 2:4].astype(F32) + self.rb[...].astype(F32)).astype(BF16)
        self.copies[5].start()

    def arrived(self):
        for copy in self.copies[2:]:
            copy.wait_recv()

    def total(self, i):
        return self.parts[self.pos, i].astype(F32) + self.fp[i].astype(F32) + self.fm[i].astype(F32)

    def finish(self):
        for copy in self.copies:
            copy.wait_send()


def attend_units(tiles):
    return [(i, slice(WIDE * g, WIDE * g + WIDE)) for i in range(len(tiles)) for g in range(CHUNKS)]


def pair_ones():
    rows, cols = (lax.broadcasted_iota(jnp.int32, (128, 128), d) for d in (0, 1))
    return ((rows // DH) == (cols // DH)).astype(F32).astype(BF16)


def pair_left():
    return (lax.broadcasted_iota(jnp.int32, (WIDE, 128), 1) < DH).astype(F32)


def pair_rows(rows):
    left = pair_left()
    return jnp.concatenate([rows * left.astype(BF16), rows * (1.0 - left).astype(BF16)], axis=0)


def head_sums(terms):
    sums = dot(jnp.concatenate([term.astype(BF16) for term in terms], axis=0), pair_ones())
    rows = terms[0].shape[0]
    return [sums[rows * i : rows * i + rows] for i in range(len(terms))]


def attend_scores(tiles, qf, kf, probs_ref, bq, bk):
    row_i, col_i = (lax.broadcasted_iota(jnp.int32, (WIDE, 128), d) for d in (0, 1))
    mask = ((row_i % 8) == (col_i % 8)).astype(F32)
    count, units = len(tiles), attend_units(tiles)
    q, k = [qf[:, c] for c in tiles], [kf[:, c] for c in tiles]
    factors = [lax.rsqrt(total * (1.0 / DH) + EPS) for total in head_sums([v * v for v in q + k])]
    qb = [(q[i] * factors[i]).astype(BF16) for i in range(count)]
    kb = [(k[i] * factors[count + i]).astype(BF16) for i in range(count)]
    for i, c in enumerate(tiles):
        qf[:, c], kf[:, c] = factors[i], factors[count + i]
        bq[:, c], bk[:, c] = qb[i], kb[i]
    raised = [jnp.exp(dot_last(qb[i][rows], pair_rows(kb[i][rows])) * 0.125) * mask for i, rows in units]
    for (i, rows), over, under in zip(units, raised, head_sums(raised)):
        probs_ref[rows, tiles[i]] = over / under


def attend_back(tiles, qf, kf, probs_ref, cb, gb, work, bq, bk):
    units = attend_units(tiles)
    index, left = range(len(units)), pair_left()

    def fold(both):
        return jnp.where(left > 0.5, both[:WIDE], both[WIDE:])

    queries = [bq[rows, tiles[i]] for i, rows in units]
    plain_keys = [bk[rows, tiles[i]] for i, rows in units]
    keys = [pair_rows(rows) for rows in plain_keys]
    upstream = [gb[rows, tiles[i]] for i, rows in units]
    probs = [probs_ref[rows, tiles[i]] for i, rows in units]
    back_probs = [dot_last(upstream[n], pair_rows(cb[rows, tiles[i]])) for n, (i, rows) in enumerate(units)]
    means = head_sums([p * b for p, b in zip(probs, back_probs)])
    scores = [(p * (b - m)).astype(BF16) for p, b, m in zip(probs, back_probs, means)]
    for n, (i, rows) in enumerate(units):
        values = fold(dot_first(probs[n].astype(BF16), upstream[n]))
        work[rows, tiles[i]] = upstream[n].astype(F32) + values
    back_q = [dot(scores[n], keys[n]) * 0.125 for n in index]
    back_k = [fold(dot_first(scores[n], queries[n])) * 0.125 for n in index]
    qn, kn = [rows.astype(F32) for rows in queries], [rows.astype(F32) for rows in plain_keys]
    mean_q = head_sums([b * v for b, v in zip(back_q, qn)])
    mean_k = head_sums([b * v for b, v in zip(back_k, kn)])
    for n, (i, rows) in enumerate(units):
        c = tiles[i]
        bq[rows, c] = (qf[rows, c] * (back_q[n] - qn[n] * (mean_q[n] * (1.0 / DH)))).astype(BF16)
        bk[rows, c] = (kf[rows, c] * (back_k[n] - kn[n] * (mean_k[n] * (1.0 / DH)))).astype(BF16)


def kernel(
    frames, w_time, w_down, w_query, w_key, grad_skip, grad_out,
    ig_out, time0_out, time1_out, down_out,
    ext, wt, wd, wq, wk, gs, go, pre, skipsum, work, qf, kf, cb, gb, bq, bk, probs,
    g_send, g_recv, c_send, c_recv, b_send, b_recv, sk, bc, spread, bpe, t_sum, d_sum,
    cs_0, p_0, ra_0, rb_0, fp_0, fm_0, p2_0, r2_0, zs_0, zr_0, f_0,
    cs_1, p_1, ra_1, rb_1, fp_1, fm_1, p2_1, r2_1, zs_1, zr_1, f_1,
    cs_x, p_x, x_ra, x_rb, x_fp, x_fm, p2_x, r2_x, zs_x, zr_x, f_x,
    local_sem, send_sem, recv_sem,
):
    tm, space, dp = lax.axis_index("tm"), lax.axis_index("space"), lax.axis_index("dp")
    core, y, zlo, x = space % 2, space // 2, tm // XS, tm % XS

    def at(tm_=None, space_=None, dp_=None):
        return {
            "tm": tm if tm_ is None else tm_,
            "space": space if space_ is None else space_,
            "dp": dp if dp_ is None else dp_,
        }

    loads = [
        pltpu.make_async_copy(src, dst, local_sem.at[i])
        for i, (src, dst) in enumerate(
            (
                (frames.at[0], ext.at[pl.ds(1, FINE)]),
                (w_time, wt),
                (w_down, wd),
                (grad_out.at[0, 0], go),
                (w_query, wq),
                (w_key, wk),
                (grad_skip.at[0], gs),
            )
        )
    ]
    loads[0].start()
    loads[1].start()

    peers_tm = [at(tm_=(tm + k) % TM) for k in range(1, TM)]
    partner = at(space_=y * 2 + 1 - core)
    peers_y = [at(space_=((y + k) % YS) * 2 + core) for k in range(1, YS)]
    peers_x = [at(tm_=zlo * XS + (x + k) % XS) for k in range(1, XS)]
    zpos = dp * 2 + zlo
    on_z = [(zpos + k) % 8 for k in range(1, 8)]
    peers_z = [at(tm_=z % 2 * XS + x, dp_=z // 2) for z in on_z]
    barrier = pltpu.get_barrier_semaphore()
    other_z = [at(tm_=tm_, dp_=(dp + k) % DP) for k in range(1, DP) for tm_ in (x, XS + x)]
    greeted = peers_tm + [partner] + peers_y + other_z
    for peer in greeted:
        pl.semaphore_signal(barrier, inc=1, device_id=peer, device_id_type=MESH)
    pl.semaphore_wait(barrier, len(greeted))

    def remote(src, dst, sem, device, landed=None):
        return pltpu.make_async_remote_copy(
            src_ref=src,
            dst_ref=dst,
            send_sem=send_sem.at[sem],
            recv_sem=recv_sem.at[sem if landed is None else landed],
            device_id=device,
            device_id_type=MESH,
        )

    def exchange(send, recv, c, first):
        copies = [
            remote(send.at[c, (tm + k) % TM], recv.at[c, tm], first + k, at(tm_=(tm + k) % TM)) for k in range(1, TM)
        ]
        own = pltpu.make_async_copy(send.at[c, tm], recv.at[c, tm], local_sem.at[7 + first // TM])
        for copy in copies:
            copy.start()
        own.start()

        def receive():
            for k in range(1, TM):
                src = (tm + TM - k) % TM
                remote(send.at[c, src], recv.at[c, src], first + k, at(tm_=src)).wait_recv()
            own.wait()

        sent.extend(copies)
        return receive

    sent = []

    def send(copy):
        copy.start()
        sent.append(copy)
        return copy

    def pack(src, dst, c, fold, width):
        rows = src[c * WIDE : (c + 1) * WIDE, :width].astype(F32)
        for f in range(TM):
            dst[c, f] = fold(rows[8 * f : 8 * f + 8]).astype(BF16)

    def unpack(src, dst, c, unfold):
        rows = [unfold(src[c, f].astype(F32)) for f in range(TM)]
        dst[c * WIDE : (c + 1) * WIDE, :] = jnp.concatenate(rows, axis=0).astype(dst.dtype)

    prev, nxt = at(tm_=(tm + TM - 1) % TM), at(tm_=(tm + 1) % TM)
    halos = []
    for c in range(CHUNKS):
        rows = pl.ds(c * WIDE, WIDE)
        first = send(remote(frames.at[0, 0, rows], ext.at[FINE + 1, rows], 72 + 2 * c, prev))
        last = send(remote(frames.at[0, FINE - 1, rows], ext.at[0, rows], 73 + 2 * c, nxt))
        halos.append((first, last))
    for load in loads[2:]:
        load.start()

    loads[0].wait()
    loads[1].wait()
    for lo, hi in COLS_FINE:
        n = hi - lo
        pre[:, :, lo:hi] = dot(ext[1:5].reshape(FINE * PIX, C1), wt[C1 : 2 * C1, lo:hi]).reshape(FINE, PIX, n)
        pre[1:4, :, lo:hi] += dot(ext[1:4].reshape(3 * PIX, C1), wt[:C1, lo:hi]).reshape(3, PIX, n)
        pre[0:3, :, lo:hi] += dot(ext[2:5].reshape(3 * PIX, C1), wt[2 * C1 :, lo:hi]).reshape(3, PIX, n)
    loads[3].wait()
    for c in range(CHUNKS):
        pack(go, g_send, c, fold_tail, C2)

    c_receive, g_receive = [], []
    for c in range(CHUNKS):
        rows = slice(c * WIDE, (c + 1) * WIDE)
        for copy in halos[c]:
            copy.wait_recv()

        @pl.when(tm == 0)
        def _():
            ext[0, rows] = jnp.zeros((WIDE, C1), BF16)

        @pl.when(tm == TM - 1)
        def _():
            ext[FINE + 1, rows] = jnp.zeros((WIDE, C1), BF16)

        for lo, hi in COLS_FINE:
            pre[0, rows, lo:hi] += dot(ext[0, rows], wt[:C1, lo:hi])
            pre[3, rows, lo:hi] += dot(ext[5, rows], wt[2 * C1 :, lo:hi])
            total = None
            for t in range(FINE):
                act = pre[t, rows, lo:hi]
                logistic = 1.0 / (1.0 + jnp.exp(-act))
                skip = (ext[t + 1, rows, lo:hi].astype(F32) + act * logistic).astype(BF16).astype(F32)
                total = skip if total is None else total + skip
                pre[t, rows, lo:hi] = logistic * (1.0 + act * (1.0 - logistic))
            skipsum[rows, lo:hi] = total.astype(BF16)
        pack(skipsum, c_send, c, fold_fine, C1)
        c_receive.append(exchange(c_send, c_recv, c, 8 * c))
    for c in range(CHUNKS):
        g_receive.append(exchange(g_send, g_recv, c, 24 + 8 * c))

    loads[2].wait()
    loads[4].wait()
    loads[5].wait()
    for c in range(CHUNKS):
        c_receive[c]()
        unpack(c_recv, sk, c, open_fine)
    for lo, hi in COLS_COARSE:
        cb[:, lo:hi] = (0.25 * dot(sk[...], wd[:, lo:hi])).astype(BF16)
    for lo, hi in COLS_COARSE:
        qf[:, lo:hi] = dot(cb[...], wq[:, lo:hi])
        kf[:, lo:hi] = dot(cb[...], wk[:, lo:hi])
    def tiles_of(i):
        return [pl.ds(pl.multiple_of((i * TILES + u) * 128, 128), 128) for u in range(TILES)]

    def some_scores(i, carry):
        attend_scores(tiles_of(i), qf, kf, probs, bq, bk)
        return carry

    def some_back(i, carry):
        attend_back(tiles_of(i), qf, kf, probs, cb, gb, work, bq, bk)
        return carry

    lax.fori_loop(0, C2 // 128 // TILES, some_scores, 0)
    for c in range(CHUNKS):
        g_receive[c]()
        unpack(g_recv, gb, c, open_tail)
    lax.fori_loop(0, C2 // 128 // TILES, some_back, 0)
    for lo, hi in COLS_COARSE:
        projected = dot_last(bq[...], wq[lo:hi, :]) + dot_last(bk[...], wk[lo:hi, :])
        bc[:, lo:hi] = (work[:, lo:hi] + projected).astype(BF16)
    for lo, hi in COLS_FINE:
        work[:, lo:hi] = 0.25 * dot_last(bc[...], wd[lo:hi, :])
    b_receive = []
    for c in range(CHUNKS):
        pack(work, b_send, c, fold_fine, C1)
        b_receive.append(exchange(b_send, b_recv, c, 48 + 8 * c))

    def time_unit(part_y, part_core, part_dp, lo, hi):
        start = pl.multiple_of(480 * part_y + 240 * part_core + 60 * part_dp // 8 * 8, 8)
        return t_sum[pl.ds(start, 64), lo:hi]

    def down_unit(part_y, part_core, part_dp):
        start = pl.multiple_of(160 * part_y + 80 * part_core + 20 * part_dp // 8 * 8, 8)
        rows = d_sum[pl.ds(start, 24), :]
        return jnp.concatenate([rows[:16], fold_tail(rows[16:]), jnp.zeros((16, 128), F32)], axis=1)

    for lo, hi in COLS_FINE:
        d_sum[lo:hi, :] = dot_first(sk[:, lo:hi], bc[...])

    def pack_down(part_y, carry):
        for h in range(DP):
            unit = down_unit(part_y, 1 - core, h).astype(BF16)
            for part_x in range(XS):
                cs_x[part_x, part_y, h] = unit[:, DC * part_x : DC * part_x + DC]
        return carry

    def add_down(part_y, carry):
        for h in range(DP):
            unit = down_unit(part_y, core, h)
            for part_x in range(XS):
                more = unit[:, DC * part_x : DC * part_x + DC]
                p_x[part_x, part_y, h] = (p_x[part_x, part_y, h].astype(F32) + more).astype(BF16)
        return carry

    lax.fori_loop(0, YS, pack_down, 0)
    swap_x = send(remote(cs_x, p_x, 106, partner))
    swap_x.wait_recv()
    lax.fori_loop(0, YS, add_down, 0)
    ring_x = Ring(remote, p_x, (x_ra, x_rb, x_fp, x_fm), x, peers_x[0], peers_x[2], 92)
    ring_x.start()

    loads[6].wait()
    for c in range(CHUNKS):
        b_receive[c]()
        unpack(b_recv, spread, c, open_fine)
    for lo, hi in COLS_FINE:
        for t in range(FINE):
            back = gs[t, :, lo:hi].astype(F32) + spread[:, lo:hi]
            bpe[t + 1, :, lo:hi] = (back * pre[t, :, lo:hi]).astype(BF16)

    ring_0 = Ring(remote, p_0, (ra_0, rb_0, fp_0, fm_0), y, peers_y[0], peers_y[2], 80)
    ring_1 = Ring(remote, p_1, (ra_1, rb_1, fp_1, fm_1), x, peers_x[0], peers_x[2], 86)

    def time_grad(piece, cs, parts, place):
        left, right = PIECES[piece]
        back_rows = bpe[1 : FINE + 1, :, left:right].reshape(FINE * PIX, right - left)
        part_y = 0
        for k in range(3):
            for lo, hi in COLS_FINE:
                block = ext[k : k + FINE, :, lo:hi].reshape(FINE * PIX, hi - lo)
                t_sum[k * C1 + lo : k * C1 + hi, left:right] = dot_first(block, back_rows)
                if part_y < YS and k * C1 + hi >= 480 * (part_y + 1):
                    for h in range(DP):
                        unit = time_unit(part_y, 1 - core, h, left, right).astype(BF16)
                        cs[(*place(part_y), h)] = unit if piece == 0 else unit.reshape(XS, 16, right - left)
                    at_y = place(part_y)
                    send(remote(cs.at[at_y], parts.at[at_y], 98 + 4 * piece + part_y, partner))
                    part_y += 1

    time_grad(0, cs_0, p_0, lambda part_y: (part_y,))
    ring_x.middle()
    for part_y, copies in (
        (ring_0.far, ring_0.copies[:2]),
        (ring_0.ahead, ring_0.copies[2:3]),
        (ring_0.behind, ring_0.copies[3:4]),
        (y, []),
    ):
        remote(cs_0.at[part_y], p_0.at[part_y], 98 + part_y, partner).wait_recv()
        for h in range(DP):
            p_0[part_y, h] = (p_0[part_y, h].astype(F32) + time_unit(part_y, core, h, *PIECES[0])).astype(BF16)
        for copy in copies:
            copy.start()

    time_grad(1, cs_1, p_1, lambda part_y: (slice(None), part_y))
    for part_y in range(YS):
        remote(cs_1.at[:, part_y], p_1.at[:, part_y], 102 + part_y, partner).wait_recv()
        for h in range(DP):
            unit = time_unit(part_y, core, h, *PIECES[1]).reshape(XS, 16, -1)
            p_1[:, part_y, h] = (p_1[:, part_y, h].astype(F32) + unit).astype(BF16)
    ring_1.start()

    def input_grad(t, count, lo, hi):
        rows = [bpe[t + k : t + k + count].reshape(count * PIX, C1) for k in range(3)]
        acc = dot_last(rows[2], wt[lo:hi, :])
        acc += dot_last(rows[1], wt[C1 + lo : C1 + hi, :])
        acc += dot_last(rows[0], wt[2 * C1 + lo : 2 * C1 + hi, :])
        acc = acc.reshape(count, PIX, hi - lo) + gs[t : t + count, :, lo:hi].astype(F32) + spread[:, lo:hi]
        gs[t : t + count, :, lo:hi] = acc.astype(BF16)

    input_grad(1, 2, *COLS_FINE[0])
    ring_0.middle()
    input_grad(1, 2, *COLS_FINE[1])
    ring_1.middle()
    back_first = send(remote(bpe.at[1], bpe.at[FINE + 1], 78, prev))
    back_last = send(remote(bpe.at[FINE], bpe.at[0], 79, nxt))
    input_grad(1, 2, *COLS_FINE[2])

    def added(copies, own, more):
        for copy in copies:
            copy.wait_recv()
        return (own.astype(F32) + sum(more[k].astype(F32) for k in range(len(copies)))).astype(BF16)

    ring_x.arrived()
    for part_y in range(YS):
        p2_x[part_y] = ring_x.total(part_y).astype(BF16)
    copies_x = [send(remote(p2_x.at[(y + k) % YS], r2_x.at[k - 1], 113 + k, peers_y[k - 1])) for k in range(1, YS)]
    ring_0.arrived()
    for h in range(DP):
        p2_0[:, h] = ring_0.total(h).astype(BF16).reshape(XS, 16, -1)
    copies_0 = [send(remote(p2_0.at[(x + k) % XS], r2_0.at[k - 1], 107 + k, peers_x[k - 1])) for k in range(1, XS)]
    ring_1.arrived()
    for part_y in range(YS):
        p2_1[part_y] = ring_1.total(part_y).astype(BF16)
    copies_1 = [send(remote(p2_1.at[(y + k) % YS], r2_1.at[k - 1], 110 + k, peers_y[k - 1])) for k in range(1, YS)]
    last_waits = []

    class OverZ:
        def __init__(self, src, slots, first, owner):
            self.src, self.slots, self.first, self.owner = src, slots, first, owner
            other = zlo if owner == 0 else 1 - zlo
            copies = []
            for k in range(DP):
                h = (dp + k) % DP
                slot = other * DP + k
                target = at(tm_=owner * XS + x, dp_=h)
                copies.append(remote(src.at[h], slots.at[slot], first + k, target, landed=first + slot))
            for copy in copies[1:]:
                copy.start()

            @pl.when(zlo != owner)
            def _():
                copies[0].start()

            def finish():
                for copy in copies[1:]:
                    copy.wait_send()

                @pl.when(zlo != owner)
                def _():
                    copies[0].wait_send()

            last_waits.append(finish)

        def gather(self, final, first):
            copies = [
                remote(final.at[x], final.at[x], first + k, peers_tm[k - 1], landed=first + TM + x)
                for k in range(1, TM)
            ]

            @pl.when(zlo == self.owner)
            def _():
                total = self.src[dp].astype(F32)
                for slot in range(1, 2 * DP):
                    ref = self.slots.at[slot]
                    remote(ref, ref, self.first + slot, partner).wait_recv()
                    total += self.slots[slot].astype(F32)
                final[x] = total.astype(BF16)
                for copy in copies:
                    copy.start()

            def finish():
                for k in range(1, XS):
                    ref = final.at[(x + k) % XS]
                    remote(ref, ref, first, partner, landed=first + TM + (x + k) % XS).wait_recv()

                @pl.when(zlo != self.owner)
                def _():
                    remote(final.at[x], final.at[x], first, partner, landed=first + TM + x).wait_recv()

                @pl.when(zlo == self.owner)
                def _():
                    for copy in copies:
                        copy.wait_send()

            last_waits.append(finish)

    sums = added(copies_x, p2_x[y], r2_x)
    for half in range(2):
        zs_x[half] = sums[:, :, half * DC // 2 : (half + 1) * DC // 2]
    z_copies = [
        send(remote(zs_x.at[z % 2, z // 2], zr_x.at[k], 133 + k, peers_z[k])) for k, z in enumerate(on_z)
    ]
    zs_0[...] = added(copies_0, p2_0[x], r2_0)
    over_z0 = OverZ(zs_0, zr_0, 117, 0)
    zs_1[...] = added(copies_1, p2_1[y], r2_1)
    over_z1 = OverZ(zs_1, zr_1, 125, 1)

    back_first.wait_recv()
    back_last.wait_recv()

    @pl.when(tm == 0)
    def _():
        bpe[0] = jnp.zeros((PIX, C1), BF16)

    @pl.when(tm == TM - 1)
    def _():
        bpe[FINE + 1] = jnp.zeros((PIX, C1), BF16)

    for lo, hi in COLS_FINE:
        input_grad(0, 1, lo, hi)
        input_grad(3, 1, lo, hi)
    store = pltpu.make_async_copy(gs, ig_out.at[0], local_sem.at[16])
    store.start()

    f_x[tm] = added(z_copies, zs_x[zlo, dp], zr_x)
    for k in range(1, TM):
        send(remote(f_x.at[tm], f_x.at[tm], 163 + k, peers_tm[k - 1]))
    over_z0.gather(f_0, 140)
    over_z1.gather(f_1, 152)
    for k in range(1, TM):
        src = (tm + TM - k) % TM
        remote(f_x.at[src], f_x.at[src], 163 + k, at(tm_=src)).wait_recv()
    for wait in last_waits:
        wait()
    time0_out[...], time1_out[...], down_out[...] = f_0[...], f_1[...], f_x[...]

    for copy in sent:
        copy.wait_send()
    for ring in (ring_0, ring_1, ring_x):
        ring.finish()
    store.wait()


def finish(ig, time0, time1, down, ig_out, time_out, down_out, held, load_sem, store_sem):
    loads = [pltpu.make_async_copy(ig.at[0, t], held.at[t], load_sem.at[t]) for t in range(FINE)]
    stores = [pltpu.make_async_copy(held.at[t], ig_out.at[0, t], store_sem.at[t]) for t in range(FINE)]
    for load in loads:
        load.start()
    odd = lax.axis_index("dp") % 2 == 1
    scale = 1.0 / math.sqrt(ROWS_ALL)
    rows = jnp.concatenate([time0[...], time1[...]], axis=2).astype(F32).reshape(64, C1) * scale
    time_out[...] = jnp.where(odd, rows[4:64], rows[:60])
    halves = [down[half * XS + part_x] for part_x in range(XS) for half in range(2)]
    wide = jnp.concatenate(halves, axis=1).astype(F32) * (0.25 * scale)
    rows = jnp.concatenate([wide[:, :C2], open_tail(wide[:, C2 : C2 + C1])], axis=0)
    down_out[...] = jnp.where(odd, rows[4:24], rows[:20])
    for load, store in zip(loads, stores):
        load.wait()
        store.start()
    for store in stores:
        store.wait()


def first_over_y(n):
    v = pltpu.VMEM
    return [
        v((YS, DP, 64, n), BF16), v((YS, DP, 64, n), BF16),
        v((2, 64, n), BF16), v((2, 64, n), BF16), v((4, 64, n), BF16), v((4, 64, n), BF16),
        v((XS, DP, 16, n), BF16), v((XS - 1, DP, 16, n), BF16),
        v((DP, 16, n), BF16), v((2 * DP, 16, n), BF16), v((XS, 16, n), BF16),
    ]


def first_over_x(n):
    v = pltpu.VMEM
    return [
        v((XS, YS, DP, 16, n), BF16), v((XS, YS, DP, 16, n), BF16),
        v((2, DP, 16, n), BF16), v((2, DP, 16, n), BF16), v((4, DP, 16, n), BF16), v((4, DP, 16, n), BF16),
        v((YS, DP, 16, n), BF16), v((YS - 1, DP, 16, n), BF16),
        v((DP, 16, n), BF16), v((2 * DP, 16, n), BF16), v((XS, 16, n), BF16),
    ]


def shards(*args):
    v, hbm = pltpu.VMEM, pl.BlockSpec(memory_space=pl.ANY)
    vmem = pl.BlockSpec(memory_space=pltpu.VMEM)
    scratch = [
        v((FINE + 2, PIX, C1), BF16), v((3 * C1, C1), BF16), v((C1, C2), BF16), v((C2, C2), BF16), v((C2, C2), BF16),
        v((FINE, PIX, C1), BF16), v((PIX, C2), BF16), v((FINE, PIX, C1), F32), v((PIX, C1), BF16),
        v((PIX, C2), F32), v((PIX, C2), F32), v((PIX, C2), F32),
        v((PIX, C2), BF16), v((PIX, C2), BF16), v((PIX, C2), BF16), v((PIX, C2), BF16), v((PIX, C2), F32),
        *[v((CHUNKS, TM, 16, C1), BF16)] * 2, *[v((CHUNKS, TM, 16, FOLD), BF16)] * 4,
        v((PIX, C1), BF16), v((PIX, C2), BF16), v((PIX, C1), F32), v((FINE + 2, PIX, C1), BF16),
        v((3 * C1, C1), F32), v((C1, C2), F32),
        *first_over_y(PIECES[0][1] - PIECES[0][0]), *first_over_x(PIECES[1][1] - PIECES[1][0]),
        v((XS, YS, DP, 16, DC), BF16), v((XS, YS, DP, 16, DC), BF16),
        *[v((2, DP, 16, DC), BF16)] * 2, *[v((4, DP, 16, DC), BF16)] * 2,
        v((YS, DP, 16, DC), BF16), v((YS - 1, DP, 16, DC), BF16),
        v((2, DP, 16, DC // 2), BF16), v((7, 16, DC // 2), BF16), v((TM, 16, DC // 2), BF16),
        pltpu.SemaphoreType.DMA((17,)), pltpu.SemaphoreType.DMA((171,)), pltpu.SemaphoreType.DMA((171,)),
    ]
    fine = jax.ShapeDtypeStruct((1, FINE, PIX, C1), BF16)
    ig, *sums = pl.pallas_call(
        kernel,
        out_shape=(
            fine,
            *[jax.ShapeDtypeStruct((XS, 16, hi - lo), BF16) for lo, hi in PIECES],
            jax.ShapeDtypeStruct((TM, 16, DC // 2), BF16),
        ),
        in_specs=[hbm] * 7,
        out_specs=(hbm, vmem, vmem, vmem),
        scratch_shapes=scratch,
        compiler_params=pltpu.CompilerParams(
            collective_id=0, has_side_effects=True, vmem_limit_bytes=60 * 1024 * 1024
        ),
        cost_estimate=pl.CostEstimate(flops=9 * 10**9, bytes_accessed=16 * 10**6, transcendentals=10**6),
    )(*args)
    return pl.pallas_call(
        finish,
        out_shape=(fine, jax.ShapeDtypeStruct((60, C1), F32), jax.ShapeDtypeStruct((20, C2), F32)),
        in_specs=[hbm, vmem, vmem, vmem],
        out_specs=(hbm, vmem, vmem),
        scratch_shapes=[
            v((FINE, PIX, C1), BF16),
            pltpu.SemaphoreType.DMA((FINE,)),
            pltpu.SemaphoreType.DMA((FINE,)),
        ],
        cost_estimate=pl.CostEstimate(flops=10**5, bytes_accessed=2 * 10**6, transcendentals=0),
    )(ig, *sums)


def solution(mesh):
    fine, whole = P("dp", "tm", "space", None), P()
    rows = P(("space", "dp"), None)
    return jax.shard_map(
        shards,
        mesh=mesh,
        in_specs=(fine, whole, whole, whole, whole, fine, fine),
        out_specs=(fine, rows, rows),
        check_vma=False,
    )
```

```python
import math

import jax
import jax.numpy as jnp
from jax import lax
from jax.experimental import pallas as pl
from jax.experimental.pallas import tpu as pltpu
from jax.sharding import PartitionSpec as P

C1, C2, DH = 640, 1280, 64
TM, YS, XS, DP = 8, 4, 4, 4
FINE, PIX = 4, 192
ROWS_ALL = 4 * 32 * 1536
EPS = 1e-06
MESH = pl.DeviceIdType.MESH
F32, BF16 = jnp.float32, jnp.bfloat16
COLS_FINE = ((0, 256), (256, 512), (512, 640))
COLS_COARSE = tuple((n, n + 256) for n in range(0, C2, 256))
CHUNKS, WIDE = 3, 64
FOLD = 384
DC = 512
TILES = 5
PIECES = ((0, 256), (256, 512), (512, 640))


def dot(left, right):
    return jnp.dot(left, right, preferred_element_type=F32)


def dot_last(left, right):
    return lax.dot_general(left, right, (((1,), (1,)), ((), ())), preferred_element_type=F32)


def dot_first(left, right):
    return lax.dot_general(left, right, (((0,), (0,)), ((), ())), preferred_element_type=F32)


def fold_tail(tail):
    return jnp.concatenate([tail[:, :C1], tail[:, C1:]], axis=0)


def fold_fine(rows):
    rest = jnp.concatenate([rows[:, FOLD:], jnp.zeros((8, 2 * FOLD - C1), F32)], axis=1)
    return jnp.concatenate([rows[:, :FOLD], rest], axis=0)


def open_fine(rows):
    return jnp.concatenate([rows[:8], rows[8:, : C1 - FOLD]], axis=1)


def open_tail(tail):
    return jnp.concatenate([tail[:8], tail[8:]], axis=1)


class Ring:
    def __init__(self, remote, parts, bufs, pos, plus, minus, first):
        self.parts, self.pos = parts, pos
        self.ra, self.rb, self.fp, self.fm = bufs
        lo, hi = pl.ds(0, 2), pl.ds(2, 2)
        self.ahead, self.behind, self.far = (pos + 1) % 4, (pos + 3) % 4, (pos + 2) % 4
        self.copies = [
            remote(parts.at[self.far, lo], self.ra, first, plus),
            remote(parts.at[self.far, hi], self.rb, first + 1, minus),
            remote(parts.at[self.ahead, hi], self.fp.at[hi], first + 2, plus),
            remote(parts.at[self.behind, lo], self.fm.at[lo], first + 3, minus),
            remote(parts.at[self.ahead, lo], self.fp.at[lo], first + 4, plus),
            remote(parts.at[self.behind, hi], self.fm.at[hi], first + 5, minus),
        ]

    def start(self):
        for copy in self.copies[:4]:
            copy.start()

    def middle(self):
        parts = self.parts
        self.copies[0].wait_recv()
        parts[self.ahead, 0:2] = (parts[self.ahead, 0:2].astype(F32) + self.ra[...].astype(F32)).astype(BF16)
        self.copies[4].start()
        self.copies[1].wait_recv()
        parts[self.behind, 2:4] = (parts[self.behind, 2:4].astype(F32) + self.rb[...].astype(F32)).astype(BF16)
        self.copies[5].start()

    def arrived(self):
        for copy in self.copies[2:]:
            copy.wait_recv()

    def total(self, i):
        return self.parts[self.pos, i].astype(F32) + self.fp[i].astype(F32) + self.fm[i].astype(F32)

    def finish(self):
        for copy in self.copies:
            copy.wait_send()


def attend_units(tiles):
    return [(i, slice(WIDE * g, WIDE * g + WIDE)) for i in range(len(tiles)) for g in range(CHUNKS)]


def pair_ones():
    rows, cols = (lax.broadcasted_iota(jnp.int32, (128, 128), d) for d in (0, 1))
    return ((rows // DH) == (cols // DH)).astype(F32).astype(BF16)


def pair_left():
    return (lax.broadcasted_iota(jnp.int32, (WIDE, 128), 1) < DH).astype(F32)


def pair_rows(rows):
    left = pair_left()
    return jnp.concatenate([rows * left.astype(BF16), rows * (1.0 - left).astype(BF16)], axis=0)


def head_sums(terms):
    sums = dot(jnp.concatenate([term.astype(BF16) for term in terms], axis=0), pair_ones())
    rows = terms[0].shape[0]
    return [sums[rows * i : rows * i + rows] for i in range(len(terms))]


def attend_scores(tiles, qf, kf, probs_ref, bq, bk):
    row_i, col_i = (lax.broadcasted_iota(jnp.int32, (WIDE, 128), d) for d in (0, 1))
    mask = ((row_i % 8) == (col_i % 8)).astype(F32)
    count, units = len(tiles), attend_units(tiles)
    q, k = [qf[:, c] for c in tiles], [kf[:, c] for c in tiles]
    factors = [lax.rsqrt(total * (1.0 / DH) + EPS) for total in head_sums([v * v for v in q + k])]
    qb = [(q[i] * factors[i]).astype(BF16) for i in range(count)]
    kb = [(k[i] * factors[count + i]).astype(BF16) for i in range(count)]
    for i, c in enumerate(tiles):
        qf[:, c], kf[:, c] = factors[i], factors[count + i]
        bq[:, c], bk[:, c] = qb[i], kb[i]
    raised = [jnp.exp(dot_last(qb[i][rows], pair_rows(kb[i][rows])) * 0.125) * mask for i, rows in units]
    for (i, rows), over, under in zip(units, raised, head_sums(raised)):
        probs_ref[rows, tiles[i]] = over / under


def attend_back(tiles, qf, kf, probs_ref, cb, gb, work, bq, bk):
    units = attend_units(tiles)
    index, left = range(len(units)), pair_left()

    def fold(both):
        return jnp.where(left > 0.5, both[:WIDE], both[WIDE:])

    queries = [bq[rows, tiles[i]] for i, rows in units]
    plain_keys = [bk[rows, tiles[i]] for i, rows in units]
    keys = [pair_rows(rows) for rows in plain_keys]
    upstream = [gb[rows, tiles[i]] for i, rows in units]
    probs = [probs_ref[rows, tiles[i]] for i, rows in units]
    back_probs = [dot_last(upstream[n], pair_rows(cb[rows, tiles[i]])) for n, (i, rows) in enumerate(units)]
    means = head_sums([p * b for p, b in zip(probs, back_probs)])
    scores = [(p * (b - m)).astype(BF16) for p, b, m in zip(probs, back_probs, means)]
    for n, (i, rows) in enumerate(units):
        values = fold(dot_first(probs[n].astype(BF16), upstream[n]))
        work[rows, tiles[i]] = upstream[n].astype(F32) + values
    back_q = [dot(scores[n], keys[n]) * 0.125 for n in index]
    back_k = [fold(dot_first(scores[n], queries[n])) * 0.125 for n in index]
    qn, kn = [rows.astype(F32) for rows in queries], [rows.astype(F32) for rows in plain_keys]
    mean_q = head_sums([b * v for b, v in zip(back_q, qn)])
    mean_k = head_sums([b * v for b, v in zip(back_k, kn)])
    for n, (i, rows) in enumerate(units):
        c = tiles[i]
        bq[rows, c] = (qf[rows, c] * (back_q[n] - qn[n] * (mean_q[n] * (1.0 / DH)))).astype(BF16)
        bk[rows, c] = (kf[rows, c] * (back_k[n] - kn[n] * (mean_k[n] * (1.0 / DH)))).astype(BF16)


def kernel(
    frames, w_time, w_down, w_query, w_key, grad_skip, grad_out,
    ig_out, time0_out, time1_out, time2_out, down_out,
    ext, wt, wd, wq, wk, gs, go, pre, skipsum, work, qf, kf, cb, gb, bq, bk, probs,
    g_send, g_recv, c_send, c_recv, b_send, b_recv, sk, bc, spread, bpe, t_sum, d_sum,
    cs_0, p_0, r_0, p2_0, r2_0, zs_0, zr_0, f_0,
    cs_1, p_1, r_1, p2_1, r2_1, zs_1, zr_1, f_1,
    cs_2, p_2, zr_2, p2_2, r2_2, xs_2, f_2,
    cs_x, p_x, x_ra, x_rb, x_fp, x_fm, p2_x, r2_x, zs_x, zr_x, f_x,
    local_sem, send_sem, recv_sem,
):
    tm, space, dp = lax.axis_index("tm"), lax.axis_index("space"), lax.axis_index("dp")
    core, y, zlo, x = space % 2, space // 2, tm // XS, tm % XS

    def at(tm_=None, space_=None, dp_=None):
        return {
            "tm": tm if tm_ is None else tm_,
            "space": space if space_ is None else space_,
            "dp": dp if dp_ is None else dp_,
        }

    loads = [
        pltpu.make_async_copy(src, dst, local_sem.at[i])
        for i, (src, dst) in enumerate(
            (
                (frames.at[0], ext.at[pl.ds(1, FINE)]),
                (w_time, wt),
                (w_down, wd),
                (grad_out.at[0, 0], go),
                (w_query, wq),
                (w_key, wk),
                (grad_skip.at[0], gs),
            )
        )
    ]
    loads[0].start()
    loads[1].start()

    peers_tm = [at(tm_=(tm + k) % TM) for k in range(1, TM)]
    partner = at(space_=y * 2 + 1 - core)
    peers_y = [at(space_=((y + k) % YS) * 2 + core) for k in range(1, YS)]
    peers_x = [at(tm_=zlo * XS + (x + k) % XS) for k in range(1, XS)]
    zpos = dp * 2 + zlo
    on_z = [(zpos + k) % 8 for k in range(1, 8)]
    peers_z = [at(tm_=z % 2 * XS + x, dp_=z // 2) for z in on_z]
    barrier = pltpu.get_barrier_semaphore()
    other_z = [at(tm_=tm_, dp_=(dp + k) % DP) for k in range(1, DP) for tm_ in (x, XS + x)]
    greeted = peers_tm + [partner] + peers_y + other_z
    for peer in greeted:
        pl.semaphore_signal(barrier, inc=1, device_id=peer, device_id_type=MESH)
    pl.semaphore_wait(barrier, len(greeted))

    def remote(src, dst, sem, device, landed=None):
        return pltpu.make_async_remote_copy(
            src_ref=src,
            dst_ref=dst,
            send_sem=send_sem.at[sem],
            recv_sem=recv_sem.at[sem if landed is None else landed],
            device_id=device,
            device_id_type=MESH,
        )

    def exchange(send, recv, c, first):
        copies = [
            remote(send.at[c, (tm + k) % TM], recv.at[c, tm], first + k, at(tm_=(tm + k) % TM)) for k in range(1, TM)
        ]
        own = pltpu.make_async_copy(send.at[c, tm], recv.at[c, tm], local_sem.at[7 + first // TM])
        for copy in copies:
            copy.start()
        own.start()

        def receive():
            for k in range(1, TM):
                src = (tm + TM - k) % TM
                remote(send.at[c, src], recv.at[c, src], first + k, at(tm_=src)).wait_recv()
            own.wait()

        sent.extend(copies)
        return receive

    sent = []

    def send(copy):
        copy.start()
        sent.append(copy)
        return copy

    def pack(src, dst, c, fold, width):
        rows = src[c * WIDE : (c + 1) * WIDE, :width].astype(F32)
        for f in range(TM):
            dst[c, f] = fold(rows[8 * f : 8 * f + 8]).astype(BF16)

    def unpack(src, dst, c, unfold):
        rows = [unfold(src[c, f].astype(F32)) for f in range(TM)]
        dst[c * WIDE : (c + 1) * WIDE, :] = jnp.concatenate(rows, axis=0).astype(dst.dtype)

    prev, nxt = at(tm_=(tm + TM - 1) % TM), at(tm_=(tm + 1) % TM)
    halos = []
    for c in range(CHUNKS):
        rows = pl.ds(c * WIDE, WIDE)
        first = send(remote(frames.at[0, 0, rows], ext.at[FINE + 1, rows], 72 + 2 * c, prev))
        last = send(remote(frames.at[0, FINE - 1, rows], ext.at[0, rows], 73 + 2 * c, nxt))
        halos.append((first, last))
    for load in loads[2:]:
        load.start()

    loads[0].wait()
    loads[1].wait()
    for lo, hi in COLS_FINE:
        n = hi - lo
        pre[:, :, lo:hi] = dot(ext[1:5].reshape(FINE * PIX, C1), wt[C1 : 2 * C1, lo:hi]).reshape(FINE, PIX, n)
        pre[1:4, :, lo:hi] += dot(ext[1:4].reshape(3 * PIX, C1), wt[:C1, lo:hi]).reshape(3, PIX, n)
        pre[0:3, :, lo:hi] += dot(ext[2:5].reshape(3 * PIX, C1), wt[2 * C1 :, lo:hi]).reshape(3, PIX, n)
    loads[3].wait()
    for c in range(CHUNKS):
        pack(go, g_send, c, fold_tail, C2)

    c_receive, g_receive = [], [exchange(g_send, g_recv, 0, 24)]
    for c in range(CHUNKS):
        rows = slice(c * WIDE, (c + 1) * WIDE)
        for copy in halos[c]:
            copy.wait_recv()

        @pl.when(tm == 0)
        def _():
            ext[0, rows] = jnp.zeros((WIDE, C1), BF16)

        @pl.when(tm == TM - 1)
        def _():
            ext[FINE + 1, rows] = jnp.zeros((WIDE, C1), BF16)

        for lo, hi in COLS_FINE:
            pre[0, rows, lo:hi] += dot(ext[0, rows], wt[:C1, lo:hi])
            pre[3, rows, lo:hi] += dot(ext[5, rows], wt[2 * C1 :, lo:hi])
            total = None
            for t in range(FINE):
                act = pre[t, rows, lo:hi]
                logistic = 1.0 / (1.0 + jnp.exp(-act))
                skip = (ext[t + 1, rows, lo:hi].astype(F32) + act * logistic).astype(BF16).astype(F32)
                total = skip if total is None else total + skip
                pre[t, rows, lo:hi] = logistic * (1.0 + act * (1.0 - logistic))
            skipsum[rows, lo:hi] = total.astype(BF16)
        pack(skipsum, c_send, c, fold_fine, C1)
        c_receive.append(exchange(c_send, c_recv, c, 8 * c))
    for c in range(1, CHUNKS):
        g_receive.append(exchange(g_send, g_recv, c, 24 + 8 * c))

    loads[2].wait()
    loads[4].wait()
    loads[5].wait()
    for c in range(CHUNKS):
        c_receive[c]()
        unpack(c_recv, sk, c, open_fine)
    for lo, hi in COLS_COARSE:
        cb[:, lo:hi] = (0.25 * dot(sk[...], wd[:, lo:hi])).astype(BF16)
    for lo, hi in COLS_COARSE:
        qf[:, lo:hi] = dot(cb[...], wq[:, lo:hi])
        kf[:, lo:hi] = dot(cb[...], wk[:, lo:hi])
    def tiles_of(i):
        return [pl.ds(pl.multiple_of((i * TILES + u) * 128, 128), 128) for u in range(TILES)]

    def some_scores(i, carry):
        attend_scores(tiles_of(i), qf, kf, probs, bq, bk)
        return carry

    def some_back(i, carry):
        attend_back(tiles_of(i), qf, kf, probs, cb, gb, work, bq, bk)
        return carry

    lax.fori_loop(0, C2 // 128 // TILES, some_scores, 0)
    for c in range(CHUNKS):
        g_receive[c]()
        unpack(g_recv, gb, c, open_tail)
    lax.fori_loop(0, C2 // 128 // TILES, some_back, 0)
    for lo, hi in COLS_COARSE:
        projected = dot_last(bq[...], wq[lo:hi, :]) + dot_last(bk[...], wk[lo:hi, :])
        bc[:, lo:hi] = (work[:, lo:hi] + projected).astype(BF16)
    for lo, hi in COLS_FINE:
        work[:, lo:hi] = 0.25 * dot_last(bc[...], wd[lo:hi, :])
    b_receive = []
    for c in range(CHUNKS):
        pack(work, b_send, c, fold_fine, C1)
        b_receive.append(exchange(b_send, b_recv, c, 48 + 8 * c))

    def time_unit(part_y, part_core, part_dp, lo, hi):
        start = pl.multiple_of(480 * part_y + 240 * part_core + 60 * part_dp // 8 * 8, 8)
        return t_sum[pl.ds(start, 64), lo:hi]

    def down_unit(part_y, part_core, part_dp):
        start = pl.multiple_of(160 * part_y + 80 * part_core + 20 * part_dp // 8 * 8, 8)
        rows = d_sum[pl.ds(start, 24), :]
        return jnp.concatenate([rows[:16], fold_tail(rows[16:]), jnp.zeros((16, 128), F32)], axis=1)

    for lo, hi in COLS_FINE:
        d_sum[lo:hi, :] = dot_first(sk[:, lo:hi], bc[...])

    def pack_down(part_y, carry):
        for h in range(DP):
            unit = down_unit(part_y, 1 - core, h).astype(BF16)
            for part_x in range(XS):
                cs_x[part_x, part_y, h] = unit[:, DC * part_x : DC * part_x + DC]
        return carry

    def add_down(part_y, carry):
        for h in range(DP):
            unit = down_unit(part_y, core, h)
            for part_x in range(XS):
                more = unit[:, DC * part_x : DC * part_x + DC]
                p_x[part_x, part_y, h] = (p_x[part_x, part_y, h].astype(F32) + more).astype(BF16)
        return carry

    lax.fori_loop(0, YS, pack_down, 0)
    swap_x = send(remote(cs_x, p_x, 106, partner))
    swap_x.wait_recv()
    lax.fori_loop(0, YS, add_down, 0)
    ring_x = Ring(remote, p_x, (x_ra, x_rb, x_fp, x_fm), x, peers_x[0], peers_x[2], 92)
    ring_x.start()

    loads[6].wait()
    for c in range(CHUNKS):
        b_receive[c]()
        unpack(b_recv, spread, c, open_fine)
    for lo, hi in COLS_FINE:
        for t in range(FINE):
            back = gs[t, :, lo:hi].astype(F32) + spread[:, lo:hi]
            bpe[t + 1, :, lo:hi] = (back * pre[t, :, lo:hi]).astype(BF16)

    def time_grad(piece, cs, parts, place, shape):
        left, right = PIECES[piece]
        back_rows = bpe[1 : FINE + 1, :, left:right].reshape(FINE * PIX, right - left)
        part_y = 0
        for k in range(3):
            for lo, hi in COLS_FINE:
                block = ext[k : k + FINE, :, lo:hi].reshape(FINE * PIX, hi - lo)
                t_sum[k * C1 + lo : k * C1 + hi, left:right] = dot_first(block, back_rows)
                if part_y < YS and k * C1 + hi >= 480 * (part_y + 1):
                    for h in range(DP):
                        unit = time_unit(part_y, 1 - core, h, left, right).astype(BF16)
                        cs[place(part_y, h)] = unit.reshape(*shape, right - left)
                    if piece < 2:
                        at_y = place(part_y, slice(None))
                        send(remote(cs.at[at_y], parts.at[at_y], 98 + 4 * piece + part_y, partner))
                    part_y += 1

    def add_time(piece, parts, place, shape, part_y):
        left, right = PIECES[piece]
        for h in range(DP):
            unit = time_unit(part_y, core, h, left, right).reshape(*shape, right - left)
            parts[place(part_y, h)] = (parts[place(part_y, h)].astype(F32) + unit).astype(BF16)

    def by_y(part_y, h):
        return (part_y, h)

    def by_x(part_y, h):
        return (slice(None), part_y, h)

    def by_z(part_y, h):
        return (h, slice(None), part_y)

    time_grad(0, cs_0, p_0, by_y, (64,))
    ring_x.middle()
    time_grad(1, cs_1, p_1, by_x, (XS, 16))
    copies_0 = []
    for k in (2, 1, 3, 0):
        part_y = (y + k) % YS
        remote(cs_0.at[part_y], p_0.at[part_y], 98 + part_y, partner).wait_recv()
        add_time(0, p_0, by_y, (64,), part_y)
        if k > 0:
            copies_0.append(send(remote(p_0.at[part_y], r_0.at[k - 1], 79 + k, peers_y[k - 1])))
    time_grad(2, cs_2, p_2, by_z, (2, 32))
    swap_2 = send(remote(cs_2, p_2, 107, partner))
    for part_y in range(YS):
        remote(cs_1.at[:, part_y], p_1.at[:, part_y], 102 + part_y, partner).wait_recv()
        add_time(1, p_1, by_x, (XS, 16), part_y)
    copies_1 = [
        send(remote(p_1.at[(x + k) % XS], r_1.at[k - 1], 82 + k, peers_x[k - 1])) for k in (2, 1, 3)
    ]
    swap_2.wait_recv()
    for part_y in range(YS):
        add_time(2, p_2, by_z, (2, 32), part_y)
    copies_2 = [send(remote(p_2.at[z // 2, z % 2], zr_2.at[k], 171 + k, peers_z[k])) for k, z in enumerate(on_z)]

    def input_grad(t, count, lo, hi):
        rows = [bpe[t + k : t + k + count].reshape(count * PIX, C1) for k in range(3)]
        acc = dot_last(rows[2], wt[lo:hi, :])
        acc += dot_last(rows[1], wt[C1 + lo : C1 + hi, :])
        acc += dot_last(rows[0], wt[2 * C1 + lo : 2 * C1 + hi, :])
        acc = acc.reshape(count, PIX, hi - lo) + gs[t : t + count, :, lo:hi].astype(F32) + spread[:, lo:hi]
        gs[t : t + count, :, lo:hi] = acc.astype(BF16)

    def arrived(copies):
        for copy in copies:
            copy.wait_recv()

    def added(copies, own, more):
        arrived(copies)
        return (own.astype(F32) + sum(more[k].astype(F32) for k in range(len(copies)))).astype(BF16)

    input_grad(1, 2, *COLS_FINE[0])
    ring_x.arrived()
    for part_y in range(YS):
        p2_x[part_y] = ring_x.total(part_y).astype(BF16)
    copies_x = [send(remote(p2_x.at[(y + k) % YS], r2_x.at[k - 1], 113 + k, peers_y[k - 1])) for k in range(1, YS)]
    input_grad(1, 2, *COLS_FINE[1])
    input_grad(1, 2, *COLS_FINE[2])
    arrived(copies_0)
    for h in range(DP):
        total = p_0[y, h].astype(F32) + sum(r_0[k, h].astype(F32) for k in range(YS - 1))
        p2_0[:, h] = total.astype(BF16).reshape(XS, 16, -1)
    copies_0 = [send(remote(p2_0.at[(x + k) % XS], r2_0.at[k - 1], 107 + k, peers_x[k - 1])) for k in range(1, XS)]
    arrived(copies_1)
    for part_y in range(YS):
        p2_1[part_y] = (p_1[x, part_y].astype(F32) + sum(r_1[k, part_y].astype(F32) for k in range(XS - 1))).astype(BF16)
    copies_1 = [send(remote(p2_1.at[(y + k) % YS], r2_1.at[k - 1], 110 + k, peers_y[k - 1])) for k in range(1, YS)]
    back_first = send(remote(bpe.at[1], bpe.at[FINE + 1], 78, prev))
    back_last = send(remote(bpe.at[FINE], bpe.at[0], 79, nxt))
    p2_2[...] = added(copies_2, p_2[dp, zlo], zr_2)
    copies_2 = [send(remote(p2_2.at[(y + k) % YS], r2_2.at[k - 1], 177 + k, peers_y[k - 1])) for k in range(1, YS)]

    last_waits = []

    class OverZ:
        def __init__(self, src, slots, first, owner):
            self.src, self.slots, self.first, self.owner = src, slots, first, owner
            other = zlo if owner == 0 else 1 - zlo
            copies = []
            for k in range(DP):
                h = (dp + k) % DP
                slot = other * DP + k
                target = at(tm_=owner * XS + x, dp_=h)
                copies.append(remote(src.at[h], slots.at[slot], first + k, target, landed=first + slot))
            for copy in copies[1:]:
                copy.start()

            @pl.when(zlo != owner)
            def _():
                copies[0].start()

            def finish():
                for copy in copies[1:]:
                    copy.wait_send()

                @pl.when(zlo != owner)
                def _():
                    copies[0].wait_send()

            last_waits.append(finish)

        def gather(self, final, first):
            copies = [
                remote(final.at[x], final.at[x], first + k, peers_tm[k - 1], landed=first + TM + x)
                for k in range(1, TM)
            ]

            @pl.when(zlo == self.owner)
            def _():
                total = self.src[dp].astype(F32)
                for slot in range(1, 2 * DP):
                    ref = self.slots.at[slot]
                    remote(ref, ref, self.first + slot, partner).wait_recv()
                    total += self.slots[slot].astype(F32)
                final[x] = total.astype(BF16)
                for copy in copies:
                    copy.start()

            def finish():
                for k in range(1, XS):
                    ref = final.at[(x + k) % XS]
                    remote(ref, ref, first, partner, landed=first + TM + (x + k) % XS).wait_recv()

                @pl.when(zlo != self.owner)
                def _():
                    remote(final.at[x], final.at[x], first, partner, landed=first + TM + x).wait_recv()

                @pl.when(zlo == self.owner)
                def _():
                    for copy in copies:
                        copy.wait_send()

            last_waits.append(finish)

    sums = added(copies_x, p2_x[y], r2_x)
    for half in range(2):
        zs_x[half] = sums[:, :, half * DC // 2 : (half + 1) * DC // 2]
    z_copies = [
        send(remote(zs_x.at[z % 2, z // 2], zr_x.at[k], 133 + k, peers_z[k])) for k, z in enumerate(on_z)
    ]
    zs_0[...] = added(copies_0, p2_0[x], r2_0)
    over_z0 = OverZ(zs_0, zr_0, 117, 0)
    zs_1[...] = added(copies_1, p2_1[y], r2_1)
    over_z1 = OverZ(zs_1, zr_1, 125, 1)

    xs_2[x] = added(copies_2, p2_2[y], r2_2)
    copies_2 = [remote(xs_2.at[x], xs_2.at[x], 187 + k, peers_x[k - 1], landed=183 + x) for k in range(1, XS)]
    for copy in copies_2:
        send(copy)
    back_first.wait_recv()
    back_last.wait_recv()

    @pl.when(tm == 0)
    def _():
        bpe[0] = jnp.zeros((PIX, C1), BF16)

    @pl.when(tm == TM - 1)
    def _():
        bpe[FINE + 1] = jnp.zeros((PIX, C1), BF16)

    for lo, hi in COLS_FINE:
        input_grad(0, 1, lo, hi)
        input_grad(3, 1, lo, hi)
    store = pltpu.make_async_copy(gs, ig_out.at[0], local_sem.at[16])
    store.start()

    for k in range(1, XS):
        src = (x + k) % XS
        remote(xs_2.at[src], xs_2.at[src], 187, partner, landed=183 + src).wait_recv()
    f_2[zlo] = sum(xs_2[k].astype(F32) for k in range(XS)).astype(BF16)
    swap_z = send(remote(f_2.at[zlo], f_2.at[zlo], 191, at(tm_=(1 - zlo) * XS + x)))
    f_x[tm] = added(z_copies, zs_x[zlo, dp], zr_x)
    for k in range(1, TM):
        send(remote(f_x.at[tm], f_x.at[tm], 163 + k, peers_tm[k - 1]))
    over_z0.gather(f_0, 140)
    over_z1.gather(f_1, 152)
    for k in range(1, TM):
        src = (tm + TM - k) % TM
        remote(f_x.at[src], f_x.at[src], 163 + k, at(tm_=src)).wait_recv()
    for wait in last_waits:
        wait()
    swap_z.wait_recv()
    time0_out[...], time1_out[...], time2_out[...], down_out[...] = f_0[...], f_1[...], f_2[...], f_x[...]

    for copy in sent:
        copy.wait_send()
    ring_x.finish()
    store.wait()


def finish(ig, time0, time1, time2, down, ig_out, time_out, down_out, held, load_sem, store_sem):
    loads = [pltpu.make_async_copy(ig.at[0, t], held.at[t], load_sem.at[t]) for t in range(FINE)]
    stores = [pltpu.make_async_copy(held.at[t], ig_out.at[0, t], store_sem.at[t]) for t in range(FINE)]
    for load in loads:
        load.start()
    odd = lax.axis_index("dp") % 2 == 1
    scale = 1.0 / math.sqrt(ROWS_ALL)
    pieces = [time[...].astype(F32).reshape(64, -1) for time in (time0, time1, time2)]
    rows = jnp.concatenate(pieces, axis=1) * scale
    time_out[...] = jnp.where(odd, rows[4:64], rows[:60])
    halves = [down[half * XS + part_x] for part_x in range(XS) for half in range(2)]
    wide = jnp.concatenate(halves, axis=1).astype(F32) * (0.25 * scale)
    rows = jnp.concatenate([wide[:, :C2], open_tail(wide[:, C2 : C2 + C1])], axis=0)
    down_out[...] = jnp.where(odd, rows[4:24], rows[:20])
    for load, store in zip(loads, stores):
        load.wait()
        store.start()
    for store in stores:
        store.wait()


def first_over_y(n):
    v = pltpu.VMEM
    return [
        v((YS, DP, 64, n), BF16), v((YS, DP, 64, n), BF16),
        v((YS - 1, DP, 64, n), BF16),
        v((XS, DP, 16, n), BF16), v((XS - 1, DP, 16, n), BF16),
        v((DP, 16, n), BF16), v((2 * DP, 16, n), BF16), v((XS, 16, n), BF16),
    ]


def first_over_x(n):
    v = pltpu.VMEM
    return [
        v((XS, YS, DP, 16, n), BF16), v((XS, YS, DP, 16, n), BF16),
        v((XS - 1, YS, DP, 16, n), BF16),
        v((YS, DP, 16, n), BF16), v((YS - 1, DP, 16, n), BF16),
        v((DP, 16, n), BF16), v((2 * DP, 16, n), BF16), v((XS, 16, n), BF16),
    ]


def first_over_z(n):
    v = pltpu.VMEM
    return [
        v((DP, 2, YS, 32, n), BF16), v((DP, 2, YS, 32, n), BF16), v((7, YS, 32, n), BF16),
        v((YS, 32, n), BF16), v((YS - 1, 32, n), BF16), v((XS, 32, n), BF16), v((2, 32, n), BF16),
    ]


def shards(*args):
    v, hbm = pltpu.VMEM, pl.BlockSpec(memory_space=pl.ANY)
    vmem = pl.BlockSpec(memory_space=pltpu.VMEM)
    scratch = [
        v((FINE + 2, PIX, C1), BF16), v((3 * C1, C1), BF16), v((C1, C2), BF16), v((C2, C2), BF16), v((C2, C2), BF16),
        v((FINE, PIX, C1), BF16), v((PIX, C2), BF16), v((FINE, PIX, C1), F32), v((PIX, C1), BF16),
        v((PIX, C2), F32), v((PIX, C2), F32), v((PIX, C2), F32),
        v((PIX, C2), BF16), v((PIX, C2), BF16), v((PIX, C2), BF16), v((PIX, C2), BF16), v((PIX, C2), F32),
        *[v((CHUNKS, TM, 16, C1), BF16)] * 2, *[v((CHUNKS, TM, 16, FOLD), BF16)] * 4,
        v((PIX, C1), BF16), v((PIX, C2), BF16), v((PIX, C1), F32), v((FINE + 2, PIX, C1), BF16),
        v((3 * C1, C1), F32), v((C1, C2), F32),
        *first_over_y(PIECES[0][1] - PIECES[0][0]), *first_over_x(PIECES[1][1] - PIECES[1][0]),
        *first_over_z(PIECES[2][1] - PIECES[2][0]),
        v((XS, YS, DP, 16, DC), BF16), v((XS, YS, DP, 16, DC), BF16),
        *[v((2, DP, 16, DC), BF16)] * 2, *[v((4, DP, 16, DC), BF16)] * 2,
        v((YS, DP, 16, DC), BF16), v((YS - 1, DP, 16, DC), BF16),
        v((2, DP, 16, DC // 2), BF16), v((7, 16, DC // 2), BF16), v((TM, 16, DC // 2), BF16),
        pltpu.SemaphoreType.DMA((17,)), pltpu.SemaphoreType.DMA((192,)), pltpu.SemaphoreType.DMA((192,)),
    ]
    fine = jax.ShapeDtypeStruct((1, FINE, PIX, C1), BF16)
    ig, *sums = pl.pallas_call(
        kernel,
        out_shape=(
            fine,
            *[jax.ShapeDtypeStruct((XS, 16, hi - lo), BF16) for lo, hi in PIECES[:2]],
            jax.ShapeDtypeStruct((2, 32, PIECES[2][1] - PIECES[2][0]), BF16),
            jax.ShapeDtypeStruct((TM, 16, DC // 2), BF16),
        ),
        in_specs=[hbm] * 7,
        out_specs=(hbm, vmem, vmem, vmem, vmem),
        scratch_shapes=scratch,
        compiler_params=pltpu.CompilerParams(
            collective_id=0, has_side_effects=True, vmem_limit_bytes=60 * 1024 * 1024
        ),
        cost_estimate=pl.CostEstimate(flops=9 * 10**9, bytes_accessed=16 * 10**6, transcendentals=10**6),
    )(*args)
    return pl.pallas_call(
        finish,
        out_shape=(fine, jax.ShapeDtypeStruct((60, C1), F32), jax.ShapeDtypeStruct((20, C2), F32)),
        in_specs=[hbm, vmem, vmem, vmem, vmem],
        out_specs=(hbm, vmem, vmem),
        scratch_shapes=[
            v((FINE, PIX, C1), BF16),
            pltpu.SemaphoreType.DMA((FINE,)),
            pltpu.SemaphoreType.DMA((FINE,)),
        ],
        cost_estimate=pl.CostEstimate(flops=10**5, bytes_accessed=2 * 10**6, transcendentals=0),
    )(ig, *sums)


def solution(mesh):
    fine, whole = P("dp", "tm", "space", None), P()
    rows = P(("space", "dp"), None)
    return jax.shard_map(
        shards,
        mesh=mesh,
        in_specs=(fine, whole, whole, whole, whole, fine, fine),
        out_specs=(fine, rows, rows),
        check_vma=False,
    )
```

```python
import math

import jax
import jax.numpy as jnp
from jax import lax
from jax.experimental import pallas as pl
from jax.experimental.pallas import tpu as pltpu
from jax.sharding import PartitionSpec as P

C1, C2, DH = 640, 1280, 64
TM, YS, XS, DP = 8, 4, 4, 4
FINE, PIX = 4, 192
ROWS_ALL = 4 * 32 * 1536
EPS = 1e-06
MESH = pl.DeviceIdType.MESH
F32, BF16 = jnp.float32, jnp.bfloat16
COLS_FINE = ((0, 256), (256, 512), (512, 640))
COLS_COARSE = tuple((n, n + 256) for n in range(0, C2, 256))
CHUNKS, WIDE = 3, 64
FOLD = 384
DC = 512
TILES = 5
PIECES = ((0, 256), (256, 512), (512, 640))


def dot(left, right):
    return jnp.dot(left, right, preferred_element_type=F32)


def dot_last(left, right):
    return lax.dot_general(left, right, (((1,), (1,)), ((), ())), preferred_element_type=F32)


def dot_first(left, right):
    return lax.dot_general(left, right, (((0,), (0,)), ((), ())), preferred_element_type=F32)


def fold_tail(tail):
    return jnp.concatenate([tail[:, :C1], tail[:, C1:]], axis=0)


def fold_fine(rows):
    rest = jnp.concatenate([rows[:, FOLD:], jnp.zeros((8, 2 * FOLD - C1), F32)], axis=1)
    return jnp.concatenate([rows[:, :FOLD], rest], axis=0)


def open_fine(rows):
    return jnp.concatenate([rows[:8], rows[8:, : C1 - FOLD]], axis=1)


def open_tail(tail):
    return jnp.concatenate([tail[:8], tail[8:]], axis=1)


class Ring:
    def __init__(self, remote, parts, bufs, pos, plus, minus, first):
        self.parts, self.pos = parts, pos
        self.ra, self.rb, self.fp, self.fm = bufs
        lo, hi = pl.ds(0, 2), pl.ds(2, 2)
        self.ahead, self.behind, self.far = (pos + 1) % 4, (pos + 3) % 4, (pos + 2) % 4
        self.copies = [
            remote(parts.at[self.far, lo], self.ra, first, plus),
            remote(parts.at[self.far, hi], self.rb, first + 1, minus),
            remote(parts.at[self.ahead, hi], self.fp.at[hi], first + 2, plus),
            remote(parts.at[self.behind, lo], self.fm.at[lo], first + 3, minus),
            remote(parts.at[self.ahead, lo], self.fp.at[lo], first + 4, plus),
            remote(parts.at[self.behind, hi], self.fm.at[hi], first + 5, minus),
        ]

    def start(self):
        for copy in self.copies[:4]:
            copy.start()

    def middle(self):
        parts = self.parts
        self.copies[0].wait_recv()
        parts[self.ahead, 0:2] = (parts[self.ahead, 0:2].astype(F32) + self.ra[...].astype(F32)).astype(BF16)
        self.copies[4].start()
        self.copies[1].wait_recv()
        parts[self.behind, 2:4] = (parts[self.behind, 2:4].astype(F32) + self.rb[...].astype(F32)).astype(BF16)
        self.copies[5].start()

    def arrived(self):
        for copy in self.copies[2:]:
            copy.wait_recv()

    def total(self, i):
        return self.parts[self.pos, i].astype(F32) + self.fp[i].astype(F32) + self.fm[i].astype(F32)

    def finish(self):
        for copy in self.copies:
            copy.wait_send()


def attend_units(tiles):
    return [(i, slice(WIDE * g, WIDE * g + WIDE)) for i in range(len(tiles)) for g in range(CHUNKS)]


def pair_ones():
    rows, cols = (lax.broadcasted_iota(jnp.int32, (128, 128), d) for d in (0, 1))
    return ((rows // DH) == (cols // DH)).astype(F32).astype(BF16)


def pair_left():
    return (lax.broadcasted_iota(jnp.int32, (WIDE, 128), 1) < DH).astype(F32)


def pair_rows(rows):
    left = pair_left()
    return jnp.concatenate([rows * left.astype(BF16), rows * (1.0 - left).astype(BF16)], axis=0)


def head_sums(terms):
    sums = dot(jnp.concatenate([term.astype(BF16) for term in terms], axis=0), pair_ones())
    rows = terms[0].shape[0]
    return [sums[rows * i : rows * i + rows] for i in range(len(terms))]


def attend_scores(tiles, qf, kf, probs_ref, bq, bk):
    row_i, col_i = (lax.broadcasted_iota(jnp.int32, (WIDE, 128), d) for d in (0, 1))
    mask = ((row_i % 8) == (col_i % 8)).astype(F32)
    count, units = len(tiles), attend_units(tiles)
    q, k = [qf[:, c] for c in tiles], [kf[:, c] for c in tiles]
    factors = [lax.rsqrt(total * (1.0 / DH) + EPS) for total in head_sums([v * v for v in q + k])]
    qb = [(q[i] * factors[i]).astype(BF16) for i in range(count)]
    kb = [(k[i] * factors[count + i]).astype(BF16) for i in range(count)]
    for i, c in enumerate(tiles):
        qf[:, c], kf[:, c] = factors[i], factors[count + i]
        bq[:, c], bk[:, c] = qb[i], kb[i]
    raised = [jnp.exp(dot_last(qb[i][rows], pair_rows(kb[i][rows])) * 0.125) * mask for i, rows in units]
    for (i, rows), over, under in zip(units, raised, head_sums(raised)):
        probs_ref[rows, tiles[i]] = over / under


def attend_back(tiles, qf, kf, probs_ref, cb, gb, work, bq, bk):
    units = attend_units(tiles)
    index, left = range(len(units)), pair_left()

    def fold(both):
        return jnp.where(left > 0.5, both[:WIDE], both[WIDE:])

    queries = [bq[rows, tiles[i]] for i, rows in units]
    plain_keys = [bk[rows, tiles[i]] for i, rows in units]
    keys = [pair_rows(rows) for rows in plain_keys]
    upstream = [gb[rows, tiles[i]] for i, rows in units]
    probs = [probs_ref[rows, tiles[i]] for i, rows in units]
    back_probs = [dot_last(upstream[n], pair_rows(cb[rows, tiles[i]])) for n, (i, rows) in enumerate(units)]
    means = head_sums([p * b for p, b in zip(probs, back_probs)])
    scores = [(p * (b - m)).astype(BF16) for p, b, m in zip(probs, back_probs, means)]
    for n, (i, rows) in enumerate(units):
        values = fold(dot_first(probs[n].astype(BF16), upstream[n]))
        work[rows, tiles[i]] = upstream[n].astype(F32) + values
    back_q = [dot(scores[n], keys[n]) * 0.125 for n in index]
    back_k = [fold(dot_first(scores[n], queries[n])) * 0.125 for n in index]
    qn, kn = [rows.astype(F32) for rows in queries], [rows.astype(F32) for rows in plain_keys]
    mean_q = head_sums([b * v for b, v in zip(back_q, qn)])
    mean_k = head_sums([b * v for b, v in zip(back_k, kn)])
    for n, (i, rows) in enumerate(units):
        c = tiles[i]
        bq[rows, c] = (qf[rows, c] * (back_q[n] - qn[n] * (mean_q[n] * (1.0 / DH)))).astype(BF16)
        bk[rows, c] = (kf[rows, c] * (back_k[n] - kn[n] * (mean_k[n] * (1.0 / DH)))).astype(BF16)


def kernel(
    frames, w_time, w_down, w_query, w_key, grad_skip, grad_out,
    ig_out, time0_out, time1_out, time2_out, down_out,
    ext, wt, wd, wq, wk, gs, go, pre, skipsum, work, qf, kf, cb, gb, bq, bk, probs,
    g_send, g_recv, c_send, c_recv, b_send, b_recv, sk, bc, spread, bpe, t_sum, d_sum,
    cs_0, p_0, r_0, p2_0, r2_0, zs_0, zr_0, f_0,
    cs_1, p_1, r_1, p2_1, r2_1, zs_1, zr_1, f_1,
    cs_2, p_2, zr_2, p2_2, r2_2, xs_2, f_2,
    cs_x, p_x, x_ra, x_rb, x_fp, x_fm, p2_x, r2_x, zs_x, zr_x, f_x,
    local_sem, send_sem, recv_sem,
):
    tm, space, dp = lax.axis_index("tm"), lax.axis_index("space"), lax.axis_index("dp")
    core, y, zlo, x = space % 2, space // 2, tm // XS, tm % XS

    def at(tm_=None, space_=None, dp_=None):
        return {
            "tm": tm if tm_ is None else tm_,
            "space": space if space_ is None else space_,
            "dp": dp if dp_ is None else dp_,
        }

    loads = [
        pltpu.make_async_copy(src, dst, local_sem.at[i])
        for i, (src, dst) in enumerate(
            (
                (frames.at[0], ext.at[pl.ds(1, FINE)]),
                (w_time, wt),
                (w_down, wd),
                (grad_out.at[0, 0], go),
                (w_query, wq),
                (w_key, wk),
                (grad_skip.at[0], gs),
            )
        )
    ]
    loads[0].start()
    loads[1].start()

    peers_tm = [at(tm_=(tm + k) % TM) for k in range(1, TM)]
    partner = at(space_=y * 2 + 1 - core)
    peers_y = [at(space_=((y + k) % YS) * 2 + core) for k in range(1, YS)]
    peers_x = [at(tm_=zlo * XS + (x + k) % XS) for k in range(1, XS)]
    zpos = dp * 2 + zlo
    on_z = [(zpos + k) % 8 for k in range(1, 8)]
    peers_z = [at(tm_=z % 2 * XS + x, dp_=z // 2) for z in on_z]
    barrier = pltpu.get_barrier_semaphore()
    other_z = [at(tm_=tm_, dp_=(dp + k) % DP) for k in range(1, DP) for tm_ in (x, XS + x)]
    greeted = peers_tm + [partner] + peers_y + other_z
    for peer in greeted:
        pl.semaphore_signal(barrier, inc=1, device_id=peer, device_id_type=MESH)
    pl.semaphore_wait(barrier, len(greeted))

    def remote(src, dst, sem, device, landed=None):
        return pltpu.make_async_remote_copy(
            src_ref=src,
            dst_ref=dst,
            send_sem=send_sem.at[sem],
            recv_sem=recv_sem.at[sem if landed is None else landed],
            device_id=device,
            device_id_type=MESH,
        )

    def exchange(send, recv, c, first):
        copies = [
            remote(send.at[c, (tm + k) % TM], recv.at[c, tm], first + k, at(tm_=(tm + k) % TM)) for k in range(1, TM)
        ]
        own = pltpu.make_async_copy(send.at[c, tm], recv.at[c, tm], local_sem.at[7 + first // TM])
        for copy in copies:
            copy.start()
        own.start()

        def receive():
            for k in range(1, TM):
                src = (tm + TM - k) % TM
                remote(send.at[c, src], recv.at[c, src], first + k, at(tm_=src)).wait_recv()
            own.wait()

        sent.extend(copies)
        return receive

    sent = []

    def send(copy):
        copy.start()
        sent.append(copy)
        return copy

    def pack(src, dst, c, fold, width):
        rows = src[c * WIDE : (c + 1) * WIDE, :width].astype(F32)
        for f in range(TM):
            dst[c, f] = fold(rows[8 * f : 8 * f + 8]).astype(BF16)

    def unpack(src, dst, c, unfold):
        rows = [unfold(src[c, f].astype(F32)) for f in range(TM)]
        dst[c * WIDE : (c + 1) * WIDE, :] = jnp.concatenate(rows, axis=0).astype(dst.dtype)

    prev, nxt = at(tm_=(tm + TM - 1) % TM), at(tm_=(tm + 1) % TM)
    halos = []
    for c in range(CHUNKS):
        rows = pl.ds(c * WIDE, WIDE)
        first = send(remote(frames.at[0, 0, rows], ext.at[FINE + 1, rows], 72 + 2 * c, prev))
        last = send(remote(frames.at[0, FINE - 1, rows], ext.at[0, rows], 73 + 2 * c, nxt))
        halos.append((first, last))
    for load in loads[2:]:
        load.start()

    loads[0].wait()
    loads[1].wait()
    for lo, hi in COLS_FINE:
        n = hi - lo
        pre[:, :, lo:hi] = dot(ext[1:5].reshape(FINE * PIX, C1), wt[C1 : 2 * C1, lo:hi]).reshape(FINE, PIX, n)
        pre[1:4, :, lo:hi] += dot(ext[1:4].reshape(3 * PIX, C1), wt[:C1, lo:hi]).reshape(3, PIX, n)
        pre[0:3, :, lo:hi] += dot(ext[2:5].reshape(3 * PIX, C1), wt[2 * C1 :, lo:hi]).reshape(3, PIX, n)
    loads[3].wait()
    for c in range(CHUNKS):
        pack(go, g_send, c, fold_tail, C2)

    c_receive, g_receive = [], [exchange(g_send, g_recv, 0, 24)]
    for c in range(CHUNKS):
        rows = slice(c * WIDE, (c + 1) * WIDE)
        for copy in halos[c]:
            copy.wait_recv()

        @pl.when(tm == 0)
        def _():
            ext[0, rows] = jnp.zeros((WIDE, C1), BF16)

        @pl.when(tm == TM - 1)
        def _():
            ext[FINE + 1, rows] = jnp.zeros((WIDE, C1), BF16)

        for lo, hi in COLS_FINE:
            pre[0, rows, lo:hi] += dot(ext[0, rows], wt[:C1, lo:hi])
            pre[3, rows, lo:hi] += dot(ext[5, rows], wt[2 * C1 :, lo:hi])
            total = None
            for t in range(FINE):
                act = pre[t, rows, lo:hi]
                logistic = 1.0 / (1.0 + jnp.exp(-act))
                skip = (ext[t + 1, rows, lo:hi].astype(F32) + act * logistic).astype(BF16).astype(F32)
                total = skip if total is None else total + skip
                pre[t, rows, lo:hi] = logistic * (1.0 + act * (1.0 - logistic))
            skipsum[rows, lo:hi] = total.astype(BF16)
        pack(skipsum, c_send, c, fold_fine, C1)
        c_receive.append(exchange(c_send, c_recv, c, 8 * c))
    for c in range(1, CHUNKS):
        g_receive.append(exchange(g_send, g_recv, c, 24 + 8 * c))

    loads[2].wait()
    loads[4].wait()
    loads[5].wait()
    for c in range(CHUNKS):
        c_receive[c]()
        unpack(c_recv, sk, c, open_fine)
    for lo, hi in COLS_COARSE:
        cb[:, lo:hi] = (0.25 * dot(sk[...], wd[:, lo:hi])).astype(BF16)
    for lo, hi in COLS_COARSE:
        qf[:, lo:hi] = dot(cb[...], wq[:, lo:hi])
        kf[:, lo:hi] = dot(cb[...], wk[:, lo:hi])
    def tiles_of(i):
        return [pl.ds(pl.multiple_of((i * TILES + u) * 128, 128), 128) for u in range(TILES)]

    def some_scores(i, carry):
        attend_scores(tiles_of(i), qf, kf, probs, bq, bk)
        return carry

    def some_back(i, carry):
        attend_back(tiles_of(i), qf, kf, probs, cb, gb, work, bq, bk)
        return carry

    lax.fori_loop(0, C2 // 128 // TILES, some_scores, 0)
    for c in range(CHUNKS):
        g_receive[c]()
        unpack(g_recv, gb, c, open_tail)
    lax.fori_loop(0, C2 // 128 // TILES, some_back, 0)
    for lo, hi in COLS_COARSE:
        projected = dot_last(bq[...], wq[lo:hi, :]) + dot_last(bk[...], wk[lo:hi, :])
        bc[:, lo:hi] = (work[:, lo:hi] + projected).astype(BF16)
    for lo, hi in COLS_FINE:
        work[:, lo:hi] = 0.25 * dot_last(bc[...], wd[lo:hi, :])
    b_receive = []
    for c in range(CHUNKS):
        pack(work, b_send, c, fold_fine, C1)
        b_receive.append(exchange(b_send, b_recv, c, 48 + 8 * c))

    def time_unit(part_y, part_core, part_dp, lo, hi):
        start = pl.multiple_of(480 * part_y + 240 * part_core + 60 * part_dp // 8 * 8, 8)
        return t_sum[pl.ds(start, 64), lo:hi]

    def down_unit(part_y, part_core, part_dp):
        start = pl.multiple_of(160 * part_y + 80 * part_core + 20 * part_dp // 8 * 8, 8)
        rows = d_sum[pl.ds(start, 24), :]
        return jnp.concatenate([rows[:16], fold_tail(rows[16:]), jnp.zeros((16, 128), F32)], axis=1)

    for lo, hi in COLS_FINE:
        d_sum[lo:hi, :] = dot_first(sk[:, lo:hi], bc[...])

    def pack_down(part_y, carry):
        for h in range(DP):
            unit = down_unit(part_y, 1 - core, h).astype(BF16)
            for part_x in range(XS):
                cs_x[part_y, part_x, h] = unit[:, DC * part_x : DC * part_x + DC]
        return carry

    def add_down(part_y, carry):
        for h in range(DP):
            unit = down_unit(part_y, core, h)
            for part_x in range(XS):
                more = unit[:, DC * part_x : DC * part_x + DC]
                p_x[part_y, part_x, h] = (p_x[part_y, part_x, h].astype(F32) + more).astype(BF16)
        return carry

    lax.fori_loop(0, YS, pack_down, 0)
    swap_x = send(remote(cs_x, p_x, 106, partner))
    swap_x.wait_recv()
    lax.fori_loop(0, YS, add_down, 0)
    ring_d = Ring(remote, p_x, (x_ra, x_rb, x_fp, x_fm), y, peers_y[0], peers_y[2], 92)
    ring_d.start()

    loads[6].wait()
    for c in range(CHUNKS):
        b_receive[c]()
        unpack(b_recv, spread, c, open_fine)
    for lo, hi in COLS_FINE:
        for t in range(FINE):
            back = gs[t, :, lo:hi].astype(F32) + spread[:, lo:hi]
            bpe[t + 1, :, lo:hi] = (back * pre[t, :, lo:hi]).astype(BF16)

    back_first = send(remote(bpe.at[1], bpe.at[FINE + 1], 78, prev))
    back_last = send(remote(bpe.at[FINE], bpe.at[0], 79, nxt))

    def time_grad(piece, cs, parts, place, shape):
        left, right = PIECES[piece]
        back_rows = bpe[1 : FINE + 1, :, left:right].reshape(FINE * PIX, right - left)
        part_y = 0
        for k in range(3):
            for lo, hi in COLS_FINE:
                block = ext[k : k + FINE, :, lo:hi].reshape(FINE * PIX, hi - lo)
                t_sum[k * C1 + lo : k * C1 + hi, left:right] = dot_first(block, back_rows)
                if part_y < YS and k * C1 + hi >= 480 * (part_y + 1):
                    for h in range(DP):
                        unit = time_unit(part_y, 1 - core, h, left, right).astype(BF16)
                        cs[place(part_y, h)] = unit.reshape(*shape, right - left)
                    if piece < 2:
                        at_y = place(part_y, slice(None))
                        send(remote(cs.at[at_y], parts.at[at_y], 98 + 4 * piece + part_y, partner))
                    part_y += 1

    def add_time(piece, parts, place, shape, part_y):
        left, right = PIECES[piece]
        for h in range(DP):
            unit = time_unit(part_y, core, h, left, right).reshape(*shape, right - left)
            parts[place(part_y, h)] = (parts[place(part_y, h)].astype(F32) + unit).astype(BF16)

    def by_y(part_y, h):
        return (part_y, h)

    def by_x(part_y, h):
        return (slice(None), part_y, h)

    def by_z(part_y, h):
        return (h, slice(None), part_y)

    time_grad(0, cs_0, p_0, by_y, (64,))
    ring_d.middle()
    time_grad(1, cs_1, p_1, by_x, (XS, 16))
    copies_0 = []
    for k in (2, 1, 3, 0):
        part_y = (y + k) % YS
        remote(cs_0.at[part_y], p_0.at[part_y], 98 + part_y, partner).wait_recv()
        add_time(0, p_0, by_y, (64,), part_y)
        if k > 0:
            copies_0.append(send(remote(p_0.at[part_y], r_0.at[k - 1], 79 + k, peers_y[k - 1])))
    time_grad(2, cs_2, p_2, by_z, (2, 32))
    swap_2 = send(remote(cs_2, p_2, 107, partner))
    for part_y in range(YS):
        remote(cs_1.at[:, part_y], p_1.at[:, part_y], 102 + part_y, partner).wait_recv()
        add_time(1, p_1, by_x, (XS, 16), part_y)
    copies_1 = [
        send(remote(p_1.at[(x + k) % XS], r_1.at[k - 1], 82 + k, peers_x[k - 1])) for k in (2, 1, 3)
    ]
    swap_2.wait_recv()
    for part_y in range(YS):
        add_time(2, p_2, by_z, (2, 32), part_y)
    copies_2 = [send(remote(p_2.at[z // 2, z % 2], zr_2.at[k], 171 + k, peers_z[k])) for k, z in enumerate(on_z)]

    def input_grad(t, count, lo, hi):
        rows = [bpe[t + k : t + k + count].reshape(count * PIX, C1) for k in range(3)]
        acc = dot_last(rows[2], wt[lo:hi, :])
        acc += dot_last(rows[1], wt[C1 + lo : C1 + hi, :])
        acc += dot_last(rows[0], wt[2 * C1 + lo : 2 * C1 + hi, :])
        acc = acc.reshape(count, PIX, hi - lo) + gs[t : t + count, :, lo:hi].astype(F32) + spread[:, lo:hi]
        gs[t : t + count, :, lo:hi] = acc.astype(BF16)

    def arrived(copies):
        for copy in copies:
            copy.wait_recv()

    def added(copies, own, more):
        arrived(copies)
        return (own.astype(F32) + sum(more[k].astype(F32) for k in range(len(copies)))).astype(BF16)

    input_grad(1, 2, *COLS_FINE[0])
    ring_d.arrived()
    for part_x in range(XS):
        p2_x[part_x] = ring_d.total(part_x).astype(BF16)
    copies_x = [send(remote(p2_x.at[(x + k) % XS], r2_x.at[k - 1], 113 + k, peers_x[k - 1])) for k in range(1, XS)]
    input_grad(1, 2, *COLS_FINE[1])
    input_grad(1, 2, *COLS_FINE[2])
    back_first.wait_recv()
    back_last.wait_recv()

    @pl.when(tm == 0)
    def _():
        bpe[0] = jnp.zeros((PIX, C1), BF16)

    @pl.when(tm == TM - 1)
    def _():
        bpe[FINE + 1] = jnp.zeros((PIX, C1), BF16)

    for lo, hi in COLS_FINE:
        input_grad(0, 1, lo, hi)
        input_grad(3, 1, lo, hi)
    store = pltpu.make_async_copy(gs, ig_out.at[0], local_sem.at[16])
    store.start()

    arrived(copies_0)
    for h in range(DP):
        total = p_0[y, h].astype(F32) + sum(r_0[k, h].astype(F32) for k in range(YS - 1))
        p2_0[:, h] = total.astype(BF16).reshape(XS, 16, -1)
    copies_0 = [send(remote(p2_0.at[(x + k) % XS], r2_0.at[k - 1], 107 + k, peers_x[k - 1])) for k in range(1, XS)]
    arrived(copies_1)
    for part_y in range(YS):
        p2_1[part_y] = (p_1[x, part_y].astype(F32) + sum(r_1[k, part_y].astype(F32) for k in range(XS - 1))).astype(BF16)
    copies_1 = [send(remote(p2_1.at[(y + k) % YS], r2_1.at[k - 1], 110 + k, peers_y[k - 1])) for k in range(1, YS)]
    p2_2[...] = added(copies_2, p_2[dp, zlo], zr_2)
    copies_2 = [send(remote(p2_2.at[(y + k) % YS], r2_2.at[k - 1], 177 + k, peers_y[k - 1])) for k in range(1, YS)]

    last_waits = []

    class OverZ:
        def __init__(self, src, slots, first, owner):
            self.src, self.slots, self.first, self.owner = src, slots, first, owner
            other = zlo if owner == 0 else 1 - zlo
            copies = []
            for k in range(DP):
                h = (dp + k) % DP
                slot = other * DP + k
                target = at(tm_=owner * XS + x, dp_=h)
                copies.append(remote(src.at[h], slots.at[slot], first + k, target, landed=first + slot))
            for copy in copies[1:]:
                copy.start()

            @pl.when(zlo != owner)
            def _():
                copies[0].start()

            def finish():
                for copy in copies[1:]:
                    copy.wait_send()

                @pl.when(zlo != owner)
                def _():
                    copies[0].wait_send()

            last_waits.append(finish)

        def gather(self, final, first):
            copies = [
                remote(final.at[x], final.at[x], first + k, peers_tm[k - 1], landed=first + TM + x)
                for k in range(1, TM)
            ]

            @pl.when(zlo == self.owner)
            def _():
                total = self.src[dp].astype(F32)
                for slot in range(1, 2 * DP):
                    ref = self.slots.at[slot]
                    remote(ref, ref, self.first + slot, partner).wait_recv()
                    total += self.slots[slot].astype(F32)
                final[x] = total.astype(BF16)
                for copy in copies:
                    copy.start()

            def finish():
                for k in range(1, XS):
                    ref = final.at[(x + k) % XS]
                    remote(ref, ref, first, partner, landed=first + TM + (x + k) % XS).wait_recv()

                @pl.when(zlo != self.owner)
                def _():
                    remote(final.at[x], final.at[x], first, partner, landed=first + TM + x).wait_recv()

                @pl.when(zlo == self.owner)
                def _():
                    for copy in copies:
                        copy.wait_send()

            last_waits.append(finish)

    sums = added(copies_x, p2_x[x], r2_x)
    for half in range(2):
        zs_x[half] = sums[:, :, half * DC // 2 : (half + 1) * DC // 2]
    z_copies = [
        send(remote(zs_x.at[z % 2, z // 2], zr_x.at[k], 133 + k, peers_z[k])) for k, z in enumerate(on_z)
    ]
    zs_0[...] = added(copies_0, p2_0[x], r2_0)
    over_z0 = OverZ(zs_0, zr_0, 117, 0)
    zs_1[...] = added(copies_1, p2_1[y], r2_1)
    over_z1 = OverZ(zs_1, zr_1, 125, 1)

    xs_2[x] = added(copies_2, p2_2[y], r2_2)
    copies_2 = [remote(xs_2.at[x], xs_2.at[x], 187 + k, peers_x[k - 1], landed=183 + x) for k in range(1, XS)]
    for copy in copies_2:
        send(copy)

    for k in range(1, XS):
        src = (x + k) % XS
        remote(xs_2.at[src], xs_2.at[src], 187, partner, landed=183 + src).wait_recv()
    f_2[zlo] = sum(xs_2[k].astype(F32) for k in range(XS)).astype(BF16)
    swap_z = send(remote(f_2.at[zlo], f_2.at[zlo], 191, at(tm_=(1 - zlo) * XS + x)))
    f_x[tm] = added(z_copies, zs_x[zlo, dp], zr_x)
    for k in range(1, TM):
        send(remote(f_x.at[tm], f_x.at[tm], 163 + k, peers_tm[k - 1]))
    over_z0.gather(f_0, 140)
    over_z1.gather(f_1, 152)
    for k in range(1, TM):
        src = (tm + TM - k) % TM
        remote(f_x.at[src], f_x.at[src], 163 + k, at(tm_=src)).wait_recv()
    for wait in last_waits:
        wait()
    swap_z.wait_recv()
    time0_out[...], time1_out[...], time2_out[...], down_out[...] = f_0[...], f_1[...], f_2[...], f_x[...]

    for copy in sent:
        copy.wait_send()
    ring_d.finish()
    store.wait()


def finish(ig, time0, time1, time2, down, ig_out, time_out, down_out, held, load_sem, store_sem):
    loads = [pltpu.make_async_copy(ig.at[0, t], held.at[t], load_sem.at[t]) for t in range(FINE)]
    stores = [pltpu.make_async_copy(held.at[t], ig_out.at[0, t], store_sem.at[t]) for t in range(FINE)]
    for load in loads:
        load.start()
    odd = lax.axis_index("dp") % 2 == 1
    scale = 1.0 / math.sqrt(ROWS_ALL)
    pieces = [time[...].astype(F32).reshape(64, -1) for time in (time0, time1, time2)]
    rows = jnp.concatenate(pieces, axis=1) * scale
    time_out[...] = jnp.where(odd, rows[4:64], rows[:60])
    halves = [down[half * XS + part_x] for part_x in range(XS) for half in range(2)]
    wide = jnp.concatenate(halves, axis=1).astype(F32) * (0.25 * scale)
    rows = jnp.concatenate([wide[:, :C2], open_tail(wide[:, C2 : C2 + C1])], axis=0)
    down_out[...] = jnp.where(odd, rows[4:24], rows[:20])
    for load, store in zip(loads, stores):
        load.wait()
        store.start()
    for store in stores:
        store.wait()


def first_over_y(n):
    v = pltpu.VMEM
    return [
        v((YS, DP, 64, n), BF16), v((YS, DP, 64, n), BF16),
        v((YS - 1, DP, 64, n), BF16),
        v((XS, DP, 16, n), BF16), v((XS - 1, DP, 16, n), BF16),
        v((DP, 16, n), BF16), v((2 * DP, 16, n), BF16), v((XS, 16, n), BF16),
    ]


def first_over_x(n):
    v = pltpu.VMEM
    return [
        v((XS, YS, DP, 16, n), BF16), v((XS, YS, DP, 16, n), BF16),
        v((XS - 1, YS, DP, 16, n), BF16),
        v((YS, DP, 16, n), BF16), v((YS - 1, DP, 16, n), BF16),
        v((DP, 16, n), BF16), v((2 * DP, 16, n), BF16), v((XS, 16, n), BF16),
    ]


def first_over_z(n):
    v = pltpu.VMEM
    return [
        v((DP, 2, YS, 32, n), BF16), v((DP, 2, YS, 32, n), BF16), v((7, YS, 32, n), BF16),
        v((YS, 32, n), BF16), v((YS - 1, 32, n), BF16), v((XS, 32, n), BF16), v((2, 32, n), BF16),
    ]


def shards(*args):
    v, hbm = pltpu.VMEM, pl.BlockSpec(memory_space=pl.ANY)
    vmem = pl.BlockSpec(memory_space=pltpu.VMEM)
    scratch = [
        v((FINE + 2, PIX, C1), BF16), v((3 * C1, C1), BF16), v((C1, C2), BF16), v((C2, C2), BF16), v((C2, C2), BF16),
        v((FINE, PIX, C1), BF16), v((PIX, C2), BF16), v((FINE, PIX, C1), F32), v((PIX, C1), BF16),
        v((PIX, C2), F32), v((PIX, C2), F32), v((PIX, C2), F32),
        v((PIX, C2), BF16), v((PIX, C2), BF16), v((PIX, C2), BF16), v((PIX, C2), BF16), v((PIX, C2), F32),
        *[v((CHUNKS, TM, 16, C1), BF16)] * 2, *[v((CHUNKS, TM, 16, FOLD), BF16)] * 4,
        v((PIX, C1), BF16), v((PIX, C2), BF16), v((PIX, C1), F32), v((FINE + 2, PIX, C1), BF16),
        v((3 * C1, C1), F32), v((C1, C2), F32),
        *first_over_y(PIECES[0][1] - PIECES[0][0]), *first_over_x(PIECES[1][1] - PIECES[1][0]),
        *first_over_z(PIECES[2][1] - PIECES[2][0]),
        v((XS, YS, DP, 16, DC), BF16), v((XS, YS, DP, 16, DC), BF16),
        *[v((2, DP, 16, DC), BF16)] * 2, *[v((4, DP, 16, DC), BF16)] * 2,
        v((YS, DP, 16, DC), BF16), v((YS - 1, DP, 16, DC), BF16),
        v((2, DP, 16, DC // 2), BF16), v((7, 16, DC // 2), BF16), v((TM, 16, DC // 2), BF16),
        pltpu.SemaphoreType.DMA((17,)), pltpu.SemaphoreType.DMA((192,)), pltpu.SemaphoreType.DMA((192,)),
    ]
    fine = jax.ShapeDtypeStruct((1, FINE, PIX, C1), BF16)
    ig, *sums = pl.pallas_call(
        kernel,
        out_shape=(
            fine,
            *[jax.ShapeDtypeStruct((XS, 16, hi - lo), BF16) for lo, hi in PIECES[:2]],
            jax.ShapeDtypeStruct((2, 32, PIECES[2][1] - PIECES[2][0]), BF16),
            jax.ShapeDtypeStruct((TM, 16, DC // 2), BF16),
        ),
        in_specs=[hbm] * 7,
        out_specs=(hbm, vmem, vmem, vmem, vmem),
        scratch_shapes=scratch,
        compiler_params=pltpu.CompilerParams(
            collective_id=0, has_side_effects=True, vmem_limit_bytes=60 * 1024 * 1024
        ),
        cost_estimate=pl.CostEstimate(flops=9 * 10**9, bytes_accessed=16 * 10**6, transcendentals=10**6),
    )(*args)
    return pl.pallas_call(
        finish,
        out_shape=(fine, jax.ShapeDtypeStruct((60, C1), F32), jax.ShapeDtypeStruct((20, C2), F32)),
        in_specs=[hbm, vmem, vmem, vmem, vmem],
        out_specs=(hbm, vmem, vmem),
        scratch_shapes=[
            v((FINE, PIX, C1), BF16),
            pltpu.SemaphoreType.DMA((FINE,)),
            pltpu.SemaphoreType.DMA((FINE,)),
        ],
        cost_estimate=pl.CostEstimate(flops=10**5, bytes_accessed=2 * 10**6, transcendentals=0),
    )(ig, *sums)


def solution(mesh):
    fine, whole = P("dp", "tm", "space", None), P()
    rows = P(("space", "dp"), None)
    return jax.shard_map(
        shards,
        mesh=mesh,
        in_specs=(fine, whole, whole, whole, whole, fine, fine),
        out_specs=(fine, rows, rows),
        check_vma=False,
    )
```

```python
import math

import jax
import jax.numpy as jnp
from jax import lax
from jax.experimental import pallas as pl
from jax.experimental.pallas import tpu as pltpu
from jax.sharding import PartitionSpec as P

C1, C2, DH = 640, 1280, 64
TM, YS, XS, DP = 8, 4, 4, 4
FINE, PIX = 4, 192
ROWS_ALL = 4 * 32 * 1536
EPS = 1e-06
MESH = pl.DeviceIdType.MESH
F32, BF16 = jnp.float32, jnp.bfloat16
COLS_FINE = ((0, 256), (256, 512), (512, 640))
COLS_COARSE = tuple((n, n + 256) for n in range(0, C2, 256))
CHUNKS, WIDE = 3, 64
FOLD = 384
DC = 512
TILES = 5
PIECES = ((0, 256), (256, 512), (512, 640))


def dot(left, right):
    return jnp.dot(left, right, preferred_element_type=F32)


def dot_last(left, right):
    return lax.dot_general(left, right, (((1,), (1,)), ((), ())), preferred_element_type=F32)


def dot_first(left, right):
    return lax.dot_general(left, right, (((0,), (0,)), ((), ())), preferred_element_type=F32)


def fold_tail(tail):
    return jnp.concatenate([tail[:, :C1], tail[:, C1:]], axis=0)


def fold_fine(rows):
    rest = jnp.concatenate([rows[:, FOLD:], jnp.zeros((8, 2 * FOLD - C1), F32)], axis=1)
    return jnp.concatenate([rows[:, :FOLD], rest], axis=0)


def open_fine(rows):
    return jnp.concatenate([rows[:8], rows[8:, : C1 - FOLD]], axis=1)


def open_tail(tail):
    return jnp.concatenate([tail[:8], tail[8:]], axis=1)


class Ring:
    def __init__(self, remote, parts, bufs, pos, plus, minus, first):
        self.parts, self.pos = parts, pos
        self.ra, self.rb, self.fp, self.fm = bufs
        lo, hi = pl.ds(0, 2), pl.ds(2, 2)
        self.ahead, self.behind, self.far = (pos + 1) % 4, (pos + 3) % 4, (pos + 2) % 4
        self.copies = [
            remote(parts.at[self.far, lo], self.ra, first, plus),
            remote(parts.at[self.far, hi], self.rb, first + 1, minus),
            remote(parts.at[self.ahead, hi], self.fp.at[hi], first + 2, plus),
            remote(parts.at[self.behind, lo], self.fm.at[lo], first + 3, minus),
            remote(parts.at[self.ahead, lo], self.fp.at[lo], first + 4, plus),
            remote(parts.at[self.behind, hi], self.fm.at[hi], first + 5, minus),
        ]

    def start(self):
        for copy in self.copies[:4]:
            copy.start()

    def middle(self):
        parts = self.parts
        self.copies[0].wait_recv()
        parts[self.ahead, 0:2] = (parts[self.ahead, 0:2].astype(F32) + self.ra[...].astype(F32)).astype(BF16)
        self.copies[4].start()
        self.copies[1].wait_recv()
        parts[self.behind, 2:4] = (parts[self.behind, 2:4].astype(F32) + self.rb[...].astype(F32)).astype(BF16)
        self.copies[5].start()

    def arrived(self):
        for copy in self.copies[2:]:
            copy.wait_recv()

    def total(self, i):
        return self.parts[self.pos, i].astype(F32) + self.fp[i].astype(F32) + self.fm[i].astype(F32)

    def finish(self):
        for copy in self.copies:
            copy.wait_send()


def attend_units(tiles):
    return [(i, slice(WIDE * g, WIDE * g + WIDE)) for i in range(len(tiles)) for g in range(CHUNKS)]


def pair_ones():
    rows, cols = (lax.broadcasted_iota(jnp.int32, (128, 128), d) for d in (0, 1))
    return ((rows // DH) == (cols // DH)).astype(F32).astype(BF16)


def pair_left():
    return (lax.broadcasted_iota(jnp.int32, (WIDE, 128), 1) < DH).astype(F32)


def pair_rows(rows):
    left = pair_left()
    return jnp.concatenate([rows * left.astype(BF16), rows * (1.0 - left).astype(BF16)], axis=0)


def head_sums(terms):
    sums = dot(jnp.concatenate([term.astype(BF16) for term in terms], axis=0), pair_ones())
    rows = terms[0].shape[0]
    return [sums[rows * i : rows * i + rows] for i in range(len(terms))]


def attend_scores(tiles, qf, kf, probs_ref, bq, bk):
    row_i, col_i = (lax.broadcasted_iota(jnp.int32, (WIDE, 128), d) for d in (0, 1))
    mask = ((row_i % 8) == (col_i % 8)).astype(F32)
    count, units = len(tiles), attend_units(tiles)
    q, k = [qf[:, c] for c in tiles], [kf[:, c] for c in tiles]
    factors = [lax.rsqrt(total * (1.0 / DH) + EPS) for total in head_sums([v * v for v in q + k])]
    qb = [(q[i] * factors[i]).astype(BF16) for i in range(count)]
    kb = [(k[i] * factors[count + i]).astype(BF16) for i in range(count)]
    for i, c in enumerate(tiles):
        qf[:, c], kf[:, c] = factors[i], factors[count + i]
        bq[:, c], bk[:, c] = qb[i], kb[i]
    raised = [jnp.exp(dot_last(qb[i][rows], pair_rows(kb[i][rows])) * 0.125) * mask for i, rows in units]
    for (i, rows), over, under in zip(units, raised, head_sums(raised)):
        probs_ref[rows, tiles[i]] = over / under


def attend_back(tiles, qf, kf, probs_ref, cb, gb, work, bq, bk):
    units = attend_units(tiles)
    index, left = range(len(units)), pair_left()

    def fold(both):
        return jnp.where(left > 0.5, both[:WIDE], both[WIDE:])

    queries = [bq[rows, tiles[i]] for i, rows in units]
    plain_keys = [bk[rows, tiles[i]] for i, rows in units]
    keys = [pair_rows(rows) for rows in plain_keys]
    upstream = [gb[rows, tiles[i]] for i, rows in units]
    probs = [probs_ref[rows, tiles[i]] for i, rows in units]
    back_probs = [dot_last(upstream[n], pair_rows(cb[rows, tiles[i]])) for n, (i, rows) in enumerate(units)]
    means = head_sums([p * b for p, b in zip(probs, back_probs)])
    scores = [(p * (b - m)).astype(BF16) for p, b, m in zip(probs, back_probs, means)]
    for n, (i, rows) in enumerate(units):
        values = fold(dot_first(probs[n].astype(BF16), upstream[n]))
        work[rows, tiles[i]] = upstream[n].astype(F32) + values
    back_q = [dot(scores[n], keys[n]) * 0.125 for n in index]
    back_k = [fold(dot_first(scores[n], queries[n])) * 0.125 for n in index]
    qn, kn = [rows.astype(F32) for rows in queries], [rows.astype(F32) for rows in plain_keys]
    mean_q = head_sums([b * v for b, v in zip(back_q, qn)])
    mean_k = head_sums([b * v for b, v in zip(back_k, kn)])
    for n, (i, rows) in enumerate(units):
        c = tiles[i]
        bq[rows, c] = (qf[rows, c] * (back_q[n] - qn[n] * (mean_q[n] * (1.0 / DH)))).astype(BF16)
        bk[rows, c] = (kf[rows, c] * (back_k[n] - kn[n] * (mean_k[n] * (1.0 / DH)))).astype(BF16)


def kernel(
    frames, w_time, w_down, w_query, w_key, grad_skip, grad_out,
    ig_out, time0_out, time1_out, time2_out, down_out,
    ext, wt, wd, wq, wk, gs, go, pre, skipsum, work, qf, kf, cb, gb, bq, bk, probs,
    g_send, g_recv, c_send, c_recv, b_send, b_recv, sk, bc, spread, bpe, t_sum, d_sum,
    cs_0, p_0, r_0, p2_0, r2_0, zs_0, zr_0, f_0,
    cs_1, p_1, r_1, p2_1, r2_1, zs_1, zr_1, f_1,
    cs_2, p_2, zr_2, p2_2, r2_2, xs_2, f_2,
    cs_x, p_x, x_ra, x_rb, x_fp, x_fm, p2_x, r2_x, zs_x, zr_x, f_x,
    local_sem, send_sem, recv_sem,
):
    tm, space, dp = lax.axis_index("tm"), lax.axis_index("space"), lax.axis_index("dp")
    core, y, zlo, x = space % 2, space // 2, tm // XS, tm % XS

    def at(tm_=None, space_=None, dp_=None):
        return {
            "tm": tm if tm_ is None else tm_,
            "space": space if space_ is None else space_,
            "dp": dp if dp_ is None else dp_,
        }

    loads = [
        pltpu.make_async_copy(src, dst, local_sem.at[i])
        for i, (src, dst) in enumerate(
            (
                (frames.at[0], ext.at[pl.ds(1, FINE)]),
                (w_time, wt),
                (w_down, wd),
                (grad_out.at[0, 0], go),
                (w_query, wq),
                (w_key, wk),
                (grad_skip.at[0], gs),
            )
        )
    ]
    loads[0].start()
    loads[1].start()

    peers_tm = [at(tm_=(tm + k) % TM) for k in range(1, TM)]
    partner = at(space_=y * 2 + 1 - core)
    peers_y = [at(space_=((y + k) % YS) * 2 + core) for k in range(1, YS)]
    peers_x = [at(tm_=zlo * XS + (x + k) % XS) for k in range(1, XS)]
    zpos = dp * 2 + zlo
    on_z = [(zpos + k) % 8 for k in range(1, 8)]
    peers_z = [at(tm_=z % 2 * XS + x, dp_=z // 2) for z in on_z]
    barrier = pltpu.get_barrier_semaphore()
    other_z = [at(tm_=tm_, dp_=(dp + k) % DP) for k in range(1, DP) for tm_ in (x, XS + x)]
    greeted = peers_tm + [partner] + peers_y + other_z
    for peer in greeted:
        pl.semaphore_signal(barrier, inc=1, device_id=peer, device_id_type=MESH)
    pl.semaphore_wait(barrier, len(greeted))

    def remote(src, dst, sem, device, landed=None):
        return pltpu.make_async_remote_copy(
            src_ref=src,
            dst_ref=dst,
            send_sem=send_sem.at[sem],
            recv_sem=recv_sem.at[sem if landed is None else landed],
            device_id=device,
            device_id_type=MESH,
        )

    def exchange(send, recv, c, first):
        copies = [
            remote(send.at[c, (tm + k) % TM], recv.at[c, tm], first + k, at(tm_=(tm + k) % TM)) for k in range(1, TM)
        ]
        own = pltpu.make_async_copy(send.at[c, tm], recv.at[c, tm], local_sem.at[7 + first // TM])
        for copy in copies:
            copy.start()
        own.start()

        def receive():
            for k in range(1, TM):
                src = (tm + TM - k) % TM
                remote(send.at[c, src], recv.at[c, src], first + k, at(tm_=src)).wait_recv()
            own.wait()

        sent.extend(copies)
        return receive

    sent = []

    def send(copy):
        copy.start()
        sent.append(copy)
        return copy

    def pack(src, dst, c, fold, width):
        rows = src[c * WIDE : (c + 1) * WIDE, :width].astype(F32)
        for f in range(TM):
            dst[c, f] = fold(rows[8 * f : 8 * f + 8]).astype(BF16)

    def unpack(src, dst, c, unfold):
        rows = [unfold(src[c, f].astype(F32)) for f in range(TM)]
        dst[c * WIDE : (c + 1) * WIDE, :] = jnp.concatenate(rows, axis=0).astype(dst.dtype)

    prev, nxt = at(tm_=(tm + TM - 1) % TM), at(tm_=(tm + 1) % TM)
    halos = []
    for c in range(CHUNKS):
        rows = pl.ds(c * WIDE, WIDE)
        first = send(remote(frames.at[0, 0, rows], ext.at[FINE + 1, rows], 72 + 2 * c, prev))
        last = send(remote(frames.at[0, FINE - 1, rows], ext.at[0, rows], 73 + 2 * c, nxt))
        halos.append((first, last))
    for load in loads[2:]:
        load.start()

    loads[0].wait()
    loads[1].wait()
    for lo, hi in COLS_FINE:
        n = hi - lo
        pre[:, :, lo:hi] = dot(ext[1:5].reshape(FINE * PIX, C1), wt[C1 : 2 * C1, lo:hi]).reshape(FINE, PIX, n)
        pre[1:4, :, lo:hi] += dot(ext[1:4].reshape(3 * PIX, C1), wt[:C1, lo:hi]).reshape(3, PIX, n)
        pre[0:3, :, lo:hi] += dot(ext[2:5].reshape(3 * PIX, C1), wt[2 * C1 :, lo:hi]).reshape(3, PIX, n)
    loads[3].wait()
    for c in range(CHUNKS):
        pack(go, g_send, c, fold_tail, C2)

    c_receive, g_receive = [], [exchange(g_send, g_recv, 0, 24)]
    for c in range(CHUNKS):
        rows = slice(c * WIDE, (c + 1) * WIDE)
        for copy in halos[c]:
            copy.wait_recv()

        @pl.when(tm == 0)
        def _():
            ext[0, rows] = jnp.zeros((WIDE, C1), BF16)

        @pl.when(tm == TM - 1)
        def _():
            ext[FINE + 1, rows] = jnp.zeros((WIDE, C1), BF16)

        for lo, hi in COLS_FINE:
            pre[0, rows, lo:hi] += dot(ext[0, rows], wt[:C1, lo:hi])
            pre[3, rows, lo:hi] += dot(ext[5, rows], wt[2 * C1 :, lo:hi])
            total = None
            for t in range(FINE):
                act = pre[t, rows, lo:hi]
                logistic = 1.0 / (1.0 + jnp.exp(-act))
                skip = (ext[t + 1, rows, lo:hi].astype(F32) + act * logistic).astype(BF16).astype(F32)
                total = skip if total is None else total + skip
                pre[t, rows, lo:hi] = logistic * (1.0 + act * (1.0 - logistic))
            skipsum[rows, lo:hi] = total.astype(BF16)
        pack(skipsum, c_send, c, fold_fine, C1)
        c_receive.append(exchange(c_send, c_recv, c, 8 * c))
    for c in range(1, CHUNKS):
        g_receive.append(exchange(g_send, g_recv, c, 24 + 8 * c))

    loads[2].wait()
    loads[4].wait()
    loads[5].wait()
    for c in range(CHUNKS):
        c_receive[c]()
        unpack(c_recv, sk, c, open_fine)
    for lo, hi in COLS_COARSE:
        cb[:, lo:hi] = (0.25 * dot(sk[...], wd[:, lo:hi])).astype(BF16)
    for lo, hi in COLS_COARSE:
        qf[:, lo:hi] = dot(cb[...], wq[:, lo:hi])
        kf[:, lo:hi] = dot(cb[...], wk[:, lo:hi])
    def tiles_of(i):
        return [pl.ds(pl.multiple_of((i * TILES + u) * 128, 128), 128) for u in range(TILES)]

    def some_scores(i, carry):
        attend_scores(tiles_of(i), qf, kf, probs, bq, bk)
        return carry

    def some_back(i, carry):
        attend_back(tiles_of(i), qf, kf, probs, cb, gb, work, bq, bk)
        return carry

    lax.fori_loop(0, C2 // 128 // TILES, some_scores, 0)
    for c in range(CHUNKS):
        g_receive[c]()
        unpack(g_recv, gb, c, open_tail)
    lax.fori_loop(0, C2 // 128 // TILES, some_back, 0)
    for lo, hi in COLS_COARSE:
        projected = dot_last(bq[...], wq[lo:hi, :]) + dot_last(bk[...], wk[lo:hi, :])
        bc[:, lo:hi] = (work[:, lo:hi] + projected).astype(BF16)
    for lo, hi in COLS_FINE:
        work[:, lo:hi] = 0.25 * dot_last(bc[...], wd[lo:hi, :])
    b_receive = []
    for c in range(CHUNKS):
        pack(work, b_send, c, fold_fine, C1)
        b_receive.append(exchange(b_send, b_recv, c, 48 + 8 * c))

    def time_unit(part_y, part_core, part_dp, lo, hi):
        start = pl.multiple_of(480 * part_y + 240 * part_core + 60 * part_dp // 8 * 8, 8)
        return t_sum[pl.ds(start, 64), lo:hi]

    def down_unit(part_y, part_core, part_dp):
        start = pl.multiple_of(160 * part_y + 80 * part_core + 20 * part_dp // 8 * 8, 8)
        rows = d_sum[pl.ds(start, 24), :]
        return jnp.concatenate([rows[:16], fold_tail(rows[16:]), jnp.zeros((16, 128), F32)], axis=1)

    for lo, hi in COLS_FINE:
        d_sum[lo:hi, :] = dot_first(sk[:, lo:hi], bc[...])

    def pack_down(part_y, carry):
        for h in range(DP):
            unit = down_unit(part_y, 1 - core, h).astype(BF16)
            for part_x in range(XS):
                cs_x[part_y, part_x, h] = unit[:, DC * part_x : DC * part_x + DC]
        return carry

    def add_down(part_y, carry):
        for h in range(DP):
            unit = down_unit(part_y, core, h)
            for part_x in range(XS):
                more = unit[:, DC * part_x : DC * part_x + DC]
                p_x[part_y, part_x, h] = (p_x[part_y, part_x, h].astype(F32) + more).astype(BF16)
        return carry

    lax.fori_loop(0, YS, pack_down, 0)
    swap_x = send(remote(cs_x, p_x, 106, partner))
    swap_x.wait_recv()
    lax.fori_loop(0, YS, add_down, 0)
    ring_d = Ring(remote, p_x, (x_ra, x_rb, x_fp, x_fm), y, peers_y[0], peers_y[2], 92)
    ring_d.start()

    loads[6].wait()
    for c in range(CHUNKS):
        b_receive[c]()
        unpack(b_recv, spread, c, open_fine)
    for lo, hi in COLS_FINE:
        for t in range(FINE):
            back = gs[t, :, lo:hi].astype(F32) + spread[:, lo:hi]
            bpe[t + 1, :, lo:hi] = (back * pre[t, :, lo:hi]).astype(BF16)

    back_first = send(remote(bpe.at[1], bpe.at[FINE + 1], 78, prev))
    back_last = send(remote(bpe.at[FINE], bpe.at[0], 79, nxt))

    def time_grad(piece, cs, parts, place, shape):
        left, right = PIECES[piece]
        back_rows = bpe[1 : FINE + 1, :, left:right].reshape(FINE * PIX, right - left)
        part_y = 0
        for k in range(3):
            for lo, hi in COLS_FINE:
                block = ext[k : k + FINE, :, lo:hi].reshape(FINE * PIX, hi - lo)
                t_sum[k * C1 + lo : k * C1 + hi, left:right] = dot_first(block, back_rows)
                if part_y < YS and k * C1 + hi >= 480 * (part_y + 1):
                    for h in range(DP):
                        unit = time_unit(part_y, 1 - core, h, left, right).astype(BF16)
                        cs[place(part_y, h)] = unit.reshape(*shape, right - left)
                    if piece < 2:
                        at_y = place(part_y, slice(None))
                        send(remote(cs.at[at_y], parts.at[at_y], 98 + 4 * piece + part_y, partner))
                    part_y += 1

    def add_time(piece, parts, place, shape, part_y):
        left, right = PIECES[piece]
        for h in range(DP):
            unit = time_unit(part_y, core, h, left, right).reshape(*shape, right - left)
            parts[place(part_y, h)] = (parts[place(part_y, h)].astype(F32) + unit).astype(BF16)

    def by_y(part_y, h):
        return (part_y, h)

    def by_x(part_y, h):
        return (slice(None), part_y, h)

    def by_z(part_y, h):
        return (h, slice(None), part_y)

    time_grad(0, cs_0, p_0, by_y, (64,))
    time_grad(1, cs_1, p_1, by_x, (XS, 16))
    ring_d.middle()
    copies_0 = []
    for k in (2, 1, 3, 0):
        part_y = (y + k) % YS
        remote(cs_0.at[part_y], p_0.at[part_y], 98 + part_y, partner).wait_recv()
        add_time(0, p_0, by_y, (64,), part_y)
        if k > 0:
            copies_0.append(send(remote(p_0.at[part_y], r_0.at[k - 1], 79 + k, peers_y[k - 1])))
    time_grad(2, cs_2, p_2, by_z, (2, 32))
    swap_2 = send(remote(cs_2, p_2, 107, partner))
    for part_y in range(YS):
        remote(cs_1.at[:, part_y], p_1.at[:, part_y], 102 + part_y, partner).wait_recv()
        add_time(1, p_1, by_x, (XS, 16), part_y)
    copies_1 = [
        send(remote(p_1.at[(x + k) % XS], r_1.at[k - 1], 82 + k, peers_x[k - 1])) for k in (2, 1, 3)
    ]
    swap_2.wait_recv()
    for part_y in range(YS):
        add_time(2, p_2, by_z, (2, 32), part_y)
    copies_2 = [send(remote(p_2.at[z // 2, z % 2], zr_2.at[k], 171 + k, peers_z[k])) for k, z in enumerate(on_z)]

    def input_grad(t, count, lo, hi):
        rows = [bpe[t + k : t + k + count].reshape(count * PIX, C1) for k in range(3)]
        acc = dot_last(rows[2], wt[lo:hi, :])
        acc += dot_last(rows[1], wt[C1 + lo : C1 + hi, :])
        acc += dot_last(rows[0], wt[2 * C1 + lo : 2 * C1 + hi, :])
        acc = acc.reshape(count, PIX, hi - lo) + gs[t : t + count, :, lo:hi].astype(F32) + spread[:, lo:hi]
        gs[t : t + count, :, lo:hi] = acc.astype(BF16)

    def arrived(copies):
        for copy in copies:
            copy.wait_recv()

    def added(copies, own, more):
        arrived(copies)
        return (own.astype(F32) + sum(more[k].astype(F32) for k in range(len(copies)))).astype(BF16)

    input_grad(1, 2, *COLS_FINE[0])
    ring_d.arrived()
    for part_x in range(XS):
        p2_x[part_x] = ring_d.total(part_x).astype(BF16)
    copies_x = [send(remote(p2_x.at[(x + k) % XS], r2_x.at[k - 1], 113 + k, peers_x[k - 1])) for k in range(1, XS)]
    input_grad(1, 2, *COLS_FINE[1])
    input_grad(1, 2, *COLS_FINE[2])
    back_first.wait_recv()
    back_last.wait_recv()

    @pl.when(tm == 0)
    def _():
        bpe[0] = jnp.zeros((PIX, C1), BF16)

    @pl.when(tm == TM - 1)
    def _():
        bpe[FINE + 1] = jnp.zeros((PIX, C1), BF16)

    for lo, hi in COLS_FINE:
        input_grad(0, 1, lo, hi)
        input_grad(3, 1, lo, hi)
    store = pltpu.make_async_copy(gs, ig_out.at[0], local_sem.at[16])
    store.start()

    arrived(copies_0)
    for h in range(DP):
        total = p_0[y, h].astype(F32) + sum(r_0[k, h].astype(F32) for k in range(YS - 1))
        p2_0[:, h] = total.astype(BF16).reshape(XS, 16, -1)
    copies_0 = [send(remote(p2_0.at[(x + k) % XS], r2_0.at[k - 1], 107 + k, peers_x[k - 1])) for k in range(1, XS)]
    arrived(copies_1)
    for part_y in range(YS):
        p2_1[part_y] = (p_1[x, part_y].astype(F32) + sum(r_1[k, part_y].astype(F32) for k in range(XS - 1))).astype(BF16)
    copies_1 = [send(remote(p2_1.at[(y + k) % YS], r2_1.at[k - 1], 110 + k, peers_y[k - 1])) for k in range(1, YS)]
    p2_2[...] = added(copies_2, p_2[dp, zlo], zr_2)
    copies_2 = [send(remote(p2_2.at[(y + k) % YS], r2_2.at[k - 1], 177 + k, peers_y[k - 1])) for k in range(1, YS)]

    last_waits = []

    class OverZ:
        def __init__(self, src, slots, first, owner):
            self.src, self.slots, self.first, self.owner = src, slots, first, owner
            other = zlo if owner == 0 else 1 - zlo
            copies = []
            for k in range(DP):
                h = (dp + k) % DP
                slot = other * DP + k
                target = at(tm_=owner * XS + x, dp_=h)
                copies.append(remote(src.at[h], slots.at[slot], first + k, target, landed=first + slot))
            for copy in copies[1:]:
                copy.start()

            @pl.when(zlo != owner)
            def _():
                copies[0].start()

            def finish():
                for copy in copies[1:]:
                    copy.wait_send()

                @pl.when(zlo != owner)
                def _():
                    copies[0].wait_send()

            last_waits.append(finish)

        def gather(self, final, first):
            copies = [
                remote(final.at[x], final.at[x], first + k, peers_tm[k - 1], landed=first + TM + x)
                for k in range(1, TM)
            ]

            @pl.when(zlo == self.owner)
            def _():
                total = self.src[dp].astype(F32)
                for slot in range(1, 2 * DP):
                    ref = self.slots.at[slot]
                    remote(ref, ref, self.first + slot, partner).wait_recv()
                    total += self.slots[slot].astype(F32)
                final[x] = total.astype(BF16)
                for copy in copies:
                    copy.start()

            def finish():
                for k in range(1, XS):
                    ref = final.at[(x + k) % XS]
                    remote(ref, ref, first, partner, landed=first + TM + (x + k) % XS).wait_recv()

                @pl.when(zlo != self.owner)
                def _():
                    remote(final.at[x], final.at[x], first, partner, landed=first + TM + x).wait_recv()

                @pl.when(zlo == self.owner)
                def _():
                    for copy in copies:
                        copy.wait_send()

            last_waits.append(finish)

    sums = added(copies_x, p2_x[x], r2_x)
    for half in range(2):
        zs_x[half] = sums[:, :, half * DC // 2 : (half + 1) * DC // 2]
    z_copies = [
        send(remote(zs_x.at[z % 2, z // 2], zr_x.at[k], 133 + k, peers_z[k])) for k, z in enumerate(on_z)
    ]
    zs_0[...] = added(copies_0, p2_0[x], r2_0)
    over_z0 = OverZ(zs_0, zr_0, 117, 0)
    zs_1[...] = added(copies_1, p2_1[y], r2_1)
    over_z1 = OverZ(zs_1, zr_1, 125, 1)

    xs_2[x] = added(copies_2, p2_2[y], r2_2)
    copies_2 = [remote(xs_2.at[x], xs_2.at[x], 187 + k, peers_x[k - 1], landed=183 + x) for k in range(1, XS)]
    for copy in copies_2:
        send(copy)

    for k in range(1, XS):
        src = (x + k) % XS
        remote(xs_2.at[src], xs_2.at[src], 187, partner, landed=183 + src).wait_recv()
    f_2[zlo] = sum(xs_2[k].astype(F32) for k in range(XS)).astype(BF16)
    swap_z = send(remote(f_2.at[zlo], f_2.at[zlo], 191, at(tm_=(1 - zlo) * XS + x)))
    f_x[tm] = added(z_copies, zs_x[zlo, dp], zr_x)
    for k in range(1, TM):
        send(remote(f_x.at[tm], f_x.at[tm], 163 + k, peers_tm[k - 1]))
    over_z0.gather(f_0, 140)
    over_z1.gather(f_1, 152)
    for k in range(1, TM):
        src = (tm + TM - k) % TM
        remote(f_x.at[src], f_x.at[src], 163 + k, at(tm_=src)).wait_recv()
    for wait in last_waits:
        wait()
    swap_z.wait_recv()
    time0_out[...], time1_out[...], time2_out[...], down_out[...] = f_0[...], f_1[...], f_2[...], f_x[...]

    for copy in sent:
        copy.wait_send()
    ring_d.finish()
    store.wait()


def finish(ig, time0, time1, time2, down, ig_out, time_out, down_out, held, load_sem, store_sem):
    loads = [pltpu.make_async_copy(ig.at[0, t], held.at[t], load_sem.at[t]) for t in range(FINE)]
    stores = [pltpu.make_async_copy(held.at[t], ig_out.at[0, t], store_sem.at[t]) for t in range(FINE)]
    for load in loads:
        load.start()
    odd = lax.axis_index("dp") % 2 == 1
    scale = 1.0 / math.sqrt(ROWS_ALL)
    pieces = [time[...].astype(F32).reshape(64, -1) for time in (time0, time1, time2)]
    rows = jnp.concatenate(pieces, axis=1) * scale
    time_out[...] = jnp.where(odd, rows[4:64], rows[:60])
    halves = [down[half * XS + part_x] for part_x in range(XS) for half in range(2)]
    wide = jnp.concatenate(halves, axis=1).astype(F32) * (0.25 * scale)
    rows = jnp.concatenate([wide[:, :C2], open_tail(wide[:, C2 : C2 + C1])], axis=0)
    down_out[...] = jnp.where(odd, rows[4:24], rows[:20])
    for load, store in zip(loads, stores):
        load.wait()
        store.start()
    for store in stores:
        store.wait()


def first_over_y(n):
    v = pltpu.VMEM
    return [
        v((YS, DP, 64, n), BF16), v((YS, DP, 64, n), BF16),
        v((YS - 1, DP, 64, n), BF16),
        v((XS, DP, 16, n), BF16), v((XS - 1, DP, 16, n), BF16),
        v((DP, 16, n), BF16), v((2 * DP, 16, n), BF16), v((XS, 16, n), BF16),
    ]


def first_over_x(n):
    v = pltpu.VMEM
    return [
        v((XS, YS, DP, 16, n), BF16), v((XS, YS, DP, 16, n), BF16),
        v((XS - 1, YS, DP, 16, n), BF16),
        v((YS, DP, 16, n), BF16), v((YS - 1, DP, 16, n), BF16),
        v((DP, 16, n), BF16), v((2 * DP, 16, n), BF16), v((XS, 16, n), BF16),
    ]


def first_over_z(n):
    v = pltpu.VMEM
    return [
        v((DP, 2, YS, 32, n), BF16), v((DP, 2, YS, 32, n), BF16), v((7, YS, 32, n), BF16),
        v((YS, 32, n), BF16), v((YS - 1, 32, n), BF16), v((XS, 32, n), BF16), v((2, 32, n), BF16),
    ]


def shards(*args):
    v, hbm = pltpu.VMEM, pl.BlockSpec(memory_space=pl.ANY)
    vmem = pl.BlockSpec(memory_space=pltpu.VMEM)
    scratch = [
        v((FINE + 2, PIX, C1), BF16), v((3 * C1, C1), BF16), v((C1, C2), BF16), v((C2, C2), BF16), v((C2, C2), BF16),
        v((FINE, PIX, C1), BF16), v((PIX, C2), BF16), v((FINE, PIX, C1), F32), v((PIX, C1), BF16),
        v((PIX, C2), F32), v((PIX, C2), F32), v((PIX, C2), F32),
        v((PIX, C2), BF16), v((PIX, C2), BF16), v((PIX, C2), BF16), v((PIX, C2), BF16), v((PIX, C2), F32),
        *[v((CHUNKS, TM, 16, C1), BF16)] * 2, *[v((CHUNKS, TM, 16, FOLD), BF16)] * 4,
        v((PIX, C1), BF16), v((PIX, C2), BF16), v((PIX, C1), F32), v((FINE + 2, PIX, C1), BF16),
        v((3 * C1, C1), F32), v((C1, C2), F32),
        *first_over_y(PIECES[0][1] - PIECES[0][0]), *first_over_x(PIECES[1][1] - PIECES[1][0]),
        *first_over_z(PIECES[2][1] - PIECES[2][0]),
        v((XS, YS, DP, 16, DC), BF16), v((XS, YS, DP, 16, DC), BF16),
        *[v((2, DP, 16, DC), BF16)] * 2, *[v((4, DP, 16, DC), BF16)] * 2,
        v((YS, DP, 16, DC), BF16), v((YS - 1, DP, 16, DC), BF16),
        v((2, DP, 16, DC // 2), BF16), v((7, 16, DC // 2), BF16), v((TM, 16, DC // 2), BF16),
        pltpu.SemaphoreType.DMA((17,)), pltpu.SemaphoreType.DMA((192,)), pltpu.SemaphoreType.DMA((192,)),
    ]
    fine = jax.ShapeDtypeStruct((1, FINE, PIX, C1), BF16)
    ig, *sums = pl.pallas_call(
        kernel,
        out_shape=(
            fine,
            *[jax.ShapeDtypeStruct((XS, 16, hi - lo), BF16) for lo, hi in PIECES[:2]],
            jax.ShapeDtypeStruct((2, 32, PIECES[2][1] - PIECES[2][0]), BF16),
            jax.ShapeDtypeStruct((TM, 16, DC // 2), BF16),
        ),
        in_specs=[hbm] * 7,
        out_specs=(hbm, vmem, vmem, vmem, vmem),
        scratch_shapes=scratch,
        compiler_params=pltpu.CompilerParams(
            collective_id=0, has_side_effects=True, vmem_limit_bytes=60 * 1024 * 1024
        ),
        cost_estimate=pl.CostEstimate(flops=9 * 10**9, bytes_accessed=16 * 10**6, transcendentals=10**6),
    )(*args)
    return pl.pallas_call(
        finish,
        out_shape=(fine, jax.ShapeDtypeStruct((60, C1), F32), jax.ShapeDtypeStruct((20, C2), F32)),
        in_specs=[hbm, vmem, vmem, vmem, vmem],
        out_specs=(hbm, vmem, vmem),
        scratch_shapes=[
            v((FINE, PIX, C1), BF16),
            pltpu.SemaphoreType.DMA((FINE,)),
            pltpu.SemaphoreType.DMA((FINE,)),
        ],
        cost_estimate=pl.CostEstimate(flops=10**5, bytes_accessed=2 * 10**6, transcendentals=0),
    )(ig, *sums)


def solution(mesh):
    fine, whole = P("dp", "tm", "space", None), P()
    rows = P(("space", "dp"), None)
    return jax.shard_map(
        shards,
        mesh=mesh,
        in_specs=(fine, whole, whole, whole, whole, fine, fine),
        out_specs=(fine, rows, rows),
        check_vma=False,
    )
```
